32 devices in a mesh: item: 2 (over core), seq: 4 (over z), tensor: 4 (over y, x).
Axes of the slice: x: 2, y: 2, z: 4, core: 2. Of those that a mesh axis runs over, the one named last changes fastest.
Arguments:
- dec_input: bfloat16 [4, 2048, 768], P('item', 'seq'), may hold values from -6 to 6
- encoder_states: bfloat16 [4, 4608, 768], P('item', 'seq'), may hold values from -6 to 6
- retrieved: int32 [4, 12, 1024], P('item', 'tensor'), may hold values from 0 to 4607, as said below
- self_wq: bfloat16 [768, 768], P(None, 'tensor'), may hold values from -0.21875 to 0.21875
- self_bq: float32 [768], P('tensor'), may hold values from -1.8 to 1.8
- self_wk: bfloat16 [768, 768], P(None, 'tensor'), may hold values from -0.21875 to 0.21875
- self_wv: bfloat16 [768, 768], P(None, 'tensor'), may hold values from -0.21875 to 0.21875
- self_bv: float32 [768], P('tensor'), may hold values from -1.8 to 1.8
- self_wo: bfloat16 [768, 768], P('tensor'), may hold values from -1.5 to 1.5
- self_bo: float32 [768], replicated, may hold values from -1.8 to 1.8
- norm1_gain: float32 [768], replicated, may hold values from 0.5 to 1.5
- norm1_bias: float32 [768], replicated, may hold values from -1.8 to 1.8
- cross_wq: bfloat16 [768, 768], P(None, 'tensor'), may hold values from -0.21875 to 0.21875
- cross_bq: float32 [768], P('tensor'), may hold values from -1.8 to 1.8
- cross_wk: bfloat16 [768, 768], P(None, 'tensor'), may hold values from -0.21875 to 0.21875
- cross_wv: bfloat16 [768, 768], P(None, 'tensor'), may hold values from -0.21875 to 0.21875
- cross_bv: float32 [768], P('tensor'), may hold values from -1.8 to 1.8
- cross_wo: bfloat16 [768, 768], P('tensor'), may hold values from -3 to 3
- cross_bo: float32 [768], replicated, may hold values from -1.8 to 1.8
- norm2_gain: float32 [768], replicated, may hold values from 0.5 to 1.5
- norm2_bias: float32 [768], replicated, may hold values from -1.8 to 1.8
- ffn_w1: bfloat16 [768, 3072], P(None, 'tensor'), may hold values from -0.21875 to 0.21875
- ffn_b1: float32 [3072], P('tensor'), may hold values from -1.8 to 1.8
- ffn_w2: bfloat16 [3072, 768], P('tensor'), may hold values from -0.109375 to 0.109375
- ffn_b2: float32 [768], replicated, may hold values from -1.8 to 1.8
- norm3_gain: float32 [768], replicated, may hold values from 0.5 to 1.5
- norm3_bias: float32 [768], replicated, may hold values from -1.8 to 1.8
- out_grad: bfloat16 [4, 2048, 768], P('item', 'seq'), may hold values from -6 to 6
Outputs:
- layer_out: bfloat16 [4, 2048, 768], P('item', 'seq')
- input_grad: bfloat16 [4, 2048, 768], P('item', 'seq')
- encoder_grad: bfloat16 [4, 4608, 768], P('item', 'seq', 'tensor')
- gself_wq: float32 [768, 768], P(('item', 'seq'), 'tensor')
- gself_bq: float32 [768], P('tensor')
- gself_wk: float32 [768, 768], P(('item', 'seq'), 'tensor')
- gself_wv: float32 [768, 768], P(('item', 'seq'), 'tensor')
- gself_bv: float32 [768], P('tensor')
- gself_wo: float32 [768, 768], P('tensor', ('item', 'seq'))
- gself_bo: float32 [768], replicated
- gnorm1_gain: float32 [768], replicated
- gnorm1_bias: float32 [768], replicated
- gcross_wq: float32 [768, 768], P(('item', 'seq'), 'tensor')
- gcross_bq: float32 [768], P('tensor')
- gcross_wk: float32 [768, 768], P(('item', 'seq'), 'tensor')
- gcross_wv: float32 [768, 768], P(('item', 'seq'), 'tensor')
- gcross_bv: float32 [768], P('tensor')
- gcross_wo: float32 [768, 768], P('tensor', ('item', 'seq'))
- gcross_bo: float32 [768], replicated
- gnorm2_gain: float32 [768], replicated
- gnorm2_bias: float32 [768], replicated
- gffn_w1: float32 [768, 3072], P(('item', 'seq'), 'tensor')
- gffn_b1: float32 [3072], P('tensor')
- gffn_w2: float32 [3072, 768], P('tensor', ('item', 'seq'))
- gffn_b2: float32 [768], replicated
- gnorm3_gain: float32 [768], replicated
- gnorm3_bias: float32 [768], replicated
The draws below stay inside these ranges and needn't reach their ends.
Inputs may be any that keep to these rules, and one draw needn't show every extreme that they name: `retrieved`: for each item and head, 1024 distinct positions below 4608, among them always 0 and 4607; a position may appear under several heads, and positions fall unevenly over the blocks of 1152.
All inputs are finite; a program needn't handle non-finite values.
Results may differ from the reference program's by a relative error of at most 0.024.
Values may be sent and summed in bfloat16 or wider, within the bound.
A program may use at most 512 MiB of HBM per device.

```python
from functools import partial
import jax
import jax.numpy as jnp
from jax import lax

D = 768
H = 12
HD = 64
FF = 3072
KTOP = 1024
ENC_DEV = 1152
SEQ_LEN = 2048
ITEMS = 4
ENC = 4608


def draw_retrieved(key, part):
    key = jax.random.fold_in(key, 7)
    key_common, key_head, key_shard = jax.random.split(key, 3)
    common = jax.random.randint(key_common, (ITEMS, 1, ENC), 0, 512)
    noise = jax.random.randint(key_head, (ITEMS, H, ENC), 0, 256)
    lift = jax.random.randint(key_shard, (ITEMS, 1, ENC // ENC_DEV), 0, 256)
    shard_lift = jnp.repeat(lift, ENC_DEV, axis=2)
    places = jnp.arange(ENC, dtype=jnp.int32)
    edges = ((places == 0) | (places == ENC - 1)).astype(jnp.int32) * (2048 * ENC)
    scores = (common + noise + shard_lift) * ENC + places + edges
    return lax.top_k(scores, KTOP)[1].astype(jnp.int32)


def steps_of(key, shape, shards, low, high):
    loudness = 1.0
    for position, parts in shards:
        heights = jax.random.uniform(jax.random.fold_in(jax.random.fold_in(key, 6), position), (parts,), jnp.float32, low / len(shards), high / len(shards))
        loudness = loudness * jnp.repeat(jnp.exp(heights), shape[position] // parts).reshape((-1,) + (1,) * (len(shape) - 1 - position))
    return loudness


def centred(stream_key, extent, width, limit, shards=(), kind=jnp.bfloat16):
    values = jax.random.normal(stream_key, extent, jnp.float32) * width
    if len(shards) > 0:
        values = steps_of(stream_key, extent, shards, -0.22, 0.18) * values
    return jnp.clip(values, min=-limit, max=limit).astype(kind)


def setup_inputs(seed: int = 0) -> dict:
    splits = jax.random.split(jax.random.key(seed), 29)
    dec_input = centred(splits[0], (ITEMS, SEQ_LEN, D), 1.0, 6.0, ((0, 2), (1, 4)))
    encoder_states = centred(splits[1], (ITEMS, ENC, D), 1.0, 6.0, ((0, 2), (1, 4)))
    retrieved = draw_retrieved(jax.random.fold_in(splits[28], 71), 0)
    self_wq = centred(splits[3], (D, D), D ** -0.5, 0.21875, ((1, 4),))
    self_bq = centred(splits[4], (D,), 0.3, 1.8, ((0, 4),), jnp.float32)
    self_wk = centred(splits[5], (D, D), D ** -0.5, 0.21875, ((1, 4),))
    self_wv = centred(splits[6], (D, D), D ** -0.5, 0.21875, ((1, 4),))
    self_bv = centred(splits[7], (D,), 0.3, 1.8, ((0, 4),), jnp.float32)
    self_wo = centred(splits[8], (D, D), 16 ** -0.5, 1.5, ((0, 4),))
    self_bo = centred(splits[9], (D,), 0.3, 1.8, (), jnp.float32)
    norm1_gain = jnp.clip(1.0 + 0.1 * jax.random.normal(splits[10], (D,), jnp.float32), 0.5, 1.5)
    norm1_bias = centred(splits[11], (D,), 0.3, 1.8, (), jnp.float32)
    cross_wq = centred(splits[12], (D, D), D ** -0.5, 0.21875, ((1, 4),))
    cross_bq = centred(splits[13], (D,), 0.3, 1.8, ((0, 4),), jnp.float32)
    cross_wk = centred(splits[14], (D, D), D ** -0.5, 0.21875, ((1, 4),))
    cross_wv = centred(splits[15], (D, D), D ** -0.5, 0.21875, ((1, 4),))
    cross_bv = centred(splits[16], (D,), 0.3, 1.8, ((0, 4),), jnp.float32)
    cross_wo = centred(splits[17], (D, D), 4 ** -0.5, 3.0, ((0, 4),))
    cross_bo = centred(splits[18], (D,), 0.3, 1.8, (), jnp.float32)
    norm2_gain = jnp.clip(1.0 + 0.1 * jax.random.normal(splits[19], (D,), jnp.float32), 0.5, 1.5)
    norm2_bias = centred(splits[20], (D,), 0.3, 1.8, (), jnp.float32)
    ffn_w1 = centred(splits[21], (D, FF), D ** -0.5, 0.21875, ((1, 4),))
    ffn_b1 = centred(splits[22], (FF,), 0.3, 1.8, ((0, 4),), jnp.float32)
    ffn_w2 = centred(splits[23], (FF, D), FF ** -0.5, 0.109375, ((0, 4),))
    ffn_b2 = centred(splits[24], (D,), 0.3, 1.8, (), jnp.float32)
    norm3_gain = jnp.clip(1.0 + 0.1 * jax.random.normal(splits[25], (D,), jnp.float32), 0.5, 1.5)
    norm3_bias = centred(splits[26], (D,), 0.3, 1.8, (), jnp.float32)
    out_grad = centred(splits[27], (ITEMS, SEQ_LEN, D), 1.0, 6.0, ((0, 2), (1, 4)))
    return {"dec_input": dec_input, "encoder_states": encoder_states, "retrieved": retrieved, "self_wq": self_wq, "self_bq": self_bq, "self_wk": self_wk, "self_wv": self_wv, "self_bv": self_bv, "self_wo": self_wo, "self_bo": self_bo, "norm1_gain": norm1_gain, "norm1_bias": norm1_bias, "cross_wq": cross_wq, "cross_bq": cross_bq, "cross_wk": cross_wk, "cross_wv": cross_wv, "cross_bv": cross_bv, "cross_wo": cross_wo, "cross_bo": cross_bo, "norm2_gain": norm2_gain, "norm2_bias": norm2_bias, "ffn_w1": ffn_w1, "ffn_b1": ffn_b1, "ffn_w2": ffn_w2, "ffn_b2": ffn_b2, "norm3_gain": norm3_gain, "norm3_bias": norm3_bias, "out_grad": out_grad}


@jax.custom_vjp
def low(v):
    return lax.optimization_barrier(v.astype(jnp.bfloat16)).astype(jnp.float32)

@jax.custom_vjp
def low_back(v):
    return v

def low_keep(v):
    return (low(v), None)

def low_pass(kept, grad):
    return (grad,)

def back_keep(v):
    return (v, None)

def back_low(kept, grad):
    return (low(grad),)
low.defvjp(low_keep, low_pass)
low_back.defvjp(back_keep, back_low)
EPS = 1e-05
HIGH = lax.Precision.HIGHEST

def matmul(first_op, second_op):
    return jnp.dot(first_op, second_op, precision=HIGH)

def layer_norm(rows_in, norm_gain, norm_shift):
    center = rows_in - lax.optimization_barrier(jnp.mean(rows_in, axis=-1, keepdims=True))
    spread = lax.optimization_barrier(jnp.mean(center * center, axis=-1, keepdims=True))
    return center * lax.rsqrt(spread + EPS) * norm_gain + norm_shift

def attend(queries, key_rows, value_rows, allowed):
    scores = low_back(jnp.einsum('the,hse->hts', queries, key_rows, precision=HIGH))
    scores = jnp.where(allowed, scores, -1e+30)
    attn_probs = low(jax.nn.softmax(scores, axis=-1))
    attn_mixed = jnp.einsum('hts,hse->the', attn_probs, value_rows, precision=HIGH)
    return low_back(low(attn_mixed.reshape(queries.shape[0], -1)))

def item_forward(params, pieces):
    self_wq, self_bq, self_wk, self_wv, self_bv, self_wo, self_bo, norm1_gain, norm1_bias, cross_wq, cross_bq, cross_wk, cross_wv, cross_bv, cross_wo, cross_bo, norm2_gain, norm2_bias, ffn_w1, ffn_b1, ffn_w2, ffn_b2, norm3_gain, norm3_bias = params
    tokens, memory, chosen = pieces
    query_one = low_back(low((matmul(tokens, self_wq) + self_bq) * 0.125)).reshape(SEQ_LEN, H, HD)
    key_one = low_back(low(matmul(tokens, self_wk))).reshape(SEQ_LEN, H, HD).transpose(1, 0, 2)
    value_one = low_back(low(matmul(tokens, self_wv) + self_bv)).reshape(SEQ_LEN, H, HD).transpose(1, 0, 2)
    positions = jnp.arange(SEQ_LEN)
    causal = positions[:, None] >= positions[None, :]
    attended = attend(query_one, key_one, value_one, causal)
    branch_one = low_back(matmul(attended, self_wo) + self_bo)
    normed_one = low(layer_norm(tokens + branch_one, norm1_gain, norm1_bias))
    query_two = low_back(low((matmul(normed_one, cross_wq) + cross_bq) * 0.125)).reshape(SEQ_LEN, H, HD)
    fetched = memory[chosen]
    key_two = low_back(low(jnp.einsum('hkd,dhe->hke', fetched, cross_wk.reshape(D, H, HD), precision=HIGH)))
    value_two = low_back(low(jnp.einsum('hkd,dhe->hke', fetched, cross_wv.reshape(D, H, HD), precision=HIGH) + cross_bv.reshape(H, 1, HD)))
    attended_two = attend(query_two, key_two, value_two, jnp.ones((1, 1), dtype=bool))
    branch_two = low_back(matmul(attended_two, cross_wo) + cross_bo)
    normed_two = low(layer_norm(normed_one + branch_two, norm2_gain, norm2_bias))
    pre_act = low_back(matmul(normed_two, ffn_w1) + ffn_b1)
    activated = low(jax.nn.gelu(pre_act, approximate=False))
    branch_three = low_back(matmul(activated, ffn_w2) + ffn_b2)
    return layer_norm(normed_two + branch_three, norm3_gain, norm3_bias)

def reference(dec_input, encoder_states, retrieved, self_wq, self_bq, self_wk, self_wv, self_bv, self_wo, self_bo, norm1_gain, norm1_bias, cross_wq, cross_bq, cross_wk, cross_wv, cross_bv, cross_wo, cross_bo, norm2_gain, norm2_bias, ffn_w1, ffn_b1, ffn_w2, ffn_b2, norm3_gain, norm3_bias, out_grad):
    params = tuple((param.astype(jnp.float32) for param in (self_wq, self_bq, self_wk, self_wv, self_bv, self_wo, self_bo, norm1_gain, norm1_bias, cross_wq, cross_bq, cross_wk, cross_wv, cross_bv, cross_wo, cross_bo, norm2_gain, norm2_bias, ffn_w1, ffn_b1, ffn_w2, ffn_b2, norm3_gain, norm3_bias)))

    def forward(tokens, memory, weights):
        return lax.map(jax.checkpoint(partial(item_forward, weights)), (tokens, memory, retrieved))
    result, pullback = jax.vjp(forward, dec_input.astype(jnp.float32), encoder_states.astype(jnp.float32), params)
    d_tokens, d_memory, grads = pullback(out_grad.astype(jnp.float32))
    return (result.astype(jnp.bfloat16), d_tokens.astype(jnp.bfloat16), d_memory.astype(jnp.bfloat16), grads[0], grads[1], grads[2], grads[3], grads[4], grads[5], grads[6], grads[7], grads[8], grads[9], grads[10], grads[11], grads[12], grads[13], grads[14], grads[15], grads[16], grads[17], grads[18], grads[19], grads[20], grads[21], grads[22], grads[23])
```

```python
import functools

import jax
import jax.numpy as jnp
from jax import lax
from jax.experimental import pallas as pl
from jax.experimental.pallas import tpu as pltpu
from jax.sharding import PartitionSpec as P

EPS = 1e-05
SCALE = 0.125
NEG = -1e30
MESH = pl.DeviceIdType.MESH
ITEM, SEQ, TENSOR = "item", "seq", "tensor"


def matmul(first_op, second_op):
    return jnp.dot(first_op, second_op, preferred_element_type=jnp.float32)


def layer_norm(rows_in, norm_gain, norm_shift):
    center = rows_in - jnp.mean(rows_in, axis=-1, keepdims=True)
    spread = jnp.mean(center * center, axis=-1, keepdims=True)
    return center * lax.rsqrt(spread + EPS) * norm_gain + norm_shift


def exact_gelu(values_in):
    return jax.nn.gelu(values_in, approximate=False)


def tensor_total(partial_rows):
    return lax.psum(partial_rows, TENSOR)


def row_total(values_in):
    return jnp.sum(values_in.astype(jnp.float32), axis=(0, 1))


def softmax_stats(scores):
    row_max = jnp.max(scores, axis=-1, keepdims=True)
    shifted = jnp.exp(scores - row_max)
    row_sum = jnp.sum(shifted, axis=-1, keepdims=True)
    return (shifted / row_sum, row_max + jnp.log(row_sum))


def owned_pick(encoder_states, kv_weights, kv_bias, flat_index, owned_mask):
    kv_table = (
        jnp.einsum("ind,dhf->inhf", encoder_states, kv_weights, preferred_element_type=jnp.float32)
        + kv_bias
    ).astype(jnp.bfloat16)
    flat_table = kv_table.reshape(-1, kv_table.shape[-1])
    picked = jnp.take(flat_table, flat_index, axis=0)
    return jnp.where(owned_mask, picked.astype(jnp.float32), 0.0)


def general_body(
    dec_input,
    encoder_states,
    retrieved,
    self_wq,
    self_bq,
    self_wk,
    self_wv,
    self_bv,
    self_wo,
    self_bo,
    norm1_gain,
    norm1_bias,
    cross_wq,
    cross_bq,
    cross_wk,
    cross_wv,
    cross_bv,
    cross_wo,
    cross_bo,
    norm2_gain,
    norm2_bias,
    ffn_w1,
    ffn_b1,
    ffn_w2,
    ffn_b2,
    norm3_gain,
    norm3_bias,
    out_grad,
):
    item_count, dec_rows, model_width = dec_input.shape
    local_heads = retrieved.shape[1]
    enc_rows = encoder_states.shape[1]
    head_cols = self_wq.shape[1]
    head_size = head_cols // local_heads
    seq_devices = lax.axis_size(SEQ)
    seq_rank = lax.axis_index(SEQ)
    seq_length = dec_rows * seq_devices
    queries = ((matmul(dec_input, self_wq) + self_bq) * SCALE).astype(jnp.bfloat16)
    keys_local = matmul(dec_input, self_wk).astype(jnp.bfloat16)
    values_local = (matmul(dec_input, self_wv) + self_bv).astype(jnp.bfloat16)
    kv_all = lax.all_gather(
        jnp.concatenate([keys_local, values_local], axis=-1), SEQ, axis=1, tiled=True
    )
    keys_all = kv_all[..., :head_cols].reshape(item_count, seq_length, local_heads, head_size)
    values_all = kv_all[..., head_cols:].reshape(item_count, seq_length, local_heads, head_size)
    query_heads = queries.reshape(item_count, dec_rows, local_heads, head_size)
    query_pos = seq_rank * dec_rows + jnp.arange(dec_rows)
    causal = query_pos[:, None] >= jnp.arange(seq_length)[None, :]

    def self_scores():
        raw_scores = jnp.einsum(
            "irhe,ilhe->ihrl", query_heads, keys_all, preferred_element_type=jnp.float32
        )
        return jnp.where(causal, raw_scores, NEG)

    prob_self, lse_self = softmax_stats(self_scores())
    attended = (
        jnp.einsum(
            "ihrl,ilhe->irhe",
            prob_self.astype(jnp.bfloat16),
            values_all,
            preferred_element_type=jnp.float32,
        )
        .astype(jnp.bfloat16)
        .reshape(item_count, dec_rows, head_cols)
    )
    branch_one = tensor_total(matmul(attended, self_wo)) + self_bo
    hidden_one = dec_input.astype(jnp.float32) + branch_one
    normed_one = layer_norm(hidden_one, norm1_gain, norm1_bias).astype(jnp.bfloat16)
    queries_x = (
        ((matmul(normed_one, cross_wq) + cross_bq) * SCALE)
        .astype(jnp.bfloat16)
        .reshape(item_count, dec_rows, local_heads, head_size)
    )
    kv_weights = jnp.concatenate(
        [
            cross_wk.reshape(model_width, local_heads, head_size),
            cross_wv.reshape(model_width, local_heads, head_size),
        ],
        axis=-1,
    )
    kv_bias = jnp.concatenate(
        [
            jnp.zeros((local_heads, head_size), jnp.float32),
            cross_bv.reshape(local_heads, head_size),
        ],
        axis=-1,
    )
    local_row = retrieved - seq_rank * enc_rows
    owned_mask = ((local_row >= 0) & (local_row < enc_rows))[..., None]
    flat_index = (
        jnp.arange(item_count, dtype=jnp.int32)[:, None, None] * enc_rows
        + jnp.clip(local_row, 0, enc_rows - 1)
    ) * local_heads + jnp.arange(local_heads, dtype=jnp.int32)[None, :, None]
    retrieved_kv = lax.psum(
        owned_pick(encoder_states, kv_weights, kv_bias, flat_index, owned_mask).astype(
            jnp.bfloat16
        ),
        SEQ,
    )

    def cross_scores(kv_pair):
        return jnp.einsum(
            "irhe,ihke->ihrk",
            queries_x,
            kv_pair[..., :head_size],
            preferred_element_type=jnp.float32,
        )

    prob_cross, lse_cross = softmax_stats(cross_scores(retrieved_kv))
    attended_x = (
        jnp.einsum(
            "ihrk,ihke->irhe",
            prob_cross.astype(jnp.bfloat16),
            retrieved_kv[..., head_size:],
            preferred_element_type=jnp.float32,
        )
        .astype(jnp.bfloat16)
        .reshape(item_count, dec_rows, head_cols)
    )
    branch_two = tensor_total(matmul(attended_x, cross_wo)) + cross_bo
    hidden_two = normed_one.astype(jnp.float32) + branch_two
    normed_two = layer_norm(hidden_two, norm2_gain, norm2_bias).astype(jnp.bfloat16)
    pre_act = matmul(normed_two, ffn_w1) + ffn_b1
    activated = exact_gelu(pre_act).astype(jnp.bfloat16)
    branch_three = tensor_total(matmul(activated, ffn_w2)) + ffn_b2
    hidden_three = normed_two.astype(jnp.float32) + branch_three
    layer_out = layer_norm(hidden_three, norm3_gain, norm3_bias)
    _, back_three = jax.vjp(layer_norm, hidden_three, norm3_gain, norm3_bias)
    d_hidden3, gnorm3_gain, gnorm3_bias = back_three(out_grad.astype(jnp.float32))
    d_branch3 = d_hidden3.astype(jnp.bfloat16)
    gffn_b2 = row_total(d_branch3)
    gffn_w2 = jnp.einsum("irf,ird->fd", activated, d_branch3, preferred_element_type=jnp.float32)
    d_activated = jnp.einsum("ird,fd->irf", d_branch3, ffn_w2, preferred_element_type=jnp.float32)
    _, gelu_back = jax.vjp(exact_gelu, pre_act)
    d_pre = gelu_back(d_activated)[0].astype(jnp.bfloat16)
    gffn_b1 = row_total(d_pre)
    gffn_w1 = jnp.einsum("ird,irf->df", normed_two, d_pre, preferred_element_type=jnp.float32)
    d_normed2 = d_hidden3 + tensor_total(
        jnp.einsum("irf,df->ird", d_pre, ffn_w1, preferred_element_type=jnp.float32)
    )
    _, back_two = jax.vjp(layer_norm, hidden_two, norm2_gain, norm2_bias)
    d_hidden2, gnorm2_gain, gnorm2_bias = back_two(d_normed2)
    d_branch2 = d_hidden2.astype(jnp.bfloat16)
    gcross_bo = row_total(d_branch2)
    gcross_wo = jnp.einsum("irc,ird->cd", attended_x, d_branch2, preferred_element_type=jnp.float32)
    d_attended2 = (
        jnp.einsum("ird,cd->irc", d_branch2, cross_wo, preferred_element_type=jnp.float32)
        .astype(jnp.bfloat16)
        .reshape(item_count, dec_rows, local_heads, head_size)
    )
    kv_back = lax.psum(
        owned_pick(encoder_states, kv_weights, kv_bias, flat_index, owned_mask).astype(
            jnp.bfloat16
        ),
        SEQ,
    )
    redo_cross = jnp.exp(cross_scores(kv_back) - lse_cross)
    dprob_cross = jnp.einsum(
        "irhe,ihke->ihrk", d_attended2, kv_back[..., head_size:], preferred_element_type=jnp.float32
    )
    d_scores2 = (
        redo_cross * (dprob_cross - jnp.sum(dprob_cross * redo_cross, axis=-1, keepdims=True))
    ).astype(jnp.bfloat16)
    d_query2 = (
        jnp.einsum(
            "ihrk,ihke->irhe",
            d_scores2,
            kv_back[..., :head_size],
            preferred_element_type=jnp.float32,
        )
        .astype(jnp.bfloat16)
        .reshape(item_count, dec_rows, head_cols)
    )
    kv_grad_part = jnp.concatenate(
        [
            jnp.einsum("ihrk,irhe->ihke", d_scores2, queries_x, preferred_element_type=jnp.float32),
            jnp.einsum(
                "ihrk,irhe->ihke",
                redo_cross.astype(jnp.bfloat16),
                d_attended2,
                preferred_element_type=jnp.float32,
            ),
        ],
        axis=-1,
    )
    kv_grad = lax.psum(kv_grad_part, SEQ).astype(jnp.bfloat16)
    kv_owned = jnp.where(owned_mask, kv_grad.astype(jnp.float32), 0.0)
    table_grad = (
        jnp.zeros((item_count * enc_rows * local_heads, 2 * head_size), jnp.float32)
        .at[flat_index.reshape(-1)]
        .add(kv_owned.reshape(-1, 2 * head_size))
    )
    table_low = table_grad.astype(jnp.bfloat16).reshape(
        item_count, enc_rows, local_heads, 2 * head_size
    )
    grad_kv_weights = jnp.einsum(
        "ind,inhf->dhf", encoder_states, table_low, preferred_element_type=jnp.float32
    )
    gcross_wk = grad_kv_weights[..., :head_size].reshape(model_width, head_cols)
    gcross_wv = grad_kv_weights[..., head_size:].reshape(model_width, head_cols)
    gcross_bv = row_total(table_low[..., head_size:]).reshape(head_cols)
    encoder_part = jnp.einsum(
        "inhf,dhf->ind", table_low, kv_weights, preferred_element_type=jnp.float32
    )
    encoder_grad = lax.psum_scatter(encoder_part, TENSOR, scatter_dimension=2, tiled=True).astype(
        jnp.bfloat16
    )
    gcross_bq = row_total(d_query2) * SCALE
    gcross_wq = (
        jnp.einsum("ird,irc->dc", normed_one, d_query2, preferred_element_type=jnp.float32) * SCALE
    )
    d_normed1 = d_hidden2 + tensor_total(
        jnp.einsum("irc,dc->ird", d_query2, cross_wq, preferred_element_type=jnp.float32) * SCALE
    )
    _, back_one = jax.vjp(layer_norm, hidden_one, norm1_gain, norm1_bias)
    d_hidden1, gnorm1_gain, gnorm1_bias = back_one(d_normed1)
    d_branch1 = d_hidden1.astype(jnp.bfloat16)
    gself_bo = row_total(d_branch1)
    gself_wo = jnp.einsum("irc,ird->cd", attended, d_branch1, preferred_element_type=jnp.float32)
    d_attended1 = (
        jnp.einsum("ird,cd->irc", d_branch1, self_wo, preferred_element_type=jnp.float32)
        .astype(jnp.bfloat16)
        .reshape(item_count, dec_rows, local_heads, head_size)
    )
    redo_self = jnp.exp(self_scores() - lse_self)
    dprob_self = jnp.einsum(
        "irhe,ilhe->ihrl", d_attended1, values_all, preferred_element_type=jnp.float32
    )
    d_scores1 = (
        redo_self * (dprob_self - jnp.sum(dprob_self * redo_self, axis=-1, keepdims=True))
    ).astype(jnp.bfloat16)
    probs_low = redo_self.astype(jnp.bfloat16)
    d_query1 = (
        jnp.einsum("ihrl,ilhe->irhe", d_scores1, keys_all, preferred_element_type=jnp.float32)
        .astype(jnp.bfloat16)
        .reshape(item_count, dec_rows, head_cols)
    )
    row_count = dec_rows * lax.axis_size(SEQ)
    key_grad = jnp.einsum(
        "ihrl,irhe->lihe", d_scores1, query_heads, preferred_element_type=jnp.float32
    ).reshape(row_count, item_count, head_cols)
    value_grad = jnp.einsum(
        "ihrl,irhe->lihe", probs_low, d_attended1, preferred_element_type=jnp.float32
    ).reshape(row_count, item_count, head_cols)
    kv_self = lax.psum_scatter(
        jnp.concatenate([key_grad, value_grad], axis=-1), SEQ, scatter_dimension=0, tiled=True
    ).astype(jnp.bfloat16)
    kv_self = jnp.swapaxes(kv_self, 0, 1)
    d_key1 = kv_self[..., :head_cols]
    d_value1 = kv_self[..., head_cols:]
    gself_bq = row_total(d_query1) * SCALE
    gself_wq = (
        jnp.einsum("ird,irc->dc", dec_input, d_query1, preferred_element_type=jnp.float32) * SCALE
    )
    gself_wk = jnp.einsum("ird,irc->dc", dec_input, d_key1, preferred_element_type=jnp.float32)
    gself_wv = jnp.einsum("ird,irc->dc", dec_input, d_value1, preferred_element_type=jnp.float32)
    gself_bv = row_total(d_value1)
    input_part = (
        jnp.einsum("irc,dc->ird", d_query1, self_wq, preferred_element_type=jnp.float32) * SCALE
        + jnp.einsum("irc,dc->ird", d_key1, self_wk, preferred_element_type=jnp.float32)
        + jnp.einsum("irc,dc->ird", d_value1, self_wv, preferred_element_type=jnp.float32)
    )
    input_grad = (d_hidden1 + tensor_total(input_part)).astype(jnp.bfloat16)
    matrices = (
        lax.psum_scatter(gself_wq, (ITEM, SEQ), scatter_dimension=0, tiled=True),
        lax.psum_scatter(gself_wk, (ITEM, SEQ), scatter_dimension=0, tiled=True),
        lax.psum_scatter(gself_wv, (ITEM, SEQ), scatter_dimension=0, tiled=True),
        lax.psum_scatter(gself_wo, (ITEM, SEQ), scatter_dimension=1, tiled=True),
        lax.psum_scatter(gcross_wq, (ITEM, SEQ), scatter_dimension=0, tiled=True),
        lax.psum_scatter(gcross_wk, (ITEM, SEQ), scatter_dimension=0, tiled=True),
        lax.psum_scatter(gcross_wv, (ITEM, SEQ), scatter_dimension=0, tiled=True),
        lax.psum_scatter(gcross_wo, (ITEM, SEQ), scatter_dimension=1, tiled=True),
        lax.psum_scatter(gffn_w1, (ITEM, SEQ), scatter_dimension=0, tiled=True),
        lax.psum_scatter(gffn_w2, (ITEM, SEQ), scatter_dimension=1, tiled=True),
    )
    vectors = lax.psum(
        (
            gself_bq,
            gself_bv,
            gself_bo,
            gnorm1_gain,
            gnorm1_bias,
            gcross_bq,
            gcross_bv,
            gcross_bo,
            gnorm2_gain,
            gnorm2_bias,
            gffn_b1,
            gffn_b2,
            gnorm3_gain,
            gnorm3_bias,
        ),
        (ITEM, SEQ),
    )
    return (
        layer_out.astype(jnp.bfloat16),
        input_grad,
        encoder_grad,
        matrices[0],
        vectors[0],
        matrices[1],
        matrices[2],
        vectors[1],
        matrices[3],
        vectors[2],
        vectors[3],
        vectors[4],
        matrices[4],
        vectors[5],
        matrices[5],
        matrices[6],
        vectors[6],
        matrices[7],
        vectors[7],
        vectors[8],
        vectors[9],
        matrices[8],
        vectors[10],
        matrices[9],
        vectors[11],
        vectors[12],
        vectors[13],
    )


VMEM_LIMIT = 56 * 1024 * 1024
FULL = 256
HALF = 128
WIDE = FULL + HALF


def column_plan_fits(mesh, arrays):
    items, cores = arrays[0].shape[0], mesh.shape[ITEM]
    ranks, depth = mesh.shape[TENSOR], mesh.shape[SEQ]
    heads = arrays[2].shape[1]
    rows = arrays[0].shape[1] // depth
    width = arrays[0].shape[2]
    return (
        cores == 2
        and ranks == 4
        and items == ranks
        and ranks == depth
        and heads == 3 * depth
        and width == 64 * heads
        and rows == cores * FULL
        and arrays[2].shape[2] % FULL == 0
    )


def here():
    return lax.axis_index(ITEM), lax.axis_index(SEQ), lax.axis_index(TENSOR)


def call_kernel(kernel, name, outs, args, scratch=(), collective_id=None, in_spaces=None, out_space=None, us=10):
    single = isinstance(outs, tuple)
    listed = [outs] if single else list(outs)
    space = pltpu.VMEM if out_space is None else out_space
    spaces = [pltpu.VMEM] * len(args) if in_spaces is None else in_spaces
    params = dict(vmem_limit_bytes=VMEM_LIMIT)
    if collective_id is not None:
        params.update(collective_id=collective_id, has_side_effects=True)
    out = pl.pallas_call(
        kernel,
        out_shape=[jax.ShapeDtypeStruct(s, d) for s, d in listed],
        in_specs=[pl.BlockSpec(memory_space=s) for s in spaces],
        out_specs=[pl.BlockSpec(memory_space=space) for _ in listed],
        scratch_shapes=list(scratch),
        compiler_params=pltpu.CompilerParams(**params),
        cost_estimate=pl.CostEstimate(flops=us * 10**9, bytes_accessed=us * 3 * 10**6, transcendentals=0),
        name=name,
    )(*args)
    return out[0] if single else out


def greet(peers):
    gate = pltpu.get_barrier_semaphore()
    for peer in peers:
        pl.semaphore_signal(gate, inc=1, device_id=peer, device_id_type=MESH)


def meet(peers):
    greet(peers)
    pl.semaphore_wait(pltpu.get_barrier_semaphore(), len(peers))


def column_peer(place, cores, rank):
    return (lax.rem(place, cores), place // cores, rank)


def remote_copy(src, dst, send, recv, device):
    return pltpu.make_async_remote_copy(
        src_ref=src, dst_ref=dst, send_sem=send, recv_sem=recv, device_id=device, device_id_type=MESH
    )


def plane_peers(cores, ranks):
    core, seq, rank = here()
    peers = []
    for step in range(1, cores * ranks):
        place = lax.rem(rank * cores + core + step, cores * ranks)
        peers.append((lax.rem(place, cores), seq, place // cores))
    return peers


class Deal:
    def __init__(self, cores, ranks, per_core, source, all_ref, send_sem, recv_sem, own_sem):
        self.cores, self.ranks, self.per_core = cores, ranks, per_core
        self.source, self.all_ref = source, all_ref
        self.send_sem, self.recv_sem, self.own_sem = send_sem, recv_sem, own_sem
        self.core, self.seq, self.rank = here()
        self.home = self.rank // per_core
        self.local = lax.rem(self.rank, per_core)

    def send(self, step):
        target = lax.rem(self.rank + step, self.ranks)
        return remote_copy(
            self.source(target),
            self.all_ref.at[self.local, self.core],
            self.send_sem.at[step],
            self.recv_sem.at[self.local, self.core],
            (self.home, self.seq, target),
        )

    def keep(self):
        return pltpu.make_async_copy(self.source(self.rank), self.all_ref.at[self.local, self.core], self.own_sem)

    def start(self):
        for step in range(1, self.ranks):
            self.send(step).start()

        @pl.when(self.core != self.home)
        def _():
            self.send(0).start()

        @pl.when(self.core == self.home)
        def _():
            self.keep().start()

    def finish(self):
        for item in range(self.per_core):
            for half in range(self.cores):
                inside = (half == self.core) & (self.core * self.per_core + item == self.rank)

                @pl.when(jnp.logical_not(inside))
                def _():
                    remote_copy(
                        self.source(0),
                        self.all_ref.at[item, half],
                        self.send_sem.at[0],
                        self.recv_sem.at[item, half],
                        (1 - self.core, self.seq, self.rank),
                    ).wait_recv()

        for step in range(1, self.ranks):
            self.send(step).wait_send()

        @pl.when(self.core != self.home)
        def _():
            self.send(0).wait_send()

        @pl.when(self.core == self.home)
        def _():
            self.keep().wait()


def deal_scratch(cores, ranks, per_core):
    dma = pltpu.SemaphoreType.DMA
    return [dma((ranks,)), dma((per_core, cores)), dma]


class PlaneGather:
    def __init__(self, all_ref, give_send, give_recv, far_send, far_recv, pass_send, pass_recv):
        self.all_ref = all_ref
        self.give_send, self.give_recv = give_send, give_recv
        self.far_send, self.far_recv = far_send, far_recv
        self.pass_send, self.pass_recv = pass_send, pass_recv
        self.core, self.seq, self.rank = here()
        low, high = lax.rem(self.rank, 2), self.rank // 2
        self.near = (2 * high + 1 - low, 2 * (1 - high) + low)
        self.far = 2 * (1 - high) + 1 - low
        self.half = all_ref.shape[2] // 2
        self.peers = [(self.core, self.seq, rank) for rank in self.near]

    def give(self, way):
        block = self.all_ref.at[self.core, self.rank]
        return remote_copy(block, block, self.give_send.at[way], self.give_recv.at[way], self.peers[way])

    def far_part(self, way, origin):
        return self.all_ref.at[self.core, origin, pl.ds(way * self.half, self.half), :]

    def onward(self, way):
        block = self.far_part(way, self.near[way])
        return remote_copy(
            block, block, self.far_send.at[way], self.far_recv.at[way], self.peers[1 - way]
        )

    def side(self, slot, block):
        return remote_copy(
            block, block, self.pass_send.at[slot], self.pass_recv.at[slot], (1 - self.core, self.seq, self.rank)
        )

    def sides(self):
        near = [self.side(way, self.all_ref.at[self.core, self.near[way]]) for way in range(2)]
        return near + [self.side(2 + way, self.far_part(way, self.far)) for way in range(2)]

    def start(self):
        for way in range(2):
            self.give(way).start()

    def forward(self):
        sides = self.sides()
        for way in range(2):
            self.give(way).wait_recv()
            self.onward(way).start()
            sides[way].start()

    def finish(self):
        sides = self.sides()
        for way in range(2):
            self.onward(way).wait_recv()
            sides[2 + way].start()
        for way in range(2):
            self.give(way).wait_send()
            self.onward(way).wait_send()
        for side in sides:
            side.wait()


def gather_scratch():
    return [pltpu.SemaphoreType.DMA((n,)) for n in (2, 2, 2, 2, 4, 4)]


class PlaneReduce:
    def __init__(self, ranks, grad_ref, got_ref, sum_ref, all_ref, swap_sem, send_sem, recv_sem):
        self.ranks, self.grad_ref, self.got_ref = ranks, grad_ref, got_ref
        self.sum_ref, self.all_ref = sum_ref, all_ref
        self.swap_sem, self.send_sem, self.recv_sem = swap_sem, send_sem, recv_sem
        self.core, self.seq, self.rank = here()
        self.peers = [(self.core, self.seq, lax.rem(self.rank + step, ranks)) for step in range(1, ranks)]

    def swap(self):
        return remote_copy(
            self.grad_ref.at[1 - self.core],
            self.got_ref,
            self.swap_sem.at[0],
            self.swap_sem.at[1],
            (1 - self.core, self.seq, self.rank),
        )

    def copy(self, step):
        peer = self.peers[step]
        return remote_copy(
            self.sum_ref.at[peer[2]], self.all_ref.at[self.rank], self.send_sem.at[step], self.recv_sem.at[step], peer
        )

    def start(self):
        self.swap().start()

    def middle(self):
        self.swap().wait()
        for rank in range(self.ranks):
            self.sum_ref[rank] = (
                self.grad_ref[self.core, rank].astype(jnp.float32) + self.got_ref[rank].astype(jnp.float32)
            ).astype(self.sum_ref.dtype)
        for step in range(self.ranks - 1):
            self.copy(step).start()

    def finish(self):
        for step in range(self.ranks - 1):
            self.copy(step).wait()
        total = self.sum_ref[self.rank].astype(jnp.float32)
        for step in range(1, self.ranks):
            total = total + self.all_ref[lax.rem(self.rank + step, self.ranks)].astype(jnp.float32)
        return total


def reduce_scratch(ranks, rows, columns, dtype):
    dma = pltpu.SemaphoreType.DMA
    block = pltpu.VMEM((ranks, rows, columns), dtype)
    return [block, block, block, dma((2,)), dma((ranks - 1,)), dma((ranks - 1,))]


def column_places(cores, depth):
    core, seq, _ = here()
    mine = seq * cores + core
    return mine, [lax.rem(mine + step, cores * depth) for step in range(1, cores * depth)]


class ColumnSend:
    def __init__(self, cores, depth, source_ref, all_ref, send_sem, recv_sem):
        self.cores, self.count = cores, cores * depth
        self.source_ref, self.all_ref = source_ref, all_ref
        self.send_sem, self.recv_sem = send_sem, recv_sem
        core, seq, self.rank = here()
        self.mine = seq * cores + core

    def copy(self, step):
        place = lax.rem(self.mine + 1 + step, self.count)
        return remote_copy(
            self.source_ref.at[place],
            self.all_ref.at[self.mine],
            self.send_sem.at[step],
            self.recv_sem.at[step],
            column_peer(place, self.cores, self.rank),
        )

    def wait_from(self, step):
        self.copy(step).wait_recv()

    def finish_sends(self):
        for step in range(self.count - 1):
            self.copy(step).wait_send()

    def finish(self):
        for step in range(self.count - 1):
            self.copy(step).wait()


def send_scratch(count):
    return [pltpu.SemaphoreType.DMA((count - 1,)), pltpu.SemaphoreType.DMA((count - 1,))]


class Chain:
    def __init__(self, depth, all_ref, send_sem, recv_sem):
        self.depth, self.all_ref = depth, all_ref
        self.send_sem, self.recv_sem = send_sem, recv_sem
        core, self.seq, rank = here()
        self.above = (core, lax.rem(self.seq + 1, depth), rank)
        self.below = (core, lax.rem(self.seq + depth - 1, depth), rank)

    def copy(self, block, way):
        part = self.all_ref.at[block]
        target = self.above if way == 0 else self.below
        return remote_copy(part, part, self.send_sem.at[way, block], self.recv_sem.at[block], target)

    def step(self, n):
        up, down = self.seq - n, self.seq + n

        @pl.when(up >= 0)
        def _():
            if n > 0:
                self.copy(up, 0).wait_recv()

            @pl.when(self.seq + 1 < self.depth)
            def _():
                self.copy(up, 0).start()

        @pl.when(down < self.depth)
        def _():
            if n > 0:
                self.copy(down, 1).wait_recv()

            @pl.when(self.seq > 0)
            def _():
                self.copy(down, 1).start()

    def finish(self):
        for n in range(self.depth):
            up, down = self.seq - n, self.seq + n

            @pl.when((up >= 0) & (self.seq + 1 < self.depth))
            def _():
                self.copy(up, 0).wait_send()

            @pl.when((down < self.depth) & (self.seq > 0))
            def _():
                self.copy(down, 1).wait_send()


def prologue_kernel(
    sizes,
    x_ref, g_ref, m_ref, idx_ref, vec_ref, wq_ref, wk_ref, wv_ref, ck_ref, cv_ref,
    xall_ref, gmine_ref, enc_ref, iall_ref, vall_ref, wall_ref,
    load_sem,
    swap_send, swap_recv, chain_send, chain_recv, side_send, side_recv, own_sem,
    idx_send, idx_recv, vec_send, vec_recv, *wsems
):
    cores, depth, ranks, per_core = sizes
    core, seq, rank = here()
    home = rank // per_core
    local = lax.rem(rank, per_core)
    sibling = (1 - core, seq, rank)
    above = (core, lax.rem(seq + 1, depth), rank)
    below = (core, lax.rem(seq + depth - 1, depth), rank)
    plane = []
    for step in range(1, cores * ranks):
        place = lax.rem(rank * cores + core + step, cores * ranks)
        plane.append((lax.rem(place, cores), seq, place // cores))
    high = wq_ref.shape[0]
    lanes = wq_ref.shape[1] // cores

    def load(n, ref, half):
        return pltpu.make_async_copy(
            ref.at[:, pl.ds(half * lanes, lanes)],
            wall_ref.at[half, rank, pl.ds(n * high, high), :],
            load_sem.at[n, half],
        )

    loads = [load(n, ref, half) for n, ref in enumerate((wq_ref, wk_ref, wv_ref, ck_ref, cv_ref)) for half in range(cores)]
    for copy in loads:
        copy.start()
    meet(plane + [above, below])

    def remote(src, dst, send, recv, device):
        return pltpu.make_async_remote_copy(
            src_ref=src, dst_ref=dst, send_sem=send, recv_sem=recv, device_id=device, device_id_type=MESH
        )

    there = pl.ds((1 - core) * FULL, FULL)
    mine = pl.ds(core * FULL, FULL)
    swap_x = remote(x_ref.at[local, there], xall_ref.at[seq, 1 - core], swap_send.at[0], swap_recv.at[0], sibling)
    swap_g = remote(g_ref.at[local, there], gmine_ref, swap_send.at[1], swap_recv.at[1], sibling)
    swap_e = remote(m_ref.at[local], enc_ref, swap_send.at[2], swap_recv.at[2], sibling)
    own_x = pltpu.make_async_copy(x_ref.at[local, mine], xall_ref.at[seq, core], own_sem.at[3])
    own_g = pltpu.make_async_copy(g_ref.at[local, mine], gmine_ref, own_sem.at[4])
    own_e = pltpu.make_async_copy(m_ref.at[local], enc_ref, own_sem.at[5])

    @pl.when(core == home)
    def _():
        swap_x.start()
        own_x.start()

    def give_index(item, half):
        return remote(
            idx_ref.at[item], iall_ref.at[rank], idx_send.at[item, half], idx_recv.at[rank],
            (half, seq, core * per_core + item),
        )

    def is_me(item, half):
        return (half == core) & (core * per_core + item == rank)

    for item in range(per_core):
        for half in range(cores):

            @pl.when(jnp.logical_not(is_me(item, half)))
            def _():
                give_index(item, half).start()

            @pl.when(is_me(item, half))
            def _():
                own = pltpu.make_async_copy(idx_ref.at[item], iall_ref.at[rank], own_sem.at[0])
                own.start()
                own.wait()

    peers = [(core, seq, lax.rem(rank + step, ranks)) for step in range(1, ranks)]

    def give_vec(step):
        return remote(vec_ref, vall_ref.at[rank], vec_send.at[step], vec_recv.at[step], peers[step - 1])

    for step in range(1, ranks):
        give_vec(step).start()
    own_vec = pltpu.make_async_copy(vec_ref, vall_ref.at[rank], own_sem.at[1])
    own_vec.start()

    weights = PlaneGather(wall_ref, *wsems)

    @pl.when(core == home)
    def _():
        own_x.wait()

    @pl.when(core != home)
    def _():
        swap_x.wait_recv()

    def chain(block, target, way):
        return remote(
            xall_ref.at[block, core], xall_ref.at[block, core], chain_send.at[way, block], chain_recv.at[block], target
        )

    def aside(block):
        return remote(
            xall_ref.at[block, core], xall_ref.at[block, core], side_send.at[block], side_recv.at[block], sibling
        )

    for step in range(depth):
        up, down = seq - step, seq + step

        @pl.when(up >= 0)
        def _():
            if step > 0:
                chain(up, above, 0).wait_recv()

            @pl.when(seq + 1 < depth)
            def _():
                chain(up, above, 0).start()

            aside(up).start()

        @pl.when(down < depth)
        def _():
            if step > 0:
                chain(down, below, 1).wait_recv()

            @pl.when(seq > 0)
            def _():
                chain(down, below, 1).start()

            if step > 0:
                aside(down).start()

        if step == 0:
            for copy in loads:
                copy.wait()
            weights.start()

            @pl.when(core == home)
            def _():
                swap_e.start()
                own_e.start()
                swap_g.start()
                own_g.start()

    weights.forward()

    for step in range(depth):
        up, down = seq - step, seq + step

        @pl.when((up >= 0) & (seq + 1 < depth))
        def _():
            chain(up, above, 0).wait_send()

        @pl.when((down < depth) & (seq > 0))
        def _():
            chain(down, below, 1).wait_send()

    for block in range(depth):
        aside(block).wait()
    for step in range(1, ranks):
        give_vec(step).wait()
    weights.finish()
    own_vec.wait()
    for item in range(per_core):
        for half in range(cores):

            @pl.when(jnp.logical_not(is_me(item, half)))
            def _():
                give_index(item, half).wait_send()

    @pl.when(core == home)
    def _():
        for copy in (swap_x, swap_g, swap_e):
            copy.wait_send()
        own_g.wait()
        own_e.wait()

    @pl.when(core != home)
    def _():
        swap_g.wait_recv()
        swap_e.wait_recv()

    for origin in range(ranks):

        @pl.when(jnp.logical_not((core == home) & (rank == origin)))
        def _():
            remote(
                idx_ref.at[0], iall_ref.at[origin], idx_send.at[0, 0], idx_recv.at[origin], sibling
            ).wait_recv()


def prologue(dec_input, out_grad, encoder_states, retrieved, vectors, weights):
    cores, depth, ranks = lax.axis_size(ITEM), lax.axis_size(SEQ), lax.axis_size(TENSOR)
    per_core, _, width = dec_input.shape
    enc_rows = encoder_states.shape[1]
    high = len(weights) * weights[0].shape[0]
    low = jnp.bfloat16
    dma = pltpu.SemaphoreType.DMA
    return call_kernel(
        functools.partial(prologue_kernel, (cores, depth, ranks, per_core)),
        "prologue",
        [
            ((depth, cores, FULL, width), low),
            ((FULL, width), low),
            ((enc_rows, width), low),
            ((ranks,) + retrieved.shape[1:], retrieved.dtype),
            ((ranks,) + vectors.shape, vectors.dtype),
            ((cores, ranks, high, width // cores), low),
        ],
        [dec_input, out_grad, encoder_states, retrieved, vectors, *weights],
        scratch=[
            dma((len(weights), cores)),
            dma((3,)),
            dma((3,)),
            dma((2, depth)),
            dma((depth,)),
            dma((depth,)),
            dma((depth,)),
            dma((6,)),
            dma((per_core, cores)),
            dma((ranks,)),
            dma((ranks,)),
            dma((ranks,)),
        ]
        + gather_scratch(),
        collective_id=1,
        in_spaces=[pl.ANY] * 10,
        us=32,
    )


def dot_nn(first_op, second_op):
    return lax.dot_general(first_op, second_op, (((1,), (0,)), ((), ())), preferred_element_type=jnp.float32)


def dot_nt(first_op, second_op):
    return lax.dot_general(first_op, second_op, (((1,), (1,)), ((), ())), preferred_element_type=jnp.float32)


def head_rows(ref, group, matrix, head_index, head):
    start = pl.multiple_of(matrix * 3 * head + head_index * head, head)
    rows = pl.ds(start, head)
    return jnp.concatenate([ref[half, group, rows, :] for half in range(ref.shape[0])], axis=1)


def kv_rows(w_ref, group, head_index, head):
    return jnp.concatenate(
        [head_rows(w_ref, group, 3, head_index, head), head_rows(w_ref, group, 4, head_index, head)], axis=0
    )


def retrieve_kernel(ranks, head, enc_ref, w_ref, b_ref, idx_ref, out_ref):
    core, seq, _ = here()
    enc_rows = enc_ref.shape[0]
    slots = idx_ref.shape[2]
    low = jnp.bfloat16
    tall = enc_rows // 3

    def picked(table, index):
        total = jnp.zeros((table.shape[0], index.shape[1]), jnp.float32)
        for part in range(3):
            place = lax.broadcasted_iota(jnp.int32, (tall, index.shape[1]), 0) + (part * tall + seq * enc_rows)
            hot = jnp.where(place == index, 1.0, 0.0).astype(low)
            total = total + dot_nn(table[:, part * tall : (part + 1) * tall], hot)
        return total.astype(low)

    def step(group, carry):
        w = jnp.concatenate([kv_rows(w_ref, group, 2 * core, head), kv_rows(w_ref, group, 1, head)], axis=0)
        table = (dot_nt(w, enc_ref[...]) + b_ref[group]).astype(low)
        whole = idx_ref[group, pl.ds(2 * core, 1), :]
        shared = idx_ref[group, pl.ds(1, 1), :]
        half = jnp.where(core == 0, shared[:, : slots // 2], shared[:, slots // 2 :])
        out_ref[group] = jnp.concatenate(
            [picked(table[: 2 * head], whole), picked(table[2 * head :], half)], axis=1
        )
        return carry

    lax.fori_loop(0, ranks, step, 0)


def retrieve(enc, w_all, bias, index):
    ranks, _, slots = index.shape
    head = w_all.shape[2] // 15
    return call_kernel(
        functools.partial(retrieve_kernel, ranks, head),
        "retrieve",
        ((ranks, 2 * head, slots + slots // 2), jnp.bfloat16),
        [enc, w_all, bias, index],
    )


def assembled(parts_ref, depth, columns=None):
    pieces = []
    for group in range(depth):
        first, second = parts_ref[2 * group], parts_ref[2 * group + 1]
        pieces += [
            first[:, :FULL],
            jnp.concatenate([first[:, FULL:WIDE], second[:, FULL:WIDE]], axis=1),
            second[:, :FULL],
        ]
    return jnp.concatenate(pieces, axis=0)


def dispersed(rows, parts_ref, depth):
    head = rows.shape[0] // (3 * depth)
    for group in range(depth):
        a = rows[3 * group * head : (3 * group + 1) * head]
        b = rows[(3 * group + 1) * head : (3 * group + 2) * head]
        c = rows[(3 * group + 2) * head : (3 * group + 3) * head]
        parts_ref[2 * group] = jnp.concatenate([a, b[:, :HALF]], axis=1)
        parts_ref[2 * group + 1] = jnp.concatenate([c, b[:, HALF:]], axis=1)


def late_square(ref, matrix, rows):
    cores, ranks = ref.shape[0], ref.shape[1]
    return jnp.concatenate(
        [
            jnp.concatenate([ref[half, rank, matrix * rows : (matrix + 1) * rows, :] for half in range(cores)], axis=1)
            for rank in range(ranks)
        ],
        axis=0,
    )


def centred_rows(h):
    center = h - jnp.mean(h, axis=-1, keepdims=True)
    spread = lax.rsqrt(jnp.mean(center * center, axis=-1, keepdims=True) + EPS)
    return center * spread, spread


def norm_back(z, spread, dy, gain):
    dz = dy * gain
    dh = spread * (
        dz - jnp.mean(dz, axis=-1, keepdims=True) - z * jnp.mean(dz * z, axis=-1, keepdims=True)
    )
    return dh, jnp.sum(dy * z, axis=0, keepdims=True), jnp.sum(dy, axis=0, keepdims=True)


def middle_kernel(
    cores, depth, ranks, per_core, part,
    o_ref, y1_ref, g_ref, w_ref, ffn_ref, bo_ref, gain2_ref, shift2_ref, b1_ref, b2_ref, gain3_ref, shift3_ref,
    layer_ref, do_ref, dh2_ref, vec_ref, grad_ref,
    slope_ref, a_ref, df_ref, out_ref, dosrc_ref, dosend, dorecv, *deal_sems
):
    low = jnp.bfloat16
    core, seq, rank = here()
    count = cores * depth
    mine, places = column_places(cores, depth)
    peers = [column_peer(place, cores, rank) for place in places]
    peers += [(half, seq, lax.rem(rank + step, ranks)) for step in range(1, ranks) for half in range(cores)]
    greet(peers)
    width = y1_ref.shape[1]
    lanes = width // cores
    o2t = assembled(o_ref, depth)
    wo2 = late_square(w_ref, 2, part)
    h2 = y1_ref[...].astype(jnp.float32) + dot_nn(o2t.T, wo2) + bo_ref[...]
    z2, spread2 = centred_rows(h2)
    y2 = (z2 * gain2_ref[...] + shift2_ref[...]).astype(low)

    def hidden_in(of, half):
        return ffn_ref[half, of, :width, :]

    def hidden_out(of):
        return jnp.concatenate([ffn_ref[half, of, width:, :] for half in range(cores)], axis=1)

    root = 0.7071067811865476
    h3 = y2.astype(jnp.float32) + b2_ref[...]
    for of in range(ranks):
        f = jnp.concatenate([dot_nn(y2, hidden_in(of, half)) for half in range(cores)], axis=1) + b1_ref[of]
        cdf = 0.5 * (1.0 + lax.erf(f * root))
        a = (f * cdf).astype(low)
        slope_ref[of] = cdf + f * (0.3989422804014327 * jnp.exp(-0.5 * f * f))
        a_ref[of] = a
        h3 = h3 + dot_nn(a, hidden_out(of))
    z3, spread3 = centred_rows(h3)
    out_ref[...] = (z3 * gain3_ref[...] + shift3_ref[...]).astype(low)
    pl.semaphore_wait(pltpu.get_barrier_semaphore(), len(peers))
    deal = Deal(cores, ranks, per_core, lambda target: out_ref, layer_ref, *deal_sems)
    deal.start()

    dh3, gg3, gs3 = norm_back(z3, spread3, g_ref[...].astype(jnp.float32), gain3_ref[...])
    e3 = dh3.astype(low)
    dy2 = dh3
    for of in range(ranks):
        df = (dot_nt(e3, hidden_out(of)) * slope_ref[of]).astype(low)
        df_ref[of] = df
        for half in range(cores):
            dy2 = dy2 + dot_nt(df[:, half * lanes : (half + 1) * lanes], hidden_in(of, half))
    dh2, gg2, gs2 = norm_back(z2, spread2, dy2, gain2_ref[...])
    e2 = dh2.astype(low)
    dispersed(dot_nt(wo2, e2).astype(low), dosrc_ref, depth)
    ask = ColumnSend(cores, depth, dosrc_ref, do_ref, dosend, dorecv)
    for step in range(count - 1):
        ask.copy(step).start()
    do_ref[mine] = dosrc_ref[mine]

    dh2_ref[...] = dh2
    vec_ref[0:1] = gg3
    vec_ref[1:2] = gs3
    vec_ref[2:3] = jnp.sum(e3.astype(jnp.float32), axis=0, keepdims=True)
    vec_ref[3:4] = gg2
    vec_ref[4:5] = gs2
    vec_ref[5:6] = jnp.sum(e2.astype(jnp.float32), axis=0, keepdims=True)
    e3t, y2t, e2t = e3.T, y2.T, e2.T
    pad = jnp.zeros((-part % 128, FULL), low)
    for of in range(ranks):
        df = df_ref[of]
        vec_ref[6 + of : 7 + of] = jnp.sum(df.astype(jnp.float32), axis=0, keepdims=True)
        o2_part = jnp.concatenate([o2t[of * part : (of + 1) * part], pad], axis=0)
        for half in range(cores):
            rows = slice(half * lanes, (half + 1) * lanes)
            grad_ref[half, of, :, :width] = dot_nn(y2t[rows], df).astype(low)
            grad_ref[half, of, :, width : 2 * width] = dot_nn(e3t[rows], a_ref[of]).astype(low)
            grad_ref[half, of, :, 2 * width :] = dot_nt(e2t[rows], o2_part).astype(low)
    ask.finish()
    deal.finish()


def middle(per_core, o2, y1, grad_mine, squares, ffn, vectors):
    cores, depth, ranks = lax.axis_size(ITEM), lax.axis_size(SEQ), lax.axis_size(TENSOR)
    places, head, _ = o2.shape
    rows, width = y1.shape
    part, lanes, hidden = 3 * head, width // cores, width
    low, full = jnp.bfloat16, jnp.float32
    columns = 2 * hidden + part + (-part % 128)
    return call_kernel(
        functools.partial(middle_kernel, cores, depth, ranks, per_core, part),
        "middle",
        [
            ((per_core, cores, rows, width), low),
            (o2.shape, low),
            ((rows, width), full),
            ((6 + ranks, width), full),
            ((cores, ranks, lanes, columns), low),
        ],
        [o2, y1, grad_mine, squares, ffn, *vectors],
        scratch=[
            pltpu.VMEM((ranks, rows, hidden), full),
            pltpu.VMEM((ranks, rows, hidden), low),
            pltpu.VMEM((ranks, rows, hidden), low),
            pltpu.VMEM((rows, width), low),
            pltpu.VMEM(o2.shape, low),
        ]
        + send_scratch(places)
        + deal_scratch(cores, ranks, per_core),
        collective_id=4,
        us=22,
    )


def encoder_back(ranks, head, enc_ref, w_ref, idx_ref, dkv_ref, part_ref, grad_ref):
    core, seq, _ = here()
    low = jnp.bfloat16
    enc_rows, width = enc_ref.shape
    slots = idx_ref.shape[2]
    cores = w_ref.shape[0]
    lanes = width // cores
    part = width // ranks
    fold = enc_rows // (2 * cores)
    enc_t = enc_ref[...].T

    tables = []
    rows_w = []
    for group in range(ranks):
        heads = []
        shared = idx_ref[group, pl.ds(1, 1), :]
        shared = jnp.where(core == 0, shared[:, : slots // 2], shared[:, slots // 2 :])
        for which, index, rows in (
            (2 * core, idx_ref[group, pl.ds(2 * core, 1), :], slice(0, slots)),
            (1, shared, slice(slots, slots + slots // 2)),
        ):
            pieces = []
            for third in range(3):
                tall = enc_rows // 3
                place = lax.broadcasted_iota(jnp.int32, (tall, index.shape[1]), 0) + (third * tall + seq * enc_rows)
                hot = jnp.where(place == index, 1.0, 0.0).astype(low)
                pieces.append(dot_nn(hot, dkv_ref[group, rows, :]).astype(low))
            table = jnp.concatenate(pieces, axis=0)
            heads.append(table)
            tables.append(table)
            rows_w.append(kv_rows(w_ref, group, which, head))
        both = jnp.concatenate(heads, axis=1)
        grad = dot_nn(enc_t, both).astype(low)
        whole, shared = grad[:, : 2 * head], grad[:, 2 * head :]
        blank = jnp.zeros_like(whole)
        left = jnp.where(core == 0, whole, blank)
        right = jnp.where(core == 0, blank, whole)
        for half in range(cores):
            rows = slice(half * lanes, (half + 1) * lanes)
            grad_ref[half, group] = jnp.concatenate([left[rows], shared[rows], right[rows]], axis=1)
    table = jnp.concatenate(tables, axis=1)
    w = jnp.concatenate(rows_w, axis=0)
    for rank in range(ranks):
        cols = w[:, rank * part : (rank + 1) * part]
        flat = dot_nn(table, cols).astype(low)
        for half in range(cores):
            low_rows = flat[2 * half * fold : (2 * half + 1) * fold]
            high_rows = flat[(2 * half + 1) * fold : (2 * half + 2) * fold]
            part_ref[half, rank] = jnp.concatenate([low_rows, high_rows], axis=1)


def last_kernel(
    cores, depth, ranks, per_core,
    parts_ref, dh1_ref, w_ref, encp_ref, self_ref, vec_ref, red2_ref, red4_ref,
    in_ref, enc_ref, wself_ref, vout_ref, w2_ref, w4_ref,
    dx_ref, got_ref, sum_ref, encall_ref, column_ref, group_ref, plane_ref, vcol_ref, vsum_ref, vplane_ref,
    r2_ref, r4_ref,
    swap_sem, col_send, col_recv, vcol_send, vcol_recv, send_sem, recv_sem, vsend, vrecv, vback_send, vback_recv,
    z_send, z_recv, *deal_sems
):
    core, seq, rank = here()
    low = jnp.bfloat16
    head = parts_ref.shape[1]
    part = 3 * head
    count = cores * depth
    mine, places = column_places(cores, depth)
    peers = [(core, seq, lax.rem(rank + step, ranks)) for step in range(1, ranks)]
    others = [(1 - core, seq, peer[2]) for peer in peers]
    greeted = [column_peer(place, cores, rank) for place in places] + peers + others
    meet(greeted)

    swap = remote_copy(encp_ref.at[1 - core], got_ref, swap_sem.at[0], swap_sem.at[1], (1 - core, seq, rank))
    swap.start()
    column = []
    for step, place in enumerate(places):
        target = column_peer(place, cores, rank)
        column.append(
            remote_copy(vec_ref.at[place], vcol_ref.at[mine], vcol_send.at[step], vcol_recv.at[step], target)
        )
        column.append(
            remote_copy(self_ref.at[place], column_ref.at[mine], col_send.at[step], col_recv.at[step], target)
        )
    for copy in column:
        copy.start()
    along = []
    for step in range(1, depth):
        target = lax.rem(seq + step, depth)
        for n, (src, dst) in enumerate(((red2_ref, r2_ref), (red4_ref, r4_ref))):
            along.append(
                remote_copy(
                    src.at[target], dst.at[seq], z_send.at[n, step - 1], z_recv.at[n, step - 1], (core, target, rank)
                )
            )
    for copy in along:
        copy.start()

    dqt = assembled(parts_ref, depth)
    stack_k, stack_v = [], []
    for group in range(depth):
        first, second = parts_ref[2 * group], parts_ref[2 * group + 1]
        for n, stack in ((0, stack_k), (1, stack_v)):
            whole = slice(WIDE + n * FULL, WIDE + (n + 1) * FULL)
            shared = slice(WIDE + (n + 2) * FULL, WIDE + (n + 3) * FULL)
            both = (first[:, shared].astype(jnp.float32) + second[:, shared].astype(jnp.float32)).astype(low)
            stack += [first[:, whole], both, second[:, whole]]
    dx = dh1_ref[...] + dot_nn(dqt.T, late_square(w_ref, 0, part)) * SCALE
    dx = dx + dot_nn(jnp.concatenate(stack_k, axis=0).T, late_square(w_ref, 1, part))
    dx = dx + dot_nn(jnp.concatenate(stack_v, axis=0).T, late_square(w_ref, 2, part))
    dx_ref[...] = dx.astype(low)
    deal = Deal(cores, ranks, per_core, lambda target: dx_ref, in_ref, *deal_sems[:3])
    deal.start()

    swap.wait()
    sum_ref[...] = (encp_ref[core].astype(jnp.float32) + got_ref[...].astype(jnp.float32)).astype(low)
    deal_enc = Deal(cores, ranks, per_core, lambda target: sum_ref.at[target], encall_ref, *deal_sems[3:])
    deal_enc.start()

    for copy in column:
        copy.wait()
    total = vec_ref[mine]
    for place in places:
        total = total + vcol_ref[place]
    vsum_ref[...] = total
    column_ref[mine] = self_ref[mine]
    for group in range(depth):
        first, second = column_ref[2 * group], column_ref[2 * group + 1]
        pieces = []
        for n in range(3):
            whole = slice(2 * n * head, (2 * n + 1) * head)
            shared = slice((2 * n + 1) * head, (2 * n + 2) * head)
            both = (first[:, shared].astype(jnp.float32) + second[:, shared].astype(jnp.float32)).astype(low)
            pieces += [first[:, whole], both, second[:, whole]]
        group_ref[group] = jnp.concatenate(pieces, axis=1)
    plane = []
    for step, peer in enumerate(peers):
        plane.append(remote_copy(vsum_ref, vplane_ref.at[rank], vsend.at[step], vrecv.at[step], peer))
        plane.append(
            remote_copy(group_ref.at[peer[2]], plane_ref.at[rank], send_sem.at[step], recv_sem.at[step], peer)
        )
    for copy in plane:
        copy.start()

    for copy in along:
        copy.wait()
    for src, dst, out in ((red2_ref, r2_ref, w2_ref), (red4_ref, r4_ref, w4_ref)):
        total = src[seq].astype(jnp.float32)
        for step in range(1, depth):
            total = total + dst[lax.rem(seq + step, depth)].astype(jnp.float32)
        out[...] = total

    for copy in plane:
        copy.wait()
    vplane_ref[rank] = vsum_ref[...]
    total = vplane_ref[0]
    for origin in range(1, ranks):
        total = total + vplane_ref[origin]
    vout_ref[mine] = total
    vectors = []
    for step, place in enumerate(places):
        vectors.append(
            remote_copy(
                vout_ref.at[mine], vout_ref.at[mine], vback_send.at[step], vback_recv.at[step],
                column_peer(place, cores, rank),
            )
        )
    for copy in vectors:
        copy.start()
    total = group_ref[rank].astype(jnp.float32)
    for step in range(1, ranks):
        total = total + plane_ref[lax.rem(rank + step, ranks)].astype(jnp.float32)
    wself_ref[...] = total
    deal_enc.finish()
    fold = encall_ref.shape[2]
    for item in range(per_core):
        for half in range(cores):
            for side in range(2):
                rows = slice((2 * half + side) * fold, (2 * half + side + 1) * fold)
                enc_ref[item, rows, :] = encall_ref[item, half, :, side * part : (side + 1) * part]
    for copy in vectors:
        copy.wait()
    deal.finish()


def last_rows(per_core, dqkv, dh1, early, enc_parts, self_parts, vectors, second, fourth):
    cores, depth, ranks = lax.axis_size(ITEM), lax.axis_size(SEQ), lax.axis_size(TENSOR)
    places, head, _ = dqkv.shape
    rows, width = dh1.shape
    low, full = jnp.bfloat16, jnp.float32
    dma = pltpu.SemaphoreType.DMA
    _, high, lanes = self_parts.shape
    wide = lanes // 2 * 3
    _, _, fold, side = enc_parts.shape
    columns = second.shape[1]
    second = second.reshape(depth, -1, columns)
    fourth = fourth.reshape(depth, -1, columns)
    along = second.shape[1]
    return call_kernel(
        functools.partial(last_kernel, cores, depth, ranks, per_core),
        "last_rows",
        [
            ((per_core, cores, rows, width), low),
            ((per_core, 2 * cores * fold, side // 2), low),
            ((high, wide), full),
            (vectors.shape, full),
            ((along, columns), full),
            ((along, columns), full),
        ],
        [dqkv, dh1, early, enc_parts, self_parts, vectors, second, fourth],
        scratch=[
            pltpu.VMEM((rows, width), low),
            pltpu.VMEM(enc_parts.shape[1:], low),
            pltpu.VMEM(enc_parts.shape[1:], low),
            pltpu.VMEM((per_core, cores, fold, side), low),
            pltpu.VMEM(self_parts.shape, low),
            pltpu.VMEM((depth, high, wide), low),
            pltpu.VMEM((ranks, high, wide), low),
            pltpu.VMEM(vectors.shape, full),
            pltpu.VMEM(vectors.shape[1:], full),
            pltpu.VMEM((ranks,) + vectors.shape[1:], full),
            pltpu.VMEM(second.shape, low),
            pltpu.VMEM(fourth.shape, low),
            dma((2,)),
        ]
        + send_scratch(places)
        + send_scratch(places)
        + [dma((ranks - 1,)) for _ in range(4)]
        + send_scratch(places)
        + [dma((2, depth - 1)), dma((2, depth - 1))]
        + deal_scratch(cores, ranks, per_core)
        + deal_scratch(cores, ranks, per_core),
        collective_id=7,
        us=30,
    )


def self_grads(blocks, cores, places, x_ref, g_ref, out_ref):
    core, seq, rank = here()
    low = jnp.bfloat16
    head = g_ref.shape[1]
    width = x_ref.shape[2]
    rows = width // places
    total = jnp.zeros((width, 6 * head), jnp.float32)
    sums = jnp.zeros((16, 6 * head), jnp.float32)
    ones = jnp.ones((16, FULL), low)
    zero = jnp.zeros((head, HALF), low)
    for block in range(blocks):
        g = g_ref[block]
        shared = jnp.where(
            core == 0,
            jnp.concatenate([g[:, FULL:WIDE], zero], axis=1),
            jnp.concatenate([zero, g[:, FULL:WIDE]], axis=1),
        )
        flat = jnp.concatenate(
            [g[:, :FULL], shared]
            + [g[:, WIDE + n * FULL : WIDE + (n + 1) * FULL] for n in (0, 2, 1, 3)],
            axis=0,
        )
        total = total + dot_nt(x_ref[block].T, flat)
        sums = sums + dot_nt(ones, flat)
    for place in range(places):
        start = ((place % cores) * (places // cores) + place // cores) * rows
        out_ref[place, :rows, :] = total[start : start + rows].astype(low)
        out_ref[place, rows:, :] = sums.astype(low)


def widen(block):
    lane = lax.broadcasted_iota(jnp.int32, block.shape, 1)
    zero = jnp.zeros_like(block)
    return jnp.concatenate([jnp.where(lane < FULL, block, zero), jnp.where(lane < FULL, zero, block)], axis=0)


def narrow(block):
    head = block.shape[0] // 2
    return jnp.concatenate([block[:head, :FULL], block[head:, FULL:]], axis=1)


def causal_block(core):
    key = lax.broadcasted_iota(jnp.int32, (FULL, WIDE), 0)
    lane = lax.broadcasted_iota(jnp.int32, (FULL, WIDE), 1)
    token = jnp.where(lane < FULL, lane, lane - FULL + HALF * core)
    return key <= token


def attend_block(block, causal, core, slots, q, k_ref, vt_ref, s_ref):
    low = jnp.bfloat16
    head = q.shape[0]
    wide = widen(q)
    last = block if causal else slots // FULL

    def rows_of(key_block):
        return pl.ds(pl.multiple_of(key_block * FULL, FULL), FULL)

    def top_of(s):
        return jnp.max(s.reshape(FULL // 8, 8, WIDE), axis=0)

    def look(key_block, top):
        rows = rows_of(key_block)
        s = dot_nn(k_ref[rows, :], wide)
        s_ref[rows, :] = s
        return jnp.maximum(top, top_of(s))

    top = lax.fori_loop(0, last, look, jnp.full((8, WIDE), NEG, jnp.float32))
    if causal:
        rows = rows_of(block)
        s = jnp.where(causal_block(core), dot_nn(k_ref[rows, :], wide), NEG)
        s_ref[rows, :] = s
        top = jnp.maximum(top, top_of(s))
        last = block + 1
    top = jnp.max(top, axis=0, keepdims=True)

    def gather(key_block, state):
        total, out = state
        rows = rows_of(key_block)
        p = jnp.exp(s_ref[rows, :] - top)
        total = total + jnp.sum(p.reshape(FULL // 8, 8, WIDE), axis=0)
        out = out + dot_nn(vt_ref[:, rows], p.astype(low))
        return total, out

    total, out = lax.fori_loop(
        0, last, gather, (jnp.zeros((8, WIDE), jnp.float32), jnp.zeros((2 * head, WIDE), jnp.float32))
    )
    total = jnp.sum(total, axis=0, keepdims=True)
    return (narrow(out) / total).astype(low), top + jnp.log(total)


def self_kernel(
    cores, depth, ranks,
    x_ref, w_ref, b_ref, wo1_ref, wq2_ref, wo2_ref,
    q_ref, k_ref, kt_ref, v_ref, vt_ref, o_ref, lse_ref, oall_ref, wall_ref,
    group_ref, s_ref, load_sem, group_sem, osend, orecv, *wsems
):
    core, seq, rank = here()
    low = jnp.bfloat16
    blocks = cores * depth
    head = q_ref.shape[1]
    high = wo1_ref.shape[0]
    lanes = wo1_ref.shape[1] // cores

    def load(n, ref, half):
        return pltpu.make_async_copy(
            ref.at[:, pl.ds(half * lanes, lanes)],
            wall_ref.at[half, rank, pl.ds(n * high, high), :],
            load_sem.at[n, half],
        )

    loads = [load(n, ref, half) for n, ref in enumerate((wo1_ref, wq2_ref, wo2_ref)) for half in range(cores)]
    groups = [pltpu.make_async_copy(w_ref.at[half, seq], group_ref.at[half, 0], group_sem.at[half]) for half in range(cores)]
    for copy in groups + loads:
        copy.start()
    mine, places = column_places(cores, depth)
    gather = PlaneGather(wall_ref, *wsems)
    peers = [column_peer(place, cores, rank) for place in places] + gather.peers
    greet(peers)

    for copy in groups + loads:
        copy.wait()
    pl.semaphore_wait(pltpu.get_barrier_semaphore(), len(peers))
    gather.start()

    w = jnp.concatenate(
        [head_rows(group_ref, 0, n, which, head) for n in range(3) for which in (2 * core, 1)], axis=0
    )
    bias = b_ref[...]

    def project(block, carry):
        lanes = pl.ds(pl.multiple_of(block * FULL, FULL), FULL)
        flat = dot_nt(w, x_ref[block])
        q = ((flat[: 2 * head] + bias[: 2 * head]) * SCALE).astype(low)
        shared = jnp.where(core == 0, q[head:, :HALF], q[head:, HALF:])
        q_ref[block] = jnp.concatenate([q[:head], shared], axis=1)
        k = flat[2 * head : 4 * head].astype(low)
        v = (flat[4 * head :] + bias[2 * head :]).astype(low)
        kt_ref[:, lanes] = k
        vt_ref[:, lanes] = v
        k_ref[lanes, :] = k.T
        v_ref[lanes, :] = v.T
        return carry

    lax.fori_loop(0, blocks, project, 0)

    back = ColumnSend(cores, depth, o_ref, oall_ref, osend, orecv)

    def attend(block):
        out, lse = attend_block(block, True, core, blocks * FULL, q_ref[block], k_ref, vt_ref, s_ref)
        o_ref[block] = out
        lse_ref[block] = lse
        return out

    def step(n, carry):
        attend(lax.rem(mine + 1 + n, blocks))
        back.copy(n).start()
        return carry

    lax.fori_loop(0, blocks - 1, step, 0)
    gather.forward()
    oall_ref[mine] = attend(mine)
    back.finish()
    gather.finish()


def attend_self(x_all, w_all, bias, head, wo1, wq2, wo2):
    cores, depth, ranks = lax.axis_size(ITEM), lax.axis_size(SEQ), lax.axis_size(TENSOR)
    places = cores * depth
    rows = places * FULL
    low = jnp.bfloat16
    dma = pltpu.SemaphoreType.DMA
    _, _, high, lanes = w_all.shape
    return call_kernel(
        functools.partial(self_kernel, cores, depth, ranks),
        "attend_self",
        [
            ((places, head, WIDE), low),
            ((rows, 2 * head), low),
            ((2 * head, rows), low),
            ((rows, 2 * head), low),
            ((2 * head, rows), low),
            ((places, head, WIDE), low),
            ((places, 1, WIDE), jnp.float32),
            ((places, head, WIDE), low),
            ((cores, ranks, 3 * wo1.shape[0], lanes), low),
        ],
        [x_all, w_all, bias, wo1, wq2, wo2],
        scratch=[
            pltpu.VMEM((cores, 1, high, lanes), low),
            pltpu.VMEM((rows, WIDE), jnp.float32),
            dma((3, cores)),
            dma((cores,)),
        ]
        + send_scratch(places)
        + gather_scratch(),
        collective_id=2,
        in_spaces=[pltpu.VMEM, pl.ANY, pltpu.VMEM, pl.ANY, pl.ANY, pl.ANY],
        us=30,
    )


def cross_kernel(
    cores, depth, part,
    o_ref, x_ref, w_ref, bo_ref, gain_ref, shift_ref, bq_ref, kv_ref,
    h_ref, y_ref, q_ref, k_ref, kt_ref, v_ref, parts_ref, lse_ref, oall_ref,
    qsrc_ref, half_ref, other_ref, vt_ref, s_ref, swap_sem, qsend, qrecv, osend, orecv,
):
    core, seq, rank = here()
    low = jnp.bfloat16
    count = cores * depth
    mine, places = column_places(cores, depth)
    peers = [column_peer(place, cores, rank) for place in places]
    greet(peers)
    slots, head = k_ref.shape[0], q_ref.shape[1]
    half_ref[...] = kv_ref[:, slots:]

    o1 = assembled(o_ref, depth).T
    h1 = x_ref[...].astype(jnp.float32) + dot_nn(o1, late_square(w_ref, 0, part)) + bo_ref[...]
    z, _ = centred_rows(h1)
    y1 = (z * gain_ref[...] + shift_ref[...]).astype(low)
    h_ref[...] = h1
    y_ref[...] = y1
    q2t = ((dot_nt(late_square(w_ref, 1, part), y1) + bq_ref[...]) * SCALE).astype(low)
    dispersed(q2t, qsrc_ref, depth)

    pl.semaphore_wait(pltpu.get_barrier_semaphore(), len(peers))
    ask = ColumnSend(cores, depth, qsrc_ref, q_ref, qsend, qrecv)
    swap = remote_copy(half_ref, other_ref, swap_sem.at[0], swap_sem.at[1], (1 - core, seq, rank))
    swap.start()
    for step in range(count - 1):
        ask.copy(step).start()
    q_ref[mine] = qsrc_ref[mine]
    swap.wait()
    whole = kv_ref[:, :slots]
    half, other = half_ref[...], other_ref[...]
    shared = jnp.concatenate([jnp.where(core == 0, half, other), jnp.where(core == 0, other, half)], axis=1)
    kt = jnp.concatenate([whole[:head], shared[:head]], axis=0)
    vt = jnp.concatenate([whole[head:], shared[head:]], axis=0)
    kt_ref[...] = kt
    vt_ref[...] = vt
    k_ref[...] = kt.T
    v_ref[...] = vt.T

    back = ColumnSend(cores, depth, parts_ref, oall_ref, osend, orecv)

    def attend(block):
        out, lse = attend_block(block, False, core, slots, q_ref[block], k_ref, vt_ref, s_ref)
        parts_ref[block] = out
        lse_ref[block] = lse
        return out

    oall_ref[mine] = attend(mine)

    def step(n, carry):
        ask.wait_from(n)
        attend(lax.rem(mine + count - 1 - n, count))
        back.copy(count - 2 - n).start()
        return carry

    lax.fori_loop(0, count - 1, step, 0)
    ask.finish_sends()
    back.finish()


def attend_cross(o1, x_mine, squares, bo, gain, shift, bq, kv_mine, slots):
    cores, depth = lax.axis_size(ITEM), lax.axis_size(SEQ)
    places, head, _ = o1.shape
    rows, width = x_mine.shape
    low, full = jnp.bfloat16, jnp.float32
    parts = (places, head, WIDE)
    return call_kernel(
        functools.partial(cross_kernel, cores, depth, 3 * head),
        "attend_cross",
        [
            ((rows, width), full),
            ((rows, width), low),
            (parts, low),
            ((slots, 2 * head), low),
            ((2 * head, slots), low),
            ((slots, 2 * head), low),
            (parts, low),
            ((places, 1, WIDE), full),
            (parts, low),
        ],
        [o1, x_mine, squares, bo, gain, shift, bq, kv_mine],
        scratch=[
            pltpu.VMEM(parts, low),
            pltpu.VMEM((2 * head, slots // 2), low),
            pltpu.VMEM((2 * head, slots // 2), low),
            pltpu.VMEM((2 * head, slots), low),
            pltpu.VMEM((slots, WIDE), full),
            pltpu.SemaphoreType.DMA((2,)),
        ]
        + send_scratch(places)
        + send_scratch(places),
        collective_id=3,
        us=28,
    )


def back_block(block, causal, core, slots, q, do, o, lse, k_ref, kt_ref, v_ref, whole_ref, shared_ref):
    low = jnp.bfloat16
    head = q.shape[0]
    wide_q, wide_do = widen(q), widen(do)
    delta = jnp.sum(do.astype(jnp.float32) * o.astype(jnp.float32), axis=0, keepdims=True)
    qd = jnp.concatenate([q, jnp.zeros_like(q)], axis=0).T
    dd = jnp.concatenate([jnp.zeros_like(do), do], axis=0).T
    mix_whole = jnp.concatenate([qd[:FULL], dd[:FULL]], axis=0)
    mix_shared = jnp.concatenate([qd[FULL:], dd[FULL:]], axis=0)

    def one(key_block, dq, masked):
        rows = pl.ds(pl.multiple_of(key_block * FULL, FULL), FULL)
        s = dot_nn(k_ref[rows, :], wide_q)
        if masked:
            s = jnp.where(causal_block(core), s, NEG)
        p = jnp.exp(s - lse)
        dp = dot_nn(v_ref[rows, :], wide_do)
        ds = (p * (dp - delta)).astype(low)
        p = p.astype(low)
        dq = dq + dot_nn(kt_ref[:, rows], ds)
        whole_ref[rows, :] += dot_nn(jnp.concatenate([ds[:, :FULL], p[:, :FULL]], axis=1), mix_whole)
        shared_ref[rows, :] += dot_nn(jnp.concatenate([ds[:, FULL:], p[:, FULL:]], axis=1), mix_shared)
        return dq

    last = block if causal else slots // FULL
    dq = lax.fori_loop(0, last, lambda kb, dq: one(kb, dq, False), jnp.zeros((2 * head, WIDE), jnp.float32))
    if causal:
        dq = one(block, dq, True)
    return narrow(dq).astype(low)


def cross_back_kernel(
    cores, depth,
    q_ref, k_ref, kt_ref, v_ref, o_ref, lse_ref, do_ref,
    dqall_ref, dkv_ref,
    dq_ref, whole_ref, shared_ref, give_ref, got_ref, swap_sem, send_sem, recv_sem,
):
    core, seq, rank = here()
    low = jnp.bfloat16
    count = cores * depth
    mine, places = column_places(cores, depth)
    peers = [column_peer(place, cores, rank) for place in places]
    greet(peers)
    slots = k_ref.shape[0]
    whole_ref[...] = jnp.zeros_like(whole_ref)
    shared_ref[...] = jnp.zeros_like(shared_ref)
    back = ColumnSend(cores, depth, dq_ref, dqall_ref, send_sem, recv_sem)

    def go(block):
        return back_block(
            block, False, core, slots, q_ref[block], do_ref[block], o_ref[block], lse_ref[block],
            k_ref, kt_ref, v_ref, whole_ref, shared_ref,
        )

    dq_ref[places[0]] = go(places[0])
    pl.semaphore_wait(pltpu.get_barrier_semaphore(), len(peers))
    back.copy(0).start()

    def step(n, carry):
        block = lax.rem(mine + 1 + n, count)
        dq_ref[block] = go(block)
        back.copy(n).start()
        return carry

    lax.fori_loop(1, count - 1, step, 0)
    dqall_ref[mine] = go(mine)
    half = slots // 2
    give_ref[...] = shared_ref[pl.ds(pl.multiple_of((1 - core) * half, half), half), :].astype(low)
    swap = remote_copy(give_ref, got_ref, swap_sem.at[0], swap_sem.at[1], (1 - core, seq, rank))
    swap.start()
    dkv_ref[:slots] = whole_ref[...].astype(low)
    swap.wait()
    kept = shared_ref[pl.ds(pl.multiple_of(core * half, half), half), :]
    dkv_ref[slots:] = (kept + got_ref[...].astype(jnp.float32)).astype(low)
    back.finish()


def attend_cross_back(q, k, kt, v, o, lse, do):
    cores, depth = lax.axis_size(ITEM), lax.axis_size(SEQ)
    places, head, _ = q.shape
    slots = k.shape[0]
    low = jnp.bfloat16
    sums = pltpu.VMEM((slots, 2 * head), jnp.float32)
    return call_kernel(
        functools.partial(cross_back_kernel, cores, depth),
        "back_cross",
        [(q.shape, low), ((slots + slots // 2, 2 * head), low)],
        [q, k, kt, v, o, lse, do],
        scratch=[
            pltpu.VMEM(q.shape, low),
            sums,
            sums,
            pltpu.VMEM((slots // 2, 2 * head), low),
            pltpu.VMEM((slots // 2, 2 * head), low),
            pltpu.SemaphoreType.DMA((2,)),
        ]
        + send_scratch(places),
        collective_id=5,
        us=24,
    )


def self_back_kernel(
    cores, depth, ranks, part,
    dq2_ref, dh2_ref, h1_ref, y1_ref, oin_ref, w_ref, gain_ref,
    q_ref, k_ref, kt_ref, v_ref, o_ref, lse_ref, dkv_ref, enc_ref, early_ref, idx_ref, x_ref,
    dh1_ref, vec_ref, gall_ref, self_ref, encp_ref, second_ref, fourth_ref,
    dosrc_ref, do_ref, g_ref, whole_ref, shared_ref, dkvall_ref, grad2_ref, grad4_ref,
    dosend, dorecv, gsend, grecv, kvsend, kvrecv, *reduce_refs
):
    core, seq, rank = here()
    low = jnp.bfloat16
    count = cores * depth
    head = part // 3
    mine, places = column_places(cores, depth)
    first = PlaneReduce(ranks, grad2_ref, *reduce_refs[:6])
    second = PlaneReduce(ranks, grad4_ref, *reduce_refs[6:])
    peers = [column_peer(place, cores, rank) for place in places] + first.peers
    greet(peers)
    chain = Chain(depth, dkvall_ref, kvsend, kvrecv)

    width = y1_ref.shape[1]
    lanes = width // cores
    dq2t = assembled(dq2_ref, depth)
    dy1 = dh2_ref[...] + dot_nn(dq2t.T, late_square(w_ref, 1, part)) * SCALE
    z1, spread1 = centred_rows(h1_ref[...])
    dh1, gg1, gs1 = norm_back(z1, spread1, dy1, gain_ref[...])
    e1 = dh1.astype(low)
    dispersed(dot_nt(late_square(w_ref, 0, part), e1).astype(low), dosrc_ref, depth)
    pl.semaphore_wait(pltpu.get_barrier_semaphore(), len(peers))
    ask = ColumnSend(cores, depth, dosrc_ref, do_ref, dosend, dorecv)
    for step in range(count - 1):
        ask.copy(step).start()
    do_ref[mine] = dosrc_ref[mine]
    dkvall_ref[seq] = dkv_ref[...]
    dh1_ref[...] = dh1
    vec_ref[0:1] = gg1
    vec_ref[1:2] = gs1
    vec_ref[2:3] = jnp.sum(e1.astype(jnp.float32), axis=0, keepdims=True)
    ones = jnp.ones((8, FULL), low)
    vec_ref[3:4] = dot_nt(ones, dq2t)[0:1] * SCALE
    o1t = assembled(oin_ref, depth)
    both = jnp.concatenate([y1_ref[...].T, e1.T], axis=1)
    blank = jnp.zeros((part, FULL), low)
    for to in range(ranks):
        rows = slice(to * part, (to + 1) * part)
        right = jnp.concatenate(
            [
                jnp.concatenate([dq2t[rows], blank], axis=1),
                jnp.concatenate([blank, o1t[rows]], axis=1),
            ],
            axis=0,
        )
        for half in range(cores):
            grad2_ref[half, to] = dot_nt(both[half * lanes : (half + 1) * lanes], right).astype(low)
    first.start()

    whole_ref[...] = jnp.zeros_like(whole_ref)
    shared_ref[...] = jnp.zeros_like(shared_ref)
    for step in range(count - 1):
        ask.wait_from(step)
    chain.step(0)

    back = ColumnSend(cores, depth, g_ref, gall_ref, gsend, grecv)

    def go(block):
        g_ref[block, :, :WIDE] = back_block(
            block, True, core, count * FULL, q_ref[block], do_ref[block], o_ref[block], lse_ref[block],
            k_ref, kt_ref, v_ref, whole_ref, shared_ref,
        )
        rows = pl.ds(pl.multiple_of(block * FULL, FULL), FULL)
        whole = whole_ref[rows, :].T.astype(low)
        shared = shared_ref[rows, :].T.astype(low)
        g_ref[block, :, WIDE:] = jnp.concatenate([whole[:head], whole[head:], shared[:head], shared[head:]], axis=1)

        @pl.when(block != mine)
        def _():
            back.copy(lax.rem(block + 2 * count - mine - 1, count)).start()

        @pl.when(block == mine)
        def _():
            gall_ref[mine] = g_ref[mine]

    def step(n, carry):
        go(count - 1 - n)
        return carry

    lax.fori_loop(0, 2, step, 0)
    first.middle()
    chain.step(1)
    lax.fori_loop(2, 4, step, 0)
    for n in range(2, depth):
        chain.step(n)
    lax.fori_loop(4, count, step, 0)

    encoder_back(ranks, head, enc_ref, early_ref, idx_ref, dkvall_ref, encp_ref, grad4_ref)
    second.start()
    self_grads(count, cores, count, x_ref, g_ref, self_ref)
    second.middle()
    second_ref[...] = first.finish().astype(low)
    chain.finish()
    ask.finish_sends()
    back.finish()
    fourth_ref[...] = second.finish().astype(low)


def attend_self_back(*args):
    cores, depth, ranks = lax.axis_size(ITEM), lax.axis_size(SEQ), lax.axis_size(TENSOR)
    dq2, dh2, h1, y1, o1, squares, gain, q, k, kt, v, o, lse, dkv, enc, early, index, x_all = args
    places, head, _ = q.shape
    rows, width = y1.shape
    low, full = jnp.bfloat16, jnp.float32
    part, lanes = 3 * head, width // cores
    all_rows = places * rows
    dma = pltpu.SemaphoreType.DMA
    grads = (cores, ranks, lanes, 2 * part)
    message = (places, head, WIDE + 4 * FULL)
    sums = pltpu.VMEM((all_rows, 2 * head), full)
    return call_kernel(
        functools.partial(self_back_kernel, cores, depth, ranks, part),
        "back_self",
        [
            ((rows, width), full),
            ((4, width), full),
            (message, low),
            ((places, width // places + 16, 6 * head), low),
            ((cores, ranks, enc.shape[0] // (2 * cores), 2 * part), low),
            ((lanes, 2 * part), low),
            ((lanes, 2 * part), low),
        ],
        list(args),
        scratch=[
            pltpu.VMEM(q.shape, low),
            pltpu.VMEM(q.shape, low),
            pltpu.VMEM(message, low),
            sums,
            sums,
            pltpu.VMEM((depth,) + dkv.shape, low),
            pltpu.VMEM(grads, low),
            pltpu.VMEM(grads, low),
        ]
        + send_scratch(places)
        + send_scratch(places)
        + [dma((2, depth)), dma((depth,))]
        + reduce_scratch(ranks, lanes, 2 * part, low)
        + reduce_scratch(ranks, lanes, 2 * part, low),
        collective_id=6,
        us=60,
    )


def column_body(
    dec_input,
    encoder_states,
    retrieved,
    self_wq,
    self_bq,
    self_wk,
    self_wv,
    self_bv,
    self_wo,
    self_bo,
    norm1_gain,
    norm1_bias,
    cross_wq,
    cross_bq,
    cross_wk,
    cross_wv,
    cross_bv,
    cross_wo,
    cross_bo,
    norm2_gain,
    norm2_bias,
    ffn_w1,
    ffn_b1,
    ffn_w2,
    ffn_b2,
    norm3_gain,
    norm3_bias,
    out_grad,
):
    low, full = jnp.bfloat16, jnp.float32
    core, seq, rank = here()
    cores, depth, ranks = lax.axis_size(ITEM), lax.axis_size(SEQ), lax.axis_size(TENSOR)
    per_core, _, width = dec_input.shape
    slots = retrieved.shape[2]
    part = self_wq.shape[1]
    head = part // 3
    places = cores * depth
    lanes = width // cores
    hidden = ffn_w1.shape[1]

    def row(vector):
        return vector.reshape(1, width)

    vectors = jnp.concatenate([self_bq, self_bv, cross_bq, cross_bv, ffn_b1]).reshape(-1, 128)
    x_all, grad_mine, enc, index, vectors, early = prologue(
        dec_input, out_grad, encoder_states, retrieved, vectors, [self_wq.T, self_wk.T, self_wv.T, cross_wk.T, cross_wv.T]
    )
    ffn = jnp.concatenate(
        [lax.dynamic_slice_in_dim(w, core * lanes, lanes, axis=1) for w in (ffn_w1, ffn_w2)], axis=0
    )
    ffn = lax.optimization_barrier((ffn, index))[0]
    ffn = lax.all_gather(ffn, TENSOR, axis=0, tiled=False)
    x_mine = x_all[seq, core]
    x_all = x_all.reshape(places, FULL, width)
    vectors = vectors.reshape(ranks, -1)
    all_bq1, all_bv1, all_bq2, all_bv2 = [vectors[:, n * part : (n + 1) * part] for n in range(4)]
    all_b1 = vectors[:, 4 * part :].reshape(ranks, 1, hidden)

    by_head = all_bv2.reshape(ranks, 3, 1, head)
    blank = jnp.zeros((ranks, 2, head), full)
    two = jnp.concatenate([lax.dynamic_slice_in_dim(by_head, 2 * core, 1, axis=1), by_head[:, 1:2]], axis=1)
    bias_kv = jnp.concatenate([blank[:, :, None], two], axis=2).reshape(ranks, 4 * head, 1)
    pieces = retrieve(enc, early, bias_kv, index)
    kv_mine = lax.psum_scatter(pieces, SEQ, scatter_dimension=0, tiled=False)

    def two_heads(rows):
        rows = lax.dynamic_index_in_dim(rows, seq, 0, keepdims=False).reshape(3, head)
        return jnp.concatenate([lax.dynamic_slice_in_dim(rows, 2 * core, 1, axis=0), rows[1:2]], axis=0)

    bias = jnp.concatenate([two_heads(all_bq1), two_heads(all_bv1)], axis=0).reshape(4 * head, 1)
    q1, k1, k1t, v1, v1t, o1_parts, lse1, o1, squares = attend_self(
        x_all, early, bias, head, self_wo, cross_wq.T, cross_wo
    )

    h1, y1, q2, k2, k2t, v2, o2_parts, lse2, o2 = attend_cross(
        o1, x_mine, squares, row(self_bo), row(norm1_gain), row(norm1_bias), all_bq2.reshape(width, 1), kv_mine, slots
    )
    ffn = lax.optimization_barrier((ffn, o1))[0]
    ffn = lax.all_gather(ffn, ITEM, axis=0, tiled=False)
    layer_out, do2, dh2, vec_mid, grad_mid = middle(
        per_core,
        o2,
        y1,
        grad_mine,
        squares,
        ffn,
        [
            row(cross_bo),
            row(norm2_gain),
            row(norm2_bias),
            all_b1,
            row(ffn_b2),
            row(norm3_gain),
            row(norm3_bias),
        ],
    )
    layer_out = layer_out.reshape(per_core, cores * FULL, width)
    first_sum = lax.psum_scatter(grad_mid, ITEM, scatter_dimension=0, tiled=False)
    dq2, dkv2 = attend_cross_back(q2, k2, k2t, v2, o2_parts, lse2, do2)
    dq2, first_sum = lax.optimization_barrier((dq2, first_sum))
    first_sum = lax.psum_scatter(first_sum, TENSOR, scatter_dimension=0, tiled=False)
    dh1, vec_second, dqkv, self_parts, enc_parts, second_sum, fourth_sum = attend_self_back(
        dq2, dh2, h1, y1, o1, squares, row(norm1_gain),
        q1, k1, k1t, v1, o1_parts, lse1, dkv2, enc, early, index, x_all,
    )
    first_sum = lax.psum_scatter(first_sum, SEQ, scatter_dimension=0, tiled=True)

    dv_heads = [jnp.sum(rows[:, head:].astype(full), axis=0) for rows in (dkv2[:slots], dkv2[slots:])]
    slot_of = jnp.arange(3 * depth)[:, None]
    bv_rows = jnp.where(slot_of == 3 * seq + 2 * core, dv_heads[0], 0.0) + jnp.where(
        slot_of == 3 * seq + 1, dv_heads[1], 0.0
    )
    vectors = jnp.concatenate([vec_mid, vec_second, bv_rows.reshape(1, width)], axis=0)
    count = vectors.shape[0]
    piece = 16 * 128
    vectors = jnp.pad(vectors.reshape(-1), (0, places * piece - count * width)).reshape(places, 16, 128)
    input_grad, encoder_grad, third_sum, summed, second_sum, fourth_sum = last_rows(
        per_core, dqkv, dh1, early, enc_parts, self_parts, vectors, second_sum, fourth_sum
    )
    input_grad = input_grad.reshape(per_core, cores * FULL, width)
    summed = summed.reshape(-1)[: count * width].reshape(count, width)

    rows = width // places
    first_sum = first_sum.astype(full)
    gself_wq = third_sum[:rows, :part] * SCALE
    gself_wk = third_sum[:rows, part : 2 * part]
    gself_wv = third_sum[:rows, 2 * part :]
    gself_bq = third_sum[rows, :part] * SCALE
    gself_bv = third_sum[rows, 2 * part :]
    gffn_w1 = first_sum[:, :hidden]
    gffn_w2 = first_sum[:, hidden : 2 * hidden].T
    gcross_wo = first_sum[:, 2 * hidden : 2 * hidden + part].T
    gcross_wq = second_sum[:, :part] * SCALE
    gself_wo = second_sum[:, part:].T
    grad_kv = fourth_sum.reshape(rows, 3, 2, head)
    gcross_wk = grad_kv[:, :, 0].reshape(rows, part)
    gcross_wv = grad_kv[:, :, 1].reshape(rows, part)

    gnorm3_gain, gnorm3_bias, gffn_b2, gnorm2_gain, gnorm2_bias, gcross_bo = [summed[n] for n in range(6)]
    gffn_b1 = lax.dynamic_index_in_dim(summed[6 : 6 + ranks], rank, 0, keepdims=False)
    gnorm1_gain, gnorm1_bias, gself_bo = [summed[6 + ranks + n] for n in range(3)]

    def rank_part(vector):
        return lax.dynamic_slice_in_dim(vector, rank * part, part)

    gcross_bq = rank_part(summed[9 + ranks])
    gcross_bv = rank_part(summed[10 + ranks])
    return (
        layer_out,
        input_grad,
        encoder_grad,
        gself_wq,
        gself_bq,
        gself_wk,
        gself_wv,
        gself_bv,
        gself_wo,
        gself_bo,
        gnorm1_gain,
        gnorm1_bias,
        gcross_wq,
        gcross_bq,
        gcross_wk,
        gcross_wv,
        gcross_bv,
        gcross_wo,
        gcross_bo,
        gnorm2_gain,
        gnorm2_bias,
        gffn_w1,
        gffn_b1,
        gffn_w2,
        gffn_b2,
        gnorm3_gain,
        gnorm3_bias,
    )


def solution(mesh):
    placed = (
        P(ITEM, SEQ, None),
        P(ITEM, SEQ, None),
        P(ITEM, TENSOR, None),
        P(None, TENSOR),
        P(TENSOR),
        P(None, TENSOR),
        P(None, TENSOR),
        P(TENSOR),
        P(TENSOR, None),
        P(),
        P(),
        P(),
        P(None, TENSOR),
        P(TENSOR),
        P(None, TENSOR),
        P(None, TENSOR),
        P(TENSOR),
        P(TENSOR, None),
        P(),
        P(),
        P(),
        P(None, TENSOR),
        P(TENSOR),
        P(TENSOR, None),
        P(),
        P(),
        P(),
        P(ITEM, SEQ, None),
    )
    reduced = (
        P(ITEM, SEQ, None),
        P(ITEM, SEQ, None),
        P(ITEM, SEQ, TENSOR),
        P((ITEM, SEQ), TENSOR),
        P(TENSOR),
        P((ITEM, SEQ), TENSOR),
        P((ITEM, SEQ), TENSOR),
        P(TENSOR),
        P(TENSOR, (ITEM, SEQ)),
        P(),
        P(),
        P(),
        P((ITEM, SEQ), TENSOR),
        P(TENSOR),
        P((ITEM, SEQ), TENSOR),
        P((ITEM, SEQ), TENSOR),
        P(TENSOR),
        P(TENSOR, (ITEM, SEQ)),
        P(),
        P(),
        P(),
        P((ITEM, SEQ), TENSOR),
        P(TENSOR),
        P(TENSOR, (ITEM, SEQ)),
        P(),
        P(),
        P(),
    )

    def layer(*arrays):
        chosen = column_body if column_plan_fits(mesh, arrays) else general_body
        return jax.shard_map(
            chosen,
            mesh=mesh,
            in_specs=placed,
            out_specs=reduced,
            check_vma=False,
        )(*arrays)

    return layer
```

```python
import functools

import jax
import jax.numpy as jnp
from jax import lax
from jax.experimental import pallas as pl
from jax.experimental.pallas import tpu as pltpu
from jax.sharding import PartitionSpec as P

EPS = 1e-05
SCALE = 0.125
NEG = -1e30
MESH = pl.DeviceIdType.MESH
ITEM, SEQ, TENSOR = "item", "seq", "tensor"


def matmul(first_op, second_op):
    return jnp.dot(first_op, second_op, preferred_element_type=jnp.float32)


def layer_norm(rows_in, norm_gain, norm_shift):
    center = rows_in - jnp.mean(rows_in, axis=-1, keepdims=True)
    spread = jnp.mean(center * center, axis=-1, keepdims=True)
    return center * lax.rsqrt(spread + EPS) * norm_gain + norm_shift


def exact_gelu(values_in):
    return jax.nn.gelu(values_in, approximate=False)


def tensor_total(partial_rows):
    return lax.psum(partial_rows, TENSOR)


def row_total(values_in):
    return jnp.sum(values_in.astype(jnp.float32), axis=(0, 1))


def softmax_stats(scores):
    row_max = jnp.max(scores, axis=-1, keepdims=True)
    shifted = jnp.exp(scores - row_max)
    row_sum = jnp.sum(shifted, axis=-1, keepdims=True)
    return (shifted / row_sum, row_max + jnp.log(row_sum))


def owned_pick(encoder_states, kv_weights, kv_bias, flat_index, owned_mask):
    kv_table = (
        jnp.einsum("ind,dhf->inhf", encoder_states, kv_weights, preferred_element_type=jnp.float32)
        + kv_bias
    ).astype(jnp.bfloat16)
    flat_table = kv_table.reshape(-1, kv_table.shape[-1])
    picked = jnp.take(flat_table, flat_index, axis=0)
    return jnp.where(owned_mask, picked.astype(jnp.float32), 0.0)


def general_body(
    dec_input,
    encoder_states,
    retrieved,
    self_wq,
    self_bq,
    self_wk,
    self_wv,
    self_bv,
    self_wo,
    self_bo,
    norm1_gain,
    norm1_bias,
    cross_wq,
    cross_bq,
    cross_wk,
    cross_wv,
    cross_bv,
    cross_wo,
    cross_bo,
    norm2_gain,
    norm2_bias,
    ffn_w1,
    ffn_b1,
    ffn_w2,
    ffn_b2,
    norm3_gain,
    norm3_bias,
    out_grad,
):
    item_count, dec_rows, model_width = dec_input.shape
    local_heads = retrieved.shape[1]
    enc_rows = encoder_states.shape[1]
    head_cols = self_wq.shape[1]
    head_size = head_cols // local_heads
    seq_devices = lax.axis_size(SEQ)
    seq_rank = lax.axis_index(SEQ)
    seq_length = dec_rows * seq_devices
    queries = ((matmul(dec_input, self_wq) + self_bq) * SCALE).astype(jnp.bfloat16)
    keys_local = matmul(dec_input, self_wk).astype(jnp.bfloat16)
    values_local = (matmul(dec_input, self_wv) + self_bv).astype(jnp.bfloat16)
    kv_all = lax.all_gather(
        jnp.concatenate([keys_local, values_local], axis=-1), SEQ, axis=1, tiled=True
    )
    keys_all = kv_all[..., :head_cols].reshape(item_count, seq_length, local_heads, head_size)
    values_all = kv_all[..., head_cols:].reshape(item_count, seq_length, local_heads, head_size)
    query_heads = queries.reshape(item_count, dec_rows, local_heads, head_size)
    query_pos = seq_rank * dec_rows + jnp.arange(dec_rows)
    causal = query_pos[:, None] >= jnp.arange(seq_length)[None, :]

    def self_scores():
        raw_scores = jnp.einsum(
            "irhe,ilhe->ihrl", query_heads, keys_all, preferred_element_type=jnp.float32
        )
        return jnp.where(causal, raw_scores, NEG)

    prob_self, lse_self = softmax_stats(self_scores())
    attended = (
        jnp.einsum(
            "ihrl,ilhe->irhe",
            prob_self.astype(jnp.bfloat16),
            values_all,
            preferred_element_type=jnp.float32,
        )
        .astype(jnp.bfloat16)
        .reshape(item_count, dec_rows, head_cols)
    )
    branch_one = tensor_total(matmul(attended, self_wo)) + self_bo
    hidden_one = dec_input.astype(jnp.float32) + branch_one
    normed_one = layer_norm(hidden_one, norm1_gain, norm1_bias).astype(jnp.bfloat16)
    queries_x = (
        ((matmul(normed_one, cross_wq) + cross_bq) * SCALE)
        .astype(jnp.bfloat16)
        .reshape(item_count, dec_rows, local_heads, head_size)
    )
    kv_weights = jnp.concatenate(
        [
            cross_wk.reshape(model_width, local_heads, head_size),
            cross_wv.reshape(model_width, local_heads, head_size),
        ],
        axis=-1,
    )
    kv_bias = jnp.concatenate(
        [
            jnp.zeros((local_heads, head_size), jnp.float32),
            cross_bv.reshape(local_heads, head_size),
        ],
        axis=-1,
    )
    local_row = retrieved - seq_rank * enc_rows
    owned_mask = ((local_row >= 0) & (local_row < enc_rows))[..., None]
    flat_index = (
        jnp.arange(item_count, dtype=jnp.int32)[:, None, None] * enc_rows
        + jnp.clip(local_row, 0, enc_rows - 1)
    ) * local_heads + jnp.arange(local_heads, dtype=jnp.int32)[None, :, None]
    retrieved_kv = lax.psum(
        owned_pick(encoder_states, kv_weights, kv_bias, flat_index, owned_mask).astype(
            jnp.bfloat16
        ),
        SEQ,
    )

    def cross_scores(kv_pair):
        return jnp.einsum(
            "irhe,ihke->ihrk",
            queries_x,
            kv_pair[..., :head_size],
            preferred_element_type=jnp.float32,
        )

    prob_cross, lse_cross = softmax_stats(cross_scores(retrieved_kv))
    attended_x = (
        jnp.einsum(
            "ihrk,ihke->irhe",
            prob_cross.astype(jnp.bfloat16),
            retrieved_kv[..., head_size:],
            preferred_element_type=jnp.float32,
        )
        .astype(jnp.bfloat16)
        .reshape(item_count, dec_rows, head_cols)
    )
    branch_two = tensor_total(matmul(attended_x, cross_wo)) + cross_bo
    hidden_two = normed_one.astype(jnp.float32) + branch_two
    normed_two = layer_norm(hidden_two, norm2_gain, norm2_bias).astype(jnp.bfloat16)
    pre_act = matmul(normed_two, ffn_w1) + ffn_b1
    activated = exact_gelu(pre_act).astype(jnp.bfloat16)
    branch_three = tensor_total(matmul(activated, ffn_w2)) + ffn_b2
    hidden_three = normed_two.astype(jnp.float32) + branch_three
    layer_out = layer_norm(hidden_three, norm3_gain, norm3_bias)
    _, back_three = jax.vjp(layer_norm, hidden_three, norm3_gain, norm3_bias)
    d_hidden3, gnorm3_gain, gnorm3_bias = back_three(out_grad.astype(jnp.float32))
    d_branch3 = d_hidden3.astype(jnp.bfloat16)
    gffn_b2 = row_total(d_branch3)
    gffn_w2 = jnp.einsum("irf,ird->fd", activated, d_branch3, preferred_element_type=jnp.float32)
    d_activated = jnp.einsum("ird,fd->irf", d_branch3, ffn_w2, preferred_element_type=jnp.float32)
    _, gelu_back = jax.vjp(exact_gelu, pre_act)
    d_pre = gelu_back(d_activated)[0].astype(jnp.bfloat16)
    gffn_b1 = row_total(d_pre)
    gffn_w1 = jnp.einsum("ird,irf->df", normed_two, d_pre, preferred_element_type=jnp.float32)
    d_normed2 = d_hidden3 + tensor_total(
        jnp.einsum("irf,df->ird", d_pre, ffn_w1, preferred_element_type=jnp.float32)
    )
    _, back_two = jax.vjp(layer_norm, hidden_two, norm2_gain, norm2_bias)
    d_hidden2, gnorm2_gain, gnorm2_bias = back_two(d_normed2)
    d_branch2 = d_hidden2.astype(jnp.bfloat16)
    gcross_bo = row_total(d_branch2)
    gcross_wo = jnp.einsum("irc,ird->cd", attended_x, d_branch2, preferred_element_type=jnp.float32)
    d_attended2 = (
        jnp.einsum("ird,cd->irc", d_branch2, cross_wo, preferred_element_type=jnp.float32)
        .astype(jnp.bfloat16)
        .reshape(item_count, dec_rows, local_heads, head_size)
    )
    kv_back = lax.psum(
        owned_pick(encoder_states, kv_weights, kv_bias, flat_index, owned_mask).astype(
            jnp.bfloat16
        ),
        SEQ,
    )
    redo_cross = jnp.exp(cross_scores(kv_back) - lse_cross)
    dprob_cross = jnp.einsum(
        "irhe,ihke->ihrk", d_attended2, kv_back[..., head_size:], preferred_element_type=jnp.float32
    )
    d_scores2 = (
        redo_cross * (dprob_cross - jnp.sum(dprob_cross * redo_cross, axis=-1, keepdims=True))
    ).astype(jnp.bfloat16)
    d_query2 = (
        jnp.einsum(
            "ihrk,ihke->irhe",
            d_scores2,
            kv_back[..., :head_size],
            preferred_element_type=jnp.float32,
        )
        .astype(jnp.bfloat16)
        .reshape(item_count, dec_rows, head_cols)
    )
    kv_grad_part = jnp.concatenate(
        [
            jnp.einsum("ihrk,irhe->ihke", d_scores2, queries_x, preferred_element_type=jnp.float32),
            jnp.einsum(
                "ihrk,irhe->ihke",
                redo_cross.astype(jnp.bfloat16),
                d_attended2,
                preferred_element_type=jnp.float32,
            ),
        ],
        axis=-1,
    )
    kv_grad = lax.psum(kv_grad_part, SEQ).astype(jnp.bfloat16)
    kv_owned = jnp.where(owned_mask, kv_grad.astype(jnp.float32), 0.0)
    table_grad = (
        jnp.zeros((item_count * enc_rows * local_heads, 2 * head_size), jnp.float32)
        .at[flat_index.reshape(-1)]
        .add(kv_owned.reshape(-1, 2 * head_size))
    )
    table_low = table_grad.astype(jnp.bfloat16).reshape(
        item_count, enc_rows, local_heads, 2 * head_size
    )
    grad_kv_weights = jnp.einsum(
        "ind,inhf->dhf", encoder_states, table_low, preferred_element_type=jnp.float32
    )
    gcross_wk = grad_kv_weights[..., :head_size].reshape(model_width, head_cols)
    gcross_wv = grad_kv_weights[..., head_size:].reshape(model_width, head_cols)
    gcross_bv = row_total(table_low[..., head_size:]).reshape(head_cols)
    encoder_part = jnp.einsum(
        "inhf,dhf->ind", table_low, kv_weights, preferred_element_type=jnp.float32
    )
    encoder_grad = lax.psum_scatter(encoder_part, TENSOR, scatter_dimension=2, tiled=True).astype(
        jnp.bfloat16
    )
    gcross_bq = row_total(d_query2) * SCALE
    gcross_wq = (
        jnp.einsum("ird,irc->dc", normed_one, d_query2, preferred_element_type=jnp.float32) * SCALE
    )
    d_normed1 = d_hidden2 + tensor_total(
        jnp.einsum("irc,dc->ird", d_query2, cross_wq, preferred_element_type=jnp.float32) * SCALE
    )
    _, back_one = jax.vjp(layer_norm, hidden_one, norm1_gain, norm1_bias)
    d_hidden1, gnorm1_gain, gnorm1_bias = back_one(d_normed1)
    d_branch1 = d_hidden1.astype(jnp.bfloat16)
    gself_bo = row_total(d_branch1)
    gself_wo = jnp.einsum("irc,ird->cd", attended, d_branch1, preferred_element_type=jnp.float32)
    d_attended1 = (
        jnp.einsum("ird,cd->irc", d_branch1, self_wo, preferred_element_type=jnp.float32)
        .astype(jnp.bfloat16)
        .reshape(item_count, dec_rows, local_heads, head_size)
    )
    redo_self = jnp.exp(self_scores() - lse_self)
    dprob_self = jnp.einsum(
        "irhe,ilhe->ihrl", d_attended1, values_all, preferred_element_type=jnp.float32
    )
    d_scores1 = (
        redo_self * (dprob_self - jnp.sum(dprob_self * redo_self, axis=-1, keepdims=True))
    ).astype(jnp.bfloat16)
    probs_low = redo_self.astype(jnp.bfloat16)
    d_query1 = (
        jnp.einsum("ihrl,ilhe->irhe", d_scores1, keys_all, preferred_element_type=jnp.float32)
        .astype(jnp.bfloat16)
        .reshape(item_count, dec_rows, head_cols)
    )
    row_count = dec_rows * lax.axis_size(SEQ)
    key_grad = jnp.einsum(
        "ihrl,irhe->lihe", d_scores1, query_heads, preferred_element_type=jnp.float32
    ).reshape(row_count, item_count, head_cols)
    value_grad = jnp.einsum(
        "ihrl,irhe->lihe", probs_low, d_attended1, preferred_element_type=jnp.float32
    ).reshape(row_count, item_count, head_cols)
    kv_self = lax.psum_scatter(
        jnp.concatenate([key_grad, value_grad], axis=-1), SEQ, scatter_dimension=0, tiled=True
    ).astype(jnp.bfloat16)
    kv_self = jnp.swapaxes(kv_self, 0, 1)
    d_key1 = kv_self[..., :head_cols]
    d_value1 = kv_self[..., head_cols:]
    gself_bq = row_total(d_query1) * SCALE
    gself_wq = (
        jnp.einsum("ird,irc->dc", dec_input, d_query1, preferred_element_type=jnp.float32) * SCALE
    )
    gself_wk = jnp.einsum("ird,irc->dc", dec_input, d_key1, preferred_element_type=jnp.float32)
    gself_wv = jnp.einsum("ird,irc->dc", dec_input, d_value1, preferred_element_type=jnp.float32)
    gself_bv = row_total(d_value1)
    input_part = (
        jnp.einsum("irc,dc->ird", d_query1, self_wq, preferred_element_type=jnp.float32) * SCALE
        + jnp.einsum("irc,dc->ird", d_key1, self_wk, preferred_element_type=jnp.float32)
        + jnp.einsum("irc,dc->ird", d_value1, self_wv, preferred_element_type=jnp.float32)
    )
    input_grad = (d_hidden1 + tensor_total(input_part)).astype(jnp.bfloat16)
    matrices = (
        lax.psum_scatter(gself_wq, (ITEM, SEQ), scatter_dimension=0, tiled=True),
        lax.psum_scatter(gself_wk, (ITEM, SEQ), scatter_dimension=0, tiled=True),
        lax.psum_scatter(gself_wv, (ITEM, SEQ), scatter_dimension=0, tiled=True),
        lax.psum_scatter(gself_wo, (ITEM, SEQ), scatter_dimension=1, tiled=True),
        lax.psum_scatter(gcross_wq, (ITEM, SEQ), scatter_dimension=0, tiled=True),
        lax.psum_scatter(gcross_wk, (ITEM, SEQ), scatter_dimension=0, tiled=True),
        lax.psum_scatter(gcross_wv, (ITEM, SEQ), scatter_dimension=0, tiled=True),
        lax.psum_scatter(gcross_wo, (ITEM, SEQ), scatter_dimension=1, tiled=True),
        lax.psum_scatter(gffn_w1, (ITEM, SEQ), scatter_dimension=0, tiled=True),
        lax.psum_scatter(gffn_w2, (ITEM, SEQ), scatter_dimension=1, tiled=True),
    )
    vectors = lax.psum(
        (
            gself_bq,
            gself_bv,
            gself_bo,
            gnorm1_gain,
            gnorm1_bias,
            gcross_bq,
            gcross_bv,
            gcross_bo,
            gnorm2_gain,
            gnorm2_bias,
            gffn_b1,
            gffn_b2,
            gnorm3_gain,
            gnorm3_bias,
        ),
        (ITEM, SEQ),
    )
    return (
        layer_out.astype(jnp.bfloat16),
        input_grad,
        encoder_grad,
        matrices[0],
        vectors[0],
        matrices[1],
        matrices[2],
        vectors[1],
        matrices[3],
        vectors[2],
        vectors[3],
        vectors[4],
        matrices[4],
        vectors[5],
        matrices[5],
        matrices[6],
        vectors[6],
        matrices[7],
        vectors[7],
        vectors[8],
        vectors[9],
        matrices[8],
        vectors[10],
        matrices[9],
        vectors[11],
        vectors[12],
        vectors[13],
    )


VMEM_LIMIT = 58 * 1024 * 1024
FULL = 256
HALF = 128
WIDE = FULL + HALF


def column_plan_fits(mesh, arrays):
    items, cores = arrays[0].shape[0], mesh.shape[ITEM]
    ranks, depth = mesh.shape[TENSOR], mesh.shape[SEQ]
    heads = arrays[2].shape[1]
    rows = arrays[0].shape[1] // depth
    width = arrays[0].shape[2]
    return (
        cores == 2
        and ranks == 4
        and items == ranks
        and ranks == depth
        and heads == 3 * depth
        and width == 64 * heads
        and rows == cores * FULL
        and arrays[2].shape[2] % FULL == 0
    )


def here():
    return lax.axis_index(ITEM), lax.axis_index(SEQ), lax.axis_index(TENSOR)


def call_kernel(kernel, name, outs, args, scratch=(), collective_id=None, in_spaces=None, out_space=None, us=10):
    single = isinstance(outs, tuple)
    listed = [outs] if single else list(outs)
    out_spaces = [pltpu.VMEM] * len(listed) if out_space is None else out_space
    spaces = [pltpu.VMEM] * len(args) if in_spaces is None else in_spaces
    params = dict(vmem_limit_bytes=VMEM_LIMIT)
    if collective_id is not None:
        params.update(collective_id=collective_id, has_side_effects=True)
    out = pl.pallas_call(
        kernel,
        out_shape=[jax.ShapeDtypeStruct(s, d) for s, d in listed],
        in_specs=[pl.BlockSpec(memory_space=s) for s in spaces],
        out_specs=[pl.BlockSpec(memory_space=s) for s in out_spaces],
        scratch_shapes=list(scratch),
        compiler_params=pltpu.CompilerParams(**params),
        cost_estimate=pl.CostEstimate(flops=us * 10**9, bytes_accessed=us * 3 * 10**6, transcendentals=0),
        name=name,
    )(*args)
    return out[0] if single else out


def greet(peers):
    gate = pltpu.get_barrier_semaphore()
    for peer in peers:
        pl.semaphore_signal(gate, inc=1, device_id=peer, device_id_type=MESH)


def meet(peers):
    greet(peers)
    pl.semaphore_wait(pltpu.get_barrier_semaphore(), len(peers))


def column_peer(place, cores, rank):
    return (lax.rem(place, cores), place // cores, rank)


def remote_copy(src, dst, send, recv, device):
    return pltpu.make_async_remote_copy(
        src_ref=src, dst_ref=dst, send_sem=send, recv_sem=recv, device_id=device, device_id_type=MESH
    )


def plane_peers(cores, ranks):
    core, seq, rank = here()
    peers = []
    for step in range(1, cores * ranks):
        place = lax.rem(rank * cores + core + step, cores * ranks)
        peers.append((lax.rem(place, cores), seq, place // cores))
    return peers


class Deal:
    def __init__(self, cores, ranks, per_core, source, all_ref, send_sem, recv_sem, own_sem):
        self.cores, self.ranks, self.per_core = cores, ranks, per_core
        self.source, self.all_ref = source, all_ref
        self.send_sem, self.recv_sem, self.own_sem = send_sem, recv_sem, own_sem
        self.core, self.seq, self.rank = here()
        self.home = self.rank // per_core
        self.local = lax.rem(self.rank, per_core)

    def send(self, step):
        target = lax.rem(self.rank + step, self.ranks)
        return remote_copy(
            self.source(target),
            self.all_ref.at[self.local, self.core],
            self.send_sem.at[step],
            self.recv_sem.at[self.local, self.core],
            (self.home, self.seq, target),
        )

    def keep(self):
        return pltpu.make_async_copy(self.source(self.rank), self.all_ref.at[self.local, self.core], self.own_sem)

    def start(self):
        for step in range(1, self.ranks):
            self.send(step).start()

        @pl.when(self.core != self.home)
        def _():
            self.send(0).start()

        @pl.when(self.core == self.home)
        def _():
            self.keep().start()

    def finish(self):
        for item in range(self.per_core):
            for half in range(self.cores):
                inside = (half == self.core) & (self.core * self.per_core + item == self.rank)

                @pl.when(jnp.logical_not(inside))
                def _():
                    remote_copy(
                        self.source(0),
                        self.all_ref.at[item, half],
                        self.send_sem.at[0],
                        self.recv_sem.at[item, half],
                        (1 - self.core, self.seq, self.rank),
                    ).wait_recv()

        for step in range(1, self.ranks):
            self.send(step).wait_send()

        @pl.when(self.core != self.home)
        def _():
            self.send(0).wait_send()

        @pl.when(self.core == self.home)
        def _():
            self.keep().wait()


def deal_scratch(cores, ranks, per_core):
    dma = pltpu.SemaphoreType.DMA
    return [dma((ranks,)), dma((per_core, cores)), dma]


class PlaneGather:
    def __init__(self, all_ref, give_send, give_recv, far_send, far_recv, pass_send, pass_recv):
        self.all_ref = all_ref
        self.give_send, self.give_recv = give_send, give_recv
        self.far_send, self.far_recv = far_send, far_recv
        self.pass_send, self.pass_recv = pass_send, pass_recv
        self.core, self.seq, self.rank = here()
        low, high = lax.rem(self.rank, 2), self.rank // 2
        self.near = (2 * high + 1 - low, 2 * (1 - high) + low)
        self.far = 2 * (1 - high) + 1 - low
        self.half = all_ref.shape[2] // 2
        self.peers = [(self.core, self.seq, rank) for rank in self.near]

    def give(self, way):
        block = self.all_ref.at[self.core, self.rank]
        return remote_copy(block, block, self.give_send.at[way], self.give_recv.at[way], self.peers[way])

    def far_part(self, way, origin):
        return self.all_ref.at[self.core, origin, pl.ds(way * self.half, self.half), :]

    def onward(self, way):
        block = self.far_part(way, self.near[way])
        return remote_copy(
            block, block, self.far_send.at[way], self.far_recv.at[way], self.peers[1 - way]
        )

    def side(self, slot, block):
        return remote_copy(
            block, block, self.pass_send.at[slot], self.pass_recv.at[slot], (1 - self.core, self.seq, self.rank)
        )

    def sides(self):
        near = [self.side(way, self.all_ref.at[self.core, self.near[way]]) for way in range(2)]
        return near + [self.side(2 + way, self.far_part(way, self.far)) for way in range(2)]

    def start(self):
        for way in range(2):
            self.give(way).start()

    def forward(self):
        sides = self.sides()
        for way in range(2):
            self.give(way).wait_recv()
            self.onward(way).start()
            sides[way].start()

    def arrive(self):
        sides = self.sides()
        for way in range(2):
            self.onward(way).wait_recv()
            sides[2 + way].start()
        for side in sides:
            side.wait_recv()

    def finish(self):
        for way in range(2):
            self.give(way).wait_send()
            self.onward(way).wait_send()
        for side in self.sides():
            side.wait_send()


def own_weights(refs, all_ref, sem):
    cores, _, _, lanes = all_ref.shape
    rank = lax.axis_index(TENSOR)
    copies, first = [], 0
    for n, ref in enumerate(refs):
        rows = ref.shape[0]
        for half in range(cores):
            copies.append(
                pltpu.make_async_copy(
                    ref.at[:, pl.ds(half * lanes, lanes)],
                    all_ref.at[half, rank, pl.ds(first, rows), :],
                    sem.at[n, half],
                )
            )
        first += rows
    return copies


def gather_scratch():
    return [pltpu.SemaphoreType.DMA((n,)) for n in (2, 2, 2, 2, 4, 4)]


class PlaneReduce:
    def __init__(self, ranks, grad_ref, got_ref, sum_ref, all_ref, swap_sem, send_sem, recv_sem):
        self.ranks, self.grad_ref, self.got_ref = ranks, grad_ref, got_ref
        self.sum_ref, self.all_ref = sum_ref, all_ref
        self.swap_sem, self.send_sem, self.recv_sem = swap_sem, send_sem, recv_sem
        self.core, self.seq, self.rank = here()
        self.peers = [(self.core, self.seq, lax.rem(self.rank + step, ranks)) for step in range(1, ranks)]

    def swap(self):
        return remote_copy(
            self.grad_ref.at[1 - self.core],
            self.got_ref,
            self.swap_sem.at[0],
            self.swap_sem.at[1],
            (1 - self.core, self.seq, self.rank),
        )

    def copy(self, step):
        peer = self.peers[step]
        return remote_copy(
            self.sum_ref.at[peer[2]], self.all_ref.at[self.rank], self.send_sem.at[step], self.recv_sem.at[step], peer
        )

    def start(self):
        self.swap().start()

    def middle(self):
        self.swap().wait()
        for rank in range(self.ranks):
            self.sum_ref[rank] = (
                self.grad_ref[self.core, rank].astype(jnp.float32) + self.got_ref[rank].astype(jnp.float32)
            ).astype(self.sum_ref.dtype)
        for step in range(self.ranks - 1):
            self.copy(step).start()

    def finish(self):
        for step in range(self.ranks - 1):
            self.copy(step).wait()
        total = self.sum_ref[self.rank].astype(jnp.float32)
        for step in range(1, self.ranks):
            total = total + self.all_ref[lax.rem(self.rank + step, self.ranks)].astype(jnp.float32)
        return total


class PlaneSum:
    def __init__(self, ranks, src_ref, first, all_ref, own_sem, send_sem, recv_sem):
        self.ranks, self.src_ref, self.first = ranks, src_ref, first
        self.all_ref, self.own_sem, self.send_sem, self.recv_sem = all_ref, own_sem, send_sem, recv_sem
        self.core, self.seq, self.rank = here()
        self.peers = [(self.core, self.seq, lax.rem(self.rank + step, ranks)) for step in range(1, ranks)]

    def block(self, rank):
        return self.src_ref.at[rank, :, pl.ds(self.first, self.all_ref.shape[2])]

    def own(self):
        return pltpu.make_async_copy(self.block(self.rank), self.all_ref.at[self.rank], self.own_sem)

    def copy(self, step):
        peer = self.peers[step]
        return remote_copy(
            self.block(peer[2]), self.all_ref.at[self.rank], self.send_sem.at[step], self.recv_sem.at[step], peer
        )

    def start(self):
        self.own().start()
        for step in range(self.ranks - 1):
            self.copy(step).start()

    def finish(self):
        self.own().wait()
        for step in range(self.ranks - 1):
            self.copy(step).wait()
        total = self.all_ref[0].astype(jnp.float32)
        for origin in range(1, self.ranks):
            total = total + self.all_ref[origin].astype(jnp.float32)
        return total


def sum_scratch(ranks, rows, columns, dtype):
    dma = pltpu.SemaphoreType.DMA
    return [pltpu.VMEM((ranks, rows, columns), dtype), dma, dma((ranks - 1,)), dma((ranks - 1,))]


def reduce_scratch(ranks, rows, columns, dtype):
    dma = pltpu.SemaphoreType.DMA
    block = pltpu.VMEM((ranks, rows, columns), dtype)
    return [block, block, block, dma((2,)), dma((ranks - 1,)), dma((ranks - 1,))]


def column_places(cores, depth):
    core, seq, _ = here()
    mine = seq * cores + core
    return mine, [lax.rem(mine + step, cores * depth) for step in range(1, cores * depth)]


class ColumnSend:
    def __init__(self, cores, depth, source_ref, all_ref, send_sem, recv_sem):
        self.cores, self.count = cores, cores * depth
        self.source_ref, self.all_ref = source_ref, all_ref
        self.send_sem, self.recv_sem = send_sem, recv_sem
        core, seq, self.rank = here()
        self.mine = seq * cores + core

    def copy(self, step):
        place = lax.rem(self.mine + 1 + step, self.count)
        return remote_copy(
            self.source_ref.at[place],
            self.all_ref.at[self.mine],
            self.send_sem.at[step],
            self.recv_sem.at[step],
            column_peer(place, self.cores, self.rank),
        )

    def wait_from(self, step):
        self.copy(step).wait_recv()

    def finish_sends(self):
        for step in range(self.count - 1):
            self.copy(step).wait_send()

    def finish(self):
        for step in range(self.count - 1):
            self.copy(step).wait()


def send_scratch(count):
    return [pltpu.SemaphoreType.DMA((count - 1,)), pltpu.SemaphoreType.DMA((count - 1,))]


class Chain:
    def __init__(self, depth, all_ref, send_sem, recv_sem):
        self.depth, self.all_ref = depth, all_ref
        self.send_sem, self.recv_sem = send_sem, recv_sem
        core, self.seq, rank = here()
        self.above = (core, lax.rem(self.seq + 1, depth), rank)
        self.below = (core, lax.rem(self.seq + depth - 1, depth), rank)

    def copy(self, block, way):
        part = self.all_ref.at[block]
        target = self.above if way == 0 else self.below
        return remote_copy(part, part, self.send_sem.at[way, block], self.recv_sem.at[block], target)

    def step(self, n):
        up, down = self.seq - n, self.seq + n

        @pl.when(up >= 0)
        def _():
            if n > 0:
                self.copy(up, 0).wait_recv()

            @pl.when(self.seq + 1 < self.depth)
            def _():
                self.copy(up, 0).start()

        @pl.when(down < self.depth)
        def _():
            if n > 0:
                self.copy(down, 1).wait_recv()

            @pl.when(self.seq > 0)
            def _():
                self.copy(down, 1).start()

    def finish(self):
        for n in range(self.depth):
            up, down = self.seq - n, self.seq + n

            @pl.when((up >= 0) & (self.seq + 1 < self.depth))
            def _():
                self.copy(up, 0).wait_send()

            @pl.when((down < self.depth) & (self.seq > 0))
            def _():
                self.copy(down, 1).wait_send()


class VectorSum:
    def __init__(self, cores, depth, ranks, out_ref, src_ref, col_ref, sum_ref, plane_ref, a_send, a_recv, b_send, b_recv, c_send, c_recv):
        self.cores, self.depth, self.ranks = cores, depth, ranks
        self.out_ref, self.src_ref, self.col_ref = out_ref, src_ref, col_ref
        self.sum_ref, self.plane_ref = sum_ref, plane_ref
        self.sems = ((a_send, a_recv), (b_send, b_recv), (c_send, c_recv))
        core, seq, self.rank = here()
        self.mine, self.places = column_places(cores, depth)
        self.peers = [(core, seq, lax.rem(self.rank + step, ranks)) for step in range(1, ranks)]

    def copies(self, stage):
        send, recv = self.sems[stage]
        if stage == 1:
            return [
                remote_copy(self.sum_ref, self.plane_ref.at[self.rank], send.at[n], recv.at[n], peer)
                for n, peer in enumerate(self.peers)
            ]
        src = self.src_ref if stage == 0 else self.out_ref
        dst = self.col_ref if stage == 0 else self.out_ref
        return [
            remote_copy(
                src.at[place if stage == 0 else self.mine],
                dst.at[self.mine],
                send.at[n],
                recv.at[n],
                column_peer(place, self.cores, self.rank),
            )
            for n, place in enumerate(self.places)
        ]

    def start(self, rows):
        height = self.src_ref.shape[1]
        for n, row in enumerate(rows):
            self.src_ref[n // height, n % height : n % height + 1, :] = row
        for copy in self.copies(0):
            copy.start()

    def second(self):
        for copy in self.copies(0):
            copy.wait()
        total = self.src_ref[self.mine]
        for place in self.places:
            total = total + self.col_ref[place]
        self.sum_ref[...] = total
        for copy in self.copies(1):
            copy.start()

    def third(self):
        for copy in self.copies(1):
            copy.wait()
        self.plane_ref[self.rank] = self.sum_ref[...]
        total = self.plane_ref[0]
        for origin in range(1, self.ranks):
            total = total + self.plane_ref[origin]
        self.out_ref[self.mine] = total
        for copy in self.copies(2):
            copy.start()

    def finish(self):
        for copy in self.copies(2):
            copy.wait()


def vector_scratch(shape, places, ranks):
    full = jnp.float32
    return [
        pltpu.VMEM(shape, full),
        pltpu.VMEM(shape, full),
        pltpu.VMEM(shape[1:], full),
        pltpu.VMEM((ranks,) + shape[1:], full),
    ] + [pltpu.SemaphoreType.DMA((n - 1,)) for n in (places, places, ranks, ranks, places, places)]


def front_kernel(
    sizes,
    x_ref, g_ref, m_ref, idx_ref, vec_ref, ck_ref, cv_ref, wq_ref, wk_ref, wv_ref, wo1_ref, wq2_ref, wo2_ref, w1_ref, w2_ref,
    bo_ref, gain_ref, shift_ref,
    xout_ref, eout_ref, wkvout_ref, wsout_ref, sqout_ref, w1out_ref, w2out_ref,
    gmine_ref, iall_ref, vall_ref, q_ref, k_ref, kt_ref, v_ref, o_ref, lse_ref, oall_ref,
    h_ref, y_ref, q2_ref, k2_ref, k2t_ref, v2_ref, o2_ref, lse2_ref, o2all_ref,
    xall_ref, enc_ref, wkv_ref, ws_ref, sq_ref, w1all_ref, w2all_ref, piece_ref, got_ref, vt_ref, s_ref,
    qsrc_ref, half_ref, other_ref, v2t_ref,
    load_kv, load_s, load_sq, load_w1, load_w2,
    swap_send, swap_recv, chain_send, chain_recv, side_send, side_recv, own_sem,
    idx_send, idx_recv, vec_send, vec_recv, kvsend, kvrecv, osend, orecv, out_sem,
    half_sem, qsend, qrecv, o2send, o2recv, *wsems
):
    cores, depth, ranks, per_core = sizes
    low = jnp.bfloat16
    core, seq, rank = here()
    home = rank // per_core
    local = lax.rem(rank, per_core)
    blocks = cores * depth
    head = q_ref.shape[1]
    sibling = (1 - core, seq, rank)
    above = (core, lax.rem(seq + 1, depth), rank)
    below = (core, lax.rem(seq + depth - 1, depth), rank)
    mine, places = column_places(cores, depth)
    gathers = [PlaneGather(ref, *wsems[6 * n : 6 * n + 6]) for n, ref in enumerate((wkv_ref, ws_ref, sq_ref, w1all_ref, w2all_ref))]
    gather_kv, gather_s, gather_sq, gather_w1, gather_w2 = gathers
    loads = [
        own_weights((ck_ref, cv_ref), wkv_ref, load_kv),
        own_weights((wq_ref, wk_ref, wv_ref), ws_ref, load_s),
        own_weights((wo1_ref, wq2_ref, wo2_ref), sq_ref, load_sq),
        own_weights((w1_ref,), w1all_ref, load_w1),
        own_weights((w2_ref,), w2all_ref, load_w2),
    ]
    for group in loads:
        for copy in group:
            copy.start()
    plane = plane_peers(cores, ranks)
    peers = plane + [column_peer(place, cores, rank) for place in places]
    meet(peers)

    def remote(src, dst, send, recv, device):
        return remote_copy(src, dst, send, recv, device)

    there = pl.ds((1 - core) * FULL, FULL)
    half_rows = pl.ds(core * FULL, FULL)
    swap_x = remote(x_ref.at[local, there], xall_ref.at[seq, 1 - core], swap_send.at[0], swap_recv.at[0], sibling)
    swap_g = remote(g_ref.at[local, there], gmine_ref, swap_send.at[1], swap_recv.at[1], sibling)
    swap_e = remote(m_ref.at[local], enc_ref, swap_send.at[2], swap_recv.at[2], sibling)
    own_x = pltpu.make_async_copy(x_ref.at[local, half_rows], xall_ref.at[seq, core], own_sem.at[3])
    own_g = pltpu.make_async_copy(g_ref.at[local, half_rows], gmine_ref, own_sem.at[4])
    own_e = pltpu.make_async_copy(m_ref.at[local], enc_ref, own_sem.at[5])

    @pl.when(core == home)
    def _():
        swap_x.start()
        own_x.start()

    for copy in loads[0]:
        copy.wait()
    gather_kv.start()

    def chain(block, target, way):
        part = xall_ref.at[block, core]
        return remote(part, part, chain_send.at[way, block], chain_recv.at[block], target)

    def aside(block):
        part = xall_ref.at[block, core]
        return remote(part, part, side_send.at[block], side_recv.at[block], sibling)

    def chain_step(step):
        up, down = seq - step, seq + step

        @pl.when(up >= 0)
        def _():
            if step > 0:
                chain(up, above, 0).wait_recv()

            @pl.when(seq + 1 < depth)
            def _():
                chain(up, above, 0).start()

            aside(up).start()

        @pl.when(down < depth)
        def _():
            if step > 0:
                chain(down, below, 1).wait_recv()

            @pl.when(seq > 0)
            def _():
                chain(down, below, 1).start()

            if step > 0:
                aside(down).start()

    @pl.when(core == home)
    def _():
        own_x.wait()

    @pl.when(core != home)
    def _():
        swap_x.wait_recv()

    chain_step(0)

    @pl.when(core == home)
    def _():
        swap_e.start()
        own_e.start()
        swap_g.start()
        own_g.start()

    def give_index(item, half):
        return remote(
            idx_ref.at[item], iall_ref.at[rank], idx_send.at[item, half], idx_recv.at[rank],
            (half, seq, core * per_core + item),
        )

    def is_me(item, half):
        return (half == core) & (core * per_core + item == rank)

    for item in range(per_core):
        for half in range(cores):

            @pl.when(jnp.logical_not(is_me(item, half)))
            def _():
                give_index(item, half).start()

            @pl.when(is_me(item, half))
            def _():
                own = pltpu.make_async_copy(idx_ref.at[item], iall_ref.at[rank], own_sem.at[0])
                own.start()
                own.wait()

    across = [(core, seq, lax.rem(rank + step, ranks)) for step in range(1, ranks)]
    vecs = [
        remote(vec_ref, vall_ref.at[rank], vec_send.at[step], vec_recv.at[step], peer)
        for step, peer in enumerate(across)
    ]
    for copy in vecs:
        copy.start()
    own_vec = pltpu.make_async_copy(vec_ref, vall_ref.at[rank], own_sem.at[1])
    own_vec.start()

    gather_kv.forward()
    for copy in loads[1]:
        copy.wait()
    gather_s.start()
    chain_step(1)
    for copy in vecs:
        copy.wait()
    own_vec.wait()

    @pl.when(core == home)
    def _():
        own_e.wait()

    @pl.when(core != home)
    def _():
        swap_e.wait_recv()

    for origin in range(ranks):

        @pl.when(jnp.logical_not((core == home) & (rank == origin)))
        def _():
            remote(
                idx_ref.at[0], iall_ref.at[origin], idx_send.at[0, 0], idx_recv.at[origin], sibling
            ).wait_recv()

    gather_kv.arrive()

    def give_kv(step):
        return remote(
            piece_ref.at[step], got_ref.at[step], kvsend.at[step], kvrecv.at[step],
            (core, lax.rem(seq + 1 + step, depth), rank),
        )

    def pick(step):
        retrieve(lax.rem(seq + 1 + step, depth), step, enc_ref, wkv_ref, vall_ref, iall_ref, piece_ref)

    pick(0)
    gather_s.forward()
    for copy in loads[2]:
        copy.wait()
    gather_sq.start()
    pick(1)
    chain_step(2)
    pick(2)
    pick(3)
    for step in range(3, depth):
        chain_step(step)
    for step in range(depth - 1):
        give_kv(step).start()
    gather_s.arrive()
    gather_sq.forward()
    for copy in loads[3]:
        copy.wait()
    gather_w1.start()
    for block in range(depth):
        aside(block).wait_recv()

    outs = [
        pltpu.make_async_copy(src, dst, out_sem.at[n])
        for n, (src, dst) in enumerate(
            (
                (xall_ref, xout_ref),
                (enc_ref, eout_ref),
                (wkv_ref, wkvout_ref),
                (ws_ref, wsout_ref),
                (sq_ref, sqout_ref),
                (w1all_ref, w1out_ref),
                (w2all_ref, w2out_ref),
            )
        )
    ]
    for copy in outs[:4]:
        copy.start()

    w = jnp.concatenate([head_rows(ws_ref, seq, n, which, head) for n in range(3) for which in (2 * core, 1)], axis=0)
    rows = [vall_ref[seq, n : n + 1, :] for n in range(2)]
    bias = column_of(
        jnp.concatenate(
            [
                piece
                for row in rows
                for piece in (jnp.where(core == 0, row[:, :head], row[:, 2 * head : 3 * head]), row[:, head : 2 * head])
            ],
            axis=1,
        )
    )

    def project(block, carry):
        lanes = pl.ds(pl.multiple_of(block * FULL, FULL), FULL)
        flat = dot_nt(w, xall_ref[block // cores, lax.rem(block, cores)])
        q = ((flat[: 2 * head] + bias[: 2 * head]) * SCALE).astype(low)
        shared = jnp.where(core == 0, q[head:, :HALF], q[head:, HALF:])
        q_ref[block] = jnp.concatenate([q[:head], shared], axis=1)
        k = flat[2 * head : 4 * head].astype(low)
        v = (flat[4 * head :] + bias[2 * head :]).astype(low)
        kt_ref[:, lanes] = k
        vt_ref[:, lanes] = v
        k_ref[lanes, :] = k.T
        v_ref[lanes, :] = v.T
        return carry

    lax.fori_loop(0, blocks, project, 0)

    back = ColumnSend(cores, depth, o_ref, oall_ref, osend, orecv)

    def attend(block):
        out, lse = attend_block(block, True, core, blocks * FULL, q_ref[block], k_ref, vt_ref, s_ref)
        o_ref[block] = out
        lse_ref[block] = lse
        return out

    def step(n, carry):
        attend(lax.rem(mine + 1 + n, blocks))
        back.copy(n).start()
        return carry

    lax.fori_loop(0, 3, step, 0)
    gather_sq.arrive()
    outs[4].start()
    lax.fori_loop(3, 6, step, 0)
    gather_w1.forward()
    for copy in loads[4]:
        copy.wait()
    gather_w2.start()
    lax.fori_loop(6, blocks - 1, step, 0)
    oall_ref[mine] = attend(mine)
    for n in range(blocks - 1):
        back.wait_from(n)

    part = 3 * head
    o1 = assembled(oall_ref, depth).T
    h1 = xall_ref[seq, core].astype(jnp.float32) + dot_nn(o1, late_square(sq_ref, 0, part)) + as_row(bo_ref)
    z, _ = centred_rows(h1)
    y1 = (z * as_row(gain_ref) + as_row(shift_ref)).astype(low)
    h_ref[...] = h1
    y_ref[...] = y1
    bias2 = column_of(jnp.concatenate([vall_ref[of, 2:3, :part] for of in range(ranks)], axis=1))
    q2t = ((dot_nt(late_square(sq_ref, 1, part), y1) + bias2) * SCALE).astype(low)
    dispersed(q2t, qsrc_ref, depth)
    ask = ColumnSend(cores, depth, qsrc_ref, q2_ref, qsend, qrecv)
    for n in range(blocks - 1):
        ask.copy(n).start()
    q2_ref[mine] = qsrc_ref[mine]

    slots = k2_ref.shape[0]
    total = piece_ref[depth - 1]
    for n in range(depth - 1):
        give_kv(n).wait_recv()
        total = total + got_ref[n]
    half_ref[...] = total[:, slots:]
    swap = remote(half_ref, other_ref, half_sem.at[0], half_sem.at[1], sibling)
    swap.start()
    gather_w1.arrive()
    outs[5].start()
    swap.wait()
    half, other = half_ref[...], other_ref[...]
    shared = jnp.concatenate([jnp.where(core == 0, half, other), jnp.where(core == 0, other, half)], axis=1)
    kt = jnp.concatenate([total[:head, :slots], shared[:head]], axis=0)
    vt = jnp.concatenate([total[head:, :slots], shared[head:]], axis=0)
    k2t_ref[...] = kt
    v2t_ref[...] = vt
    k2_ref[...] = kt.T
    v2_ref[...] = vt.T

    back2 = ColumnSend(cores, depth, o2_ref, o2all_ref, o2send, o2recv)

    def attend2(block):
        out, lse = attend_block(block, False, core, slots, q2_ref[block], k2_ref, v2t_ref, s_ref)
        o2_ref[block] = out
        lse2_ref[block] = lse
        return out

    o2all_ref[mine] = attend2(mine)

    def step2(n, carry):
        ask.wait_from(n)
        attend2(lax.rem(mine + blocks - 1 - n, blocks))
        back2.copy(blocks - 2 - n).start()
        return carry

    lax.fori_loop(0, 2, step2, 0)
    gather_w2.forward()
    lax.fori_loop(2, 5, step2, 0)
    gather_w2.arrive()
    outs[6].start()
    lax.fori_loop(5, blocks - 1, step2, 0)

    for n in range(depth - 1):
        give_kv(n).wait_send()
    for n in range(depth):
        up, down = seq - n, seq + n

        @pl.when((up >= 0) & (seq + 1 < depth))
        def _():
            chain(up, above, 0).wait_send()

        @pl.when((down < depth) & (seq > 0))
        def _():
            chain(down, below, 1).wait_send()

        aside(n).wait_send()

    @pl.when(core == home)
    def _():
        for copy in (swap_x, swap_g, swap_e):
            copy.wait_send()
        own_g.wait()

    @pl.when(core != home)
    def _():
        swap_g.wait_recv()

    for item in range(per_core):
        for half in range(cores):

            @pl.when(jnp.logical_not(is_me(item, half)))
            def _():
                give_index(item, half).wait_send()

    ask.finish_sends()
    back.finish_sends()
    back2.finish()
    for gather in gathers:
        gather.finish()
    for copy in outs:
        copy.wait()


def front(dec_input, out_grad, encoder_states, retrieved, vectors, kv, selfs, squares, w1, w2, rows1):
    cores, depth, ranks = lax.axis_size(ITEM), lax.axis_size(SEQ), lax.axis_size(TENSOR)
    per_core, _, width = dec_input.shape
    enc_rows = encoder_states.shape[1]
    slots = retrieved.shape[2]
    part = kv[0].shape[0]
    head = part // 3
    places = cores * depth
    rows = places * FULL
    lanes = width // cores
    low, full = jnp.bfloat16, jnp.float32
    dma = pltpu.SemaphoreType.DMA

    def all_of(weights):
        return (cores, ranks, sum(w.shape[0] for w in weights), lanes)

    big = [(depth, cores, FULL, width), (enc_rows, width)] + [all_of(w) for w in (kv, selfs, squares, [w1], [w2])]
    kv_shape = (2 * head, slots + slots // 2)
    parts = (places, head, WIDE)
    small = [
        ((FULL, width), low),
        ((ranks,) + retrieved.shape[1:], retrieved.dtype),
        ((ranks,) + vectors.shape, vectors.dtype),
        ((places, head, WIDE), low),
        ((rows, 2 * head), low),
        ((2 * head, rows), low),
        ((rows, 2 * head), low),
        ((places, head, WIDE), low),
        ((places, 1, WIDE), full),
        (parts, low),
        ((FULL, width), full),
        ((FULL, width), low),
        (parts, low),
        ((slots, 2 * head), low),
        ((2 * head, slots), low),
        ((slots, 2 * head), low),
        (parts, low),
        ((places, 1, WIDE), full),
        (parts, low),
    ]
    return call_kernel(
        functools.partial(front_kernel, (cores, depth, ranks, per_core)),
        "front",
        [(shape, low) for shape in big] + small,
        [dec_input, out_grad, encoder_states, retrieved, vectors, *kv, *selfs, *squares, w1, w2, *rows1],
        scratch=[pltpu.VMEM(shape, low) for shape in big]
        + [
            pltpu.VMEM((depth,) + kv_shape, low),
            pltpu.VMEM((depth - 1,) + kv_shape, low),
            pltpu.VMEM((2 * head, rows), low),
            pltpu.VMEM((rows, WIDE), full),
            pltpu.VMEM(parts, low),
            pltpu.VMEM((2 * head, slots // 2), low),
            pltpu.VMEM((2 * head, slots // 2), low),
            pltpu.VMEM((2 * head, slots), low),
            dma((2, cores)),
            dma((3, cores)),
            dma((3, cores)),
            dma((1, cores)),
            dma((1, cores)),
            dma((3,)),
            dma((3,)),
            dma((2, depth)),
            dma((depth,)),
            dma((depth,)),
            dma((depth,)),
            dma((6,)),
            dma((per_core, cores)),
            dma((ranks,)),
        ]
        + send_scratch(ranks)
        + send_scratch(depth)
        + send_scratch(places)
        + [dma((7,)), dma((2,))]
        + send_scratch(places)
        + send_scratch(places)
        + gather_scratch() * 5,
        collective_id=1,
        in_spaces=[pl.ANY] * 15 + [pltpu.VMEM] * 3,
        out_space=[pl.ANY] * 7 + [pltpu.VMEM] * len(small),
        us=90,
    )


def dot_nn(first_op, second_op):
    return lax.dot_general(first_op, second_op, (((1,), (0,)), ((), ())), preferred_element_type=jnp.float32)


def dot_nt(first_op, second_op):
    return lax.dot_general(first_op, second_op, (((1,), (1,)), ((), ())), preferred_element_type=jnp.float32)


def head_rows(ref, group, matrix, head_index, head):
    start = pl.multiple_of(matrix * 3 * head + head_index * head, head)
    rows = pl.ds(start, head)
    return jnp.concatenate([ref[half, group, rows, :] for half in range(ref.shape[0])], axis=1)


def as_row(ref):
    return ref[...].reshape(1, ref.shape[0])


def column_of(row):
    return jnp.broadcast_to(row, (8, row.shape[1])).T[:, :1]


def kv_rows(w_ref, group, head_index, head):
    return jnp.concatenate(
        [head_rows(w_ref, group, 0, head_index, head), head_rows(w_ref, group, 1, head_index, head)], axis=0
    )


def retrieve(group, step, enc_ref, w_ref, vec_ref, idx_ref, out_ref):
    core, seq, _ = here()
    enc_rows = enc_ref.shape[0]
    slots = idx_ref.shape[2]
    head = out_ref.shape[1] // 2
    low = jnp.bfloat16
    tall = enc_rows // 3

    def picked(table, index):
        total = jnp.zeros((table.shape[0], index.shape[1]), jnp.float32)
        for part in range(3):
            place = lax.broadcasted_iota(jnp.int32, (tall, index.shape[1]), 0) + (part * tall + seq * enc_rows)
            hot = jnp.where(place == index, 1.0, 0.0).astype(low)
            total = total + dot_nn(table[:, part * tall : (part + 1) * tall], hot)
        return total.astype(low)

    w = jnp.concatenate([kv_rows(w_ref, group, 2 * core, head), kv_rows(w_ref, group, 1, head)], axis=0)
    row = vec_ref[group, 3:4, :]
    blank = jnp.zeros((1, head), jnp.float32)
    first = jnp.where(core == 0, row[:, :head], row[:, 2 * head : 3 * head])
    bias = column_of(jnp.concatenate([blank, first, blank, row[:, head : 2 * head]], axis=1))
    table = (dot_nt(w, enc_ref[...]) + bias).astype(low)
    whole = idx_ref[group, pl.ds(2 * core, 1), :]
    shared = idx_ref[group, pl.ds(1, 1), :]
    half = jnp.where(core == 0, shared[:, : slots // 2], shared[:, slots // 2 :])
    out_ref[step] = jnp.concatenate([picked(table[: 2 * head], whole), picked(table[2 * head :], half)], axis=1)


def assembled(parts_ref, depth, columns=None):
    pieces = []
    for group in range(depth):
        first, second = parts_ref[2 * group], parts_ref[2 * group + 1]
        pieces += [
            first[:, :FULL],
            jnp.concatenate([first[:, FULL:WIDE], second[:, FULL:WIDE]], axis=1),
            second[:, :FULL],
        ]
    return jnp.concatenate(pieces, axis=0)


def dispersed(rows, parts_ref, depth):
    head = rows.shape[0] // (3 * depth)
    for group in range(depth):
        a = rows[3 * group * head : (3 * group + 1) * head]
        b = rows[(3 * group + 1) * head : (3 * group + 2) * head]
        c = rows[(3 * group + 2) * head : (3 * group + 3) * head]
        parts_ref[2 * group] = jnp.concatenate([a, b[:, :HALF]], axis=1)
        parts_ref[2 * group + 1] = jnp.concatenate([c, b[:, HALF:]], axis=1)


def late_square(ref, matrix, rows):
    cores, ranks = ref.shape[0], ref.shape[1]
    return jnp.concatenate(
        [
            jnp.concatenate([ref[half, rank, matrix * rows : (matrix + 1) * rows, :] for half in range(cores)], axis=1)
            for rank in range(ranks)
        ],
        axis=0,
    )


def centred_rows(h):
    center = h - jnp.mean(h, axis=-1, keepdims=True)
    spread = lax.rsqrt(jnp.mean(center * center, axis=-1, keepdims=True) + EPS)
    return center * spread, spread


def norm_back(z, spread, dy, gain):
    dz = dy * gain
    dh = spread * (
        dz - jnp.mean(dz, axis=-1, keepdims=True) - z * jnp.mean(dz * z, axis=-1, keepdims=True)
    )
    return dh, jnp.sum(dy * z, axis=0, keepdims=True), jnp.sum(dy, axis=0, keepdims=True)


def middle_kernel(
    cores, depth, ranks, per_core, part,
    o_ref, y1_ref, g_ref, w_ref, w1_in, w2_in, bo_ref, gain2_ref, shift2_ref, b1_ref, b2_ref, gain3_ref, shift3_ref,
    layer_ref, do_ref, dh2_ref, vec_ref, grad_ref,
    w1_ref, w2_ref, slope_ref, a_ref, df_ref, out_ref, dosrc_ref, turn_ref, give_ref, got_ref,
    ffn_sem, grad_sem, dosend, dorecv, *deal_sems
):
    low = jnp.bfloat16
    core, seq, rank = here()
    count = cores * depth
    mine, places = column_places(cores, depth)
    peers = [column_peer(place, cores, rank) for place in places]
    peers += [(half, seq, lax.rem(rank + step, ranks)) for step in range(1, ranks) for half in range(cores)]
    greet(peers)
    width = y1_ref.shape[1]
    lanes = width // cores
    loads = [
        pltpu.make_async_copy(src, dst, ffn_sem.at[n]) for n, (src, dst) in enumerate(((w1_in, w1_ref), (w2_in, w2_ref)))
    ]
    for load in loads:
        load.start()
    o2t = assembled(o_ref, depth)
    wo2 = late_square(w_ref, 2, part)
    h2 = y1_ref[...].astype(jnp.float32) + dot_nn(o2t.T, wo2) + as_row(bo_ref)
    z2, spread2 = centred_rows(h2)
    y2 = (z2 * as_row(gain2_ref) + as_row(shift2_ref)).astype(low)

    def hidden_in(of, half):
        return w1_ref[half, of]

    def hidden_out(of):
        return jnp.concatenate([w2_ref[half, of] for half in range(cores)], axis=1)

    root = 0.7071067811865476
    h3 = y2.astype(jnp.float32) + as_row(b2_ref)
    for load in loads:
        load.wait()
    for of in range(ranks):
        f = jnp.concatenate([dot_nn(y2, hidden_in(of, half)) for half in range(cores)], axis=1) + b1_ref[of, 4:5, :]
        cdf = 0.5 * (1.0 + lax.erf(f * root))
        a = (f * cdf).astype(low)
        slope_ref[of] = cdf + f * (0.3989422804014327 * jnp.exp(-0.5 * f * f))
        a_ref[of] = a
        h3 = h3 + dot_nn(a, hidden_out(of))
    z3, spread3 = centred_rows(h3)
    out_ref[...] = (z3 * as_row(gain3_ref) + as_row(shift3_ref)).astype(low)
    pl.semaphore_wait(pltpu.get_barrier_semaphore(), len(peers))
    deal = Deal(cores, ranks, per_core, lambda target: out_ref, layer_ref, *deal_sems)
    deal.start()

    dh3, gg3, gs3 = norm_back(z3, spread3, g_ref[...].astype(jnp.float32), as_row(gain3_ref))
    e3 = dh3.astype(low)
    dy2 = dh3
    for of in range(ranks):
        df = (dot_nt(e3, hidden_out(of)) * slope_ref[of]).astype(low)
        df_ref[of] = df
        for half in range(cores):
            dy2 = dy2 + dot_nt(df[:, half * lanes : (half + 1) * lanes], hidden_in(of, half))
    dh2, gg2, gs2 = norm_back(z2, spread2, dy2, as_row(gain2_ref))
    e2 = dh2.astype(low)
    dispersed(dot_nt(wo2, e2).astype(low), dosrc_ref, depth)
    ask = ColumnSend(cores, depth, dosrc_ref, do_ref, dosend, dorecv)
    for step in range(count - 1):
        ask.copy(step).start()
    do_ref[mine] = dosrc_ref[mine]

    dh2_ref[...] = dh2
    vec_ref[0:1] = gg3
    vec_ref[1:2] = gs3
    vec_ref[2:3] = jnp.sum(e3.astype(jnp.float32), axis=0, keepdims=True)
    vec_ref[3:4] = gg2
    vec_ref[4:5] = gs2
    vec_ref[5:6] = jnp.sum(e2.astype(jnp.float32), axis=0, keepdims=True)
    turn_ref[0] = y2.T
    turn_ref[1] = e3.T
    turn_ref[2] = e2.T
    pad = jnp.zeros((-part % 128, FULL), low)

    def grad_of(of, half):
        rows = pl.ds(pl.multiple_of(half * lanes, lanes), lanes)
        o2_part = jnp.concatenate([o2t[of * part : (of + 1) * part], pad], axis=0)
        return (
            dot_nn(turn_ref[0, rows, :], df_ref[of]),
            dot_nn(turn_ref[1, rows, :], a_ref[of]),
            dot_nt(turn_ref[2, rows, :], o2_part),
        )

    spans = (slice(0, width), slice(width, 2 * width), slice(2 * width, None))

    def swap(of):
        return remote_copy(
            give_ref.at[of], got_ref.at[of], grad_sem.at[0, of], grad_sem.at[1, of], (1 - core, seq, rank)
        )

    for of in range(ranks):
        vec_ref[6 + of : 7 + of] = jnp.sum(df_ref[of].astype(jnp.float32), axis=0, keepdims=True)
        for span, grad in zip(spans, grad_of(of, 1 - core)):
            give_ref[of, :, span] = grad.astype(low)
        swap(of).start()
    for of in range(ranks):
        grads = grad_of(of, core)
        swap(of).wait_recv()
        for span, grad in zip(spans, grads):
            grad_ref[of, :, span] = (grad + got_ref[of, :, span].astype(jnp.float32)).astype(low)
    for of in range(ranks):
        swap(of).wait_send()
    ask.finish()
    deal.finish()


def middle(per_core, o2, y1, grad_mine, squares, w1, w2, vectors):
    cores, depth, ranks = lax.axis_size(ITEM), lax.axis_size(SEQ), lax.axis_size(TENSOR)
    places, head, _ = o2.shape
    rows, width = y1.shape
    part, lanes, hidden = 3 * head, width // cores, width
    low, full = jnp.bfloat16, jnp.float32
    columns = 2 * hidden + part + (-part % 128)
    return call_kernel(
        functools.partial(middle_kernel, cores, depth, ranks, per_core, part),
        "middle",
        [
            ((per_core, cores, rows, width), low),
            (o2.shape, low),
            ((rows, width), full),
            ((6 + ranks, width), full),
            ((ranks, lanes, columns), low),
        ],
        [o2, y1, grad_mine, squares, w1, w2, *vectors],
        scratch=[
            pltpu.VMEM(w1.shape, low),
            pltpu.VMEM(w2.shape, low),
            pltpu.VMEM((ranks, rows, hidden), full),
            pltpu.VMEM((ranks, rows, hidden), low),
            pltpu.VMEM((ranks, rows, hidden), low),
            pltpu.VMEM((rows, width), low),
            pltpu.VMEM(o2.shape, low),
            pltpu.VMEM((3, width, rows), low),
            pltpu.VMEM((ranks, lanes, columns), low),
            pltpu.VMEM((ranks, lanes, columns), low),
            pltpu.SemaphoreType.DMA((2,)),
            pltpu.SemaphoreType.DMA((2, ranks)),
        ]
        + send_scratch(places)
        + deal_scratch(cores, ranks, per_core),
        collective_id=4,
        in_spaces=[pltpu.VMEM] * 4 + [pl.ANY] * 2 + [pltpu.VMEM] * len(vectors),
        us=22,
    )


def encoder_back(ranks, head, enc_ref, w_ref, idx_ref, dkv_ref, part_ref, grad_ref):
    core, seq, _ = here()
    low = jnp.bfloat16
    enc_rows, width = enc_ref.shape
    slots = idx_ref.shape[2]
    cores = w_ref.shape[0]
    lanes = width // cores
    part = width // ranks
    fold = enc_rows // (2 * cores)
    enc_t = enc_ref[...].T

    tables = []
    rows_w = []
    for group in range(ranks):
        heads = []
        shared = idx_ref[group, pl.ds(1, 1), :]
        shared = jnp.where(core == 0, shared[:, : slots // 2], shared[:, slots // 2 :])
        for which, index, rows in (
            (2 * core, idx_ref[group, pl.ds(2 * core, 1), :], slice(0, slots)),
            (1, shared, slice(slots, slots + slots // 2)),
        ):
            pieces = []
            for third in range(3):
                tall = enc_rows // 3
                place = lax.broadcasted_iota(jnp.int32, (tall, index.shape[1]), 0) + (third * tall + seq * enc_rows)
                hot = jnp.where(place == index, 1.0, 0.0).astype(low)
                pieces.append(dot_nn(hot, dkv_ref[group, rows, :]).astype(low))
            table = jnp.concatenate(pieces, axis=0)
            heads.append(table)
            tables.append(table)
            rows_w.append(kv_rows(w_ref, group, which, head))
        both = jnp.concatenate(heads, axis=1)
        grad = dot_nn(enc_t, both).astype(low)
        whole, shared = grad[:, : 2 * head], grad[:, 2 * head :]
        blank = jnp.zeros_like(whole)
        left = jnp.where(core == 0, whole, blank)
        right = jnp.where(core == 0, blank, whole)
        for half in range(cores):
            rows = slice(half * lanes, (half + 1) * lanes)
            grad_ref[half, group] = jnp.concatenate([left[rows], shared[rows], right[rows]], axis=1)
    table = jnp.concatenate(tables, axis=1)
    w = jnp.concatenate(rows_w, axis=0)
    for rank in range(ranks):
        cols = w[:, rank * part : (rank + 1) * part]
        flat = dot_nn(table, cols).astype(low)
        for half in range(cores):
            low_rows = flat[2 * half * fold : (2 * half + 1) * fold]
            high_rows = flat[(2 * half + 1) * fold : (2 * half + 2) * fold]
            part_ref[half, rank] = jnp.concatenate([low_rows, high_rows], axis=1)


class SeqSum:
    def __init__(self, depth, src_ref, all_ref, send_sem, recv_sem):
        self.depth, self.src_ref, self.all_ref = depth, src_ref, all_ref
        self.send_sem, self.recv_sem = send_sem, recv_sem
        self.core, self.seq, self.rank = here()

    def copy(self, step):
        target = lax.rem(self.seq + 1 + step, self.depth)
        return remote_copy(
            self.src_ref.at[target],
            self.all_ref.at[self.seq],
            self.send_sem.at[step],
            self.recv_sem.at[step],
            (self.core, target, self.rank),
        )

    def start(self):
        for step in range(self.depth - 1):
            self.copy(step).start()

    def finish(self):
        for step in range(self.depth - 1):
            self.copy(step).wait()
        self.all_ref[self.seq] = self.src_ref[self.seq]
        total = self.all_ref[0].astype(jnp.float32)
        for origin in range(1, self.depth):
            total = total + self.all_ref[origin].astype(jnp.float32)
        return total


def input_rows(depth, parts_ref, dh1_ref, w_ref):
    low = jnp.bfloat16
    part = 3 * parts_ref.shape[1]
    dqt = assembled(parts_ref, depth)
    stack_k, stack_v = [], []
    for group in range(depth):
        first, second = parts_ref[2 * group], parts_ref[2 * group + 1]
        for n, stack in ((0, stack_k), (1, stack_v)):
            whole = slice(WIDE + n * FULL, WIDE + (n + 1) * FULL)
            shared = slice(WIDE + 2 * FULL + n * HALF, WIDE + 2 * FULL + (n + 1) * HALF)
            both = jnp.concatenate([first[:, shared], second[:, shared]], axis=1)
            stack += [first[:, whole], both, second[:, whole]]
    dx = dh1_ref[...] + dot_nn(dqt.T, late_square(w_ref, 0, part)) * SCALE
    dx = dx + dot_nn(jnp.concatenate(stack_k, axis=0).T, late_square(w_ref, 1, part))
    dx = dx + dot_nn(jnp.concatenate(stack_v, axis=0).T, late_square(w_ref, 2, part))
    return dx.astype(low)


def merge_heads(depth, head, column_ref, group_ref):
    low = group_ref.dtype
    for group in range(depth):
        first, second = column_ref[2 * group], column_ref[2 * group + 1]
        pieces = []
        for n in range(3):
            whole = slice(2 * n * head, (2 * n + 1) * head)
            shared = slice((2 * n + 1) * head, (2 * n + 2) * head)
            both = (first[:, shared].astype(jnp.float32) + second[:, shared].astype(jnp.float32)).astype(low)
            pieces += [first[:, whole], both, second[:, whole]]
        group_ref[group] = jnp.concatenate(pieces, axis=1)


def outputs_kernel(
    ranks, part, head,
    total_ref, squares_ref, pairs_ref, rest_ref, vec_ref,
    wq1_ref, wk1_ref, wv1_ref, wo1_ref, wq2_ref, wk2_ref, wv2_ref, wo2_ref, w2_ref,
    bq1_ref, bv1_ref, bo1_ref, g1_ref, s1_ref, bq2_ref, bv2_ref, bo2_ref, g2_ref, s2_ref, b1_ref, b2_ref, g3_ref, s3_ref,
):
    rank = lax.axis_index(TENSOR)
    height = vec_ref.shape[1]

    def line(n):
        return vec_ref[n // height, n % height : n % height + 1, :]

    def whole(row):
        return row.reshape(row.shape[1])

    def rank_part(row):
        found = row[:, :part]
        for other in range(1, ranks):
            found = jnp.where(rank == other, row[:, other * part : (other + 1) * part], found)
        return whole(found)

    for ref, n in ((g3_ref, 0), (s3_ref, 1), (b2_ref, 2), (g2_ref, 3), (s2_ref, 4), (bo2_ref, 5)):
        ref[...] = whole(line(n))
    hidden = line(6)
    for other in range(1, ranks):
        hidden = jnp.where(rank == other, line(6 + other), hidden)
    b1_ref[...] = whole(hidden)
    for ref, n in ((g1_ref, 0), (s1_ref, 1), (bo1_ref, 2)):
        ref[...] = whole(line(6 + ranks + n))
    bq2_ref[...] = rank_part(line(9 + ranks))
    bv2_ref[...] = rank_part(line(10 + ranks))
    squares = squares_ref[...]
    wq2_ref[...] = squares[:, :part] * SCALE
    wo1_ref[...] = squares[:, part:].T
    pairs = pairs_ref[...]
    for n, ref in enumerate((wk2_ref, wv2_ref)):
        ref[...] = jnp.concatenate(
            [pairs[:, (2 * k + n) * head : (2 * k + n + 1) * head] for k in range(3)], axis=1
        )
    span = w2_ref.shape[1]
    w2_ref[...] = rest_ref[:, :span]
    wo2_ref[...] = rest_ref[:, span : span + part].T
    total = total_ref[...]
    rows = wq1_ref.shape[0]
    wq1_ref[...] = total[:rows, :part] * SCALE
    wk1_ref[...] = total[:rows, part : 2 * part]
    wv1_ref[...] = total[:rows, 2 * part :]
    bq1_ref[...] = whole(total[rows : rows + 1, :part] * SCALE)
    bv1_ref[...] = whole(total[rows : rows + 1, 2 * part :])


def outputs(head, width, total, squares, pairs, rest, vectors):
    ranks = lax.axis_size(TENSOR)
    few, part, full = squares.shape[0], 3 * head, jnp.float32
    square, turned = ((few, part), full), ((part, few), full)
    long, short = ((width,), full), ((part,), full)
    return call_kernel(
        functools.partial(outputs_kernel, ranks, part, head),
        "outputs",
        [square, square, square, turned, square, square, square, turned, ((few, width), full)]
        + [short, short, long, long, long, short, short, long, long, long, long, long, long, long],
        [total, squares, pairs, rest, vectors],
        us=2,
    )


def self_grads(blocks, cores, places, x_ref, g_ref, out_ref):
    core, seq, rank = here()
    low = jnp.bfloat16
    head = g_ref.shape[1]
    width = x_ref.shape[2]
    rows = width // places
    total = jnp.zeros((width, 6 * head), jnp.float32)
    sums = jnp.zeros((16, 6 * head), jnp.float32)
    ones = jnp.ones((16, FULL), low)
    zero = jnp.zeros((head, HALF), low)
    for block in range(blocks):
        g = g_ref[block]

        def own_half(first):
            part = g[:, first : first + HALF]
            return jnp.where(
                core == 0, jnp.concatenate([part, zero], axis=1), jnp.concatenate([zero, part], axis=1)
            )

        whole = WIDE + 2 * FULL
        flat = jnp.concatenate(
            [
                g[:, :FULL],
                own_half(FULL),
                g[:, WIDE : WIDE + FULL],
                own_half(whole),
                g[:, WIDE + FULL : whole],
                own_half(whole + HALF),
            ],
            axis=0,
        )
        total = total + dot_nt(x_ref[block].T, flat)
        sums = sums + dot_nt(ones, flat)
    for place in range(places):
        start = ((place % cores) * (places // cores) + place // cores) * rows
        out_ref[place, :rows, :] = total[start : start + rows].astype(low)
        out_ref[place, rows:, :] = sums.astype(low)


def widen(block):
    lane = lax.broadcasted_iota(jnp.int32, block.shape, 1)
    zero = jnp.zeros_like(block)
    return jnp.concatenate([jnp.where(lane < FULL, block, zero), jnp.where(lane < FULL, zero, block)], axis=0)


def narrow(block):
    head = block.shape[0] // 2
    return jnp.concatenate([block[:head, :FULL], block[head:, FULL:]], axis=1)


def causal_block(core):
    key = lax.broadcasted_iota(jnp.int32, (FULL, WIDE), 0)
    lane = lax.broadcasted_iota(jnp.int32, (FULL, WIDE), 1)
    token = jnp.where(lane < FULL, lane, lane - FULL + HALF * core)
    return key <= token


def attend_block(block, causal, core, slots, q, k_ref, vt_ref, s_ref):
    low = jnp.bfloat16
    head = q.shape[0]
    wide = widen(q)
    last = block if causal else slots // FULL

    def rows_of(key_block):
        return pl.ds(pl.multiple_of(key_block * FULL, FULL), FULL)

    def top_of(s):
        return jnp.max(s.reshape(FULL // 8, 8, WIDE), axis=0)

    def look(key_block, top):
        rows = rows_of(key_block)
        s = dot_nn(k_ref[rows, :], wide)
        s_ref[rows, :] = s
        return jnp.maximum(top, top_of(s))

    top = lax.fori_loop(0, last, look, jnp.full((8, WIDE), NEG, jnp.float32))
    if causal:
        rows = rows_of(block)
        s = jnp.where(causal_block(core), dot_nn(k_ref[rows, :], wide), NEG)
        s_ref[rows, :] = s
        top = jnp.maximum(top, top_of(s))
        last = block + 1
    top = jnp.max(top, axis=0, keepdims=True)

    def gather(key_block, state):
        total, out = state
        rows = rows_of(key_block)
        p = jnp.exp(s_ref[rows, :] - top)
        total = total + jnp.sum(p.reshape(FULL // 8, 8, WIDE), axis=0)
        out = out + dot_nn(vt_ref[:, rows], p.astype(low))
        return total, out

    total, out = lax.fori_loop(
        0, last, gather, (jnp.zeros((8, WIDE), jnp.float32), jnp.zeros((2 * head, WIDE), jnp.float32))
    )
    total = jnp.sum(total, axis=0, keepdims=True)
    return (narrow(out) / total).astype(low), top + jnp.log(total)


def back_block(block, causal, core, slots, q, do, o, lse, k_ref, kt_ref, v_ref, whole_ref, shared_ref):
    low = jnp.bfloat16
    head = q.shape[0]
    wide_q, wide_do = widen(q), widen(do)
    delta = jnp.sum(do.astype(jnp.float32) * o.astype(jnp.float32), axis=0, keepdims=True)
    qd = jnp.concatenate([q, jnp.zeros_like(q)], axis=0).T
    dd = jnp.concatenate([jnp.zeros_like(do), do], axis=0).T
    mix_whole = jnp.concatenate([qd[:FULL], dd[:FULL]], axis=0)
    mix_shared = jnp.concatenate([qd[FULL:], dd[FULL:]], axis=0)

    def one(key_block, dq, masked):
        rows = pl.ds(pl.multiple_of(key_block * FULL, FULL), FULL)
        s = dot_nn(k_ref[rows, :], wide_q)
        if masked:
            s = jnp.where(causal_block(core), s, NEG)
        p = jnp.exp(s - lse)
        dp = dot_nn(v_ref[rows, :], wide_do)
        ds = (p * (dp - delta)).astype(low)
        p = p.astype(low)
        dq = dq + dot_nn(kt_ref[:, rows], ds)
        whole_ref[rows, :] += dot_nn(jnp.concatenate([ds[:, :FULL], p[:, :FULL]], axis=1), mix_whole)
        shared_ref[rows, :] += dot_nn(jnp.concatenate([ds[:, FULL:], p[:, FULL:]], axis=1), mix_shared)
        return dq

    last = block if causal else slots // FULL
    dq = lax.fori_loop(0, last, lambda kb, dq: one(kb, dq, False), jnp.zeros((2 * head, WIDE), jnp.float32))
    if causal:
        dq = one(block, dq, True)
    return narrow(dq).astype(low)


def cross_back_kernel(
    cores, depth,
    q_ref, k_ref, kt_ref, v_ref, o_ref, lse_ref, do_ref, grad_ref,
    dqall_ref, dkv_ref, bv_ref, sum_ref,
    dq_ref, whole_ref, shared_ref, give_ref, got_ref, swap_sem, send_sem, recv_sem, *sum_refs
):
    core, seq, rank = here()
    low = jnp.bfloat16
    count = cores * depth
    mine, places = column_places(cores, depth)
    hidden = PlaneSum(grad_ref.shape[0], grad_ref, 0, *sum_refs)
    peers = [column_peer(place, cores, rank) for place in places] + hidden.peers
    greet(peers)
    slots = k_ref.shape[0]
    whole_ref[...] = jnp.zeros_like(whole_ref)
    shared_ref[...] = jnp.zeros_like(shared_ref)
    back = ColumnSend(cores, depth, dq_ref, dqall_ref, send_sem, recv_sem)

    def go(block):
        return back_block(
            block, False, core, slots, q_ref[block], do_ref[block], o_ref[block], lse_ref[block],
            k_ref, kt_ref, v_ref, whole_ref, shared_ref,
        )

    pl.semaphore_wait(pltpu.get_barrier_semaphore(), len(peers))
    hidden.start()
    dq_ref[places[0]] = go(places[0])
    back.copy(0).start()

    def step(n, carry):
        block = lax.rem(mine + 1 + n, count)
        dq_ref[block] = go(block)
        back.copy(n).start()
        return carry

    lax.fori_loop(1, count - 1, step, 0)
    dqall_ref[mine] = go(mine)
    half = slots // 2
    give_ref[...] = shared_ref[pl.ds(pl.multiple_of((1 - core) * half, half), half), :].astype(low)
    swap = remote_copy(give_ref, got_ref, swap_sem.at[0], swap_sem.at[1], (1 - core, seq, rank))
    swap.start()
    dkv_ref[:slots] = whole_ref[...].astype(low)
    swap.wait()
    kept = shared_ref[pl.ds(pl.multiple_of(core * half, half), half), :]
    dkv_ref[slots:] = (kept + got_ref[...].astype(jnp.float32)).astype(low)
    head = q_ref.shape[1]
    first = jnp.sum(dkv_ref[:slots].astype(jnp.float32), axis=0, keepdims=True)[:, head:]
    second = jnp.sum(dkv_ref[slots:].astype(jnp.float32), axis=0, keepdims=True)[:, head:]
    bv_ref[...] = jnp.concatenate(
        [
            jnp.where(n == 3 * seq + 2 * core, first, jnp.where(n == 3 * seq + 1, second, 0.0))
            for n in range(3 * depth)
        ],
        axis=1,
    )
    back.finish()
    sum_ref[...] = hidden.finish().astype(low)


def attend_cross_back(q, k, kt, v, o, lse, do, grad, columns):
    cores, depth, ranks = lax.axis_size(ITEM), lax.axis_size(SEQ), lax.axis_size(TENSOR)
    lanes = grad.shape[1]
    places, head, _ = q.shape
    slots = k.shape[0]
    low = jnp.bfloat16
    sums = pltpu.VMEM((slots, 2 * head), jnp.float32)
    return call_kernel(
        functools.partial(cross_back_kernel, cores, depth),
        "back_cross",
        [
            (q.shape, low),
            ((slots + slots // 2, 2 * head), low),
            ((1, 3 * depth * head), jnp.float32),
            ((lanes, columns), low),
        ],
        [q, k, kt, v, o, lse, do, grad],
        scratch=[
            pltpu.VMEM(q.shape, low),
            sums,
            sums,
            pltpu.VMEM((slots // 2, 2 * head), low),
            pltpu.VMEM((slots // 2, 2 * head), low),
            pltpu.SemaphoreType.DMA((2,)),
        ]
        + send_scratch(places)
        + sum_scratch(ranks, lanes, columns, low),
        collective_id=5,
        in_spaces=[pltpu.VMEM] * 7 + [pl.ANY],
        us=24,
    )


def self_back_kernel(
    cores, depth, ranks, part,
    dq2_ref, dh2_ref, h1_ref, y1_ref, oin_ref, w_in, gain_ref,
    q_ref, k_ref, kt_ref, v_ref, o_ref, lse_ref, dkv_ref, idx_ref, vmid_ref, bv_ref, red1_ref,
    enc_in, wkv_in, ws_in, x_in, grad_ref,
    in_ref, encg_ref, total_ref, squares_ref, pairs_ref, rest_ref, w1_ref, vout_ref,
    w_ref, enc_ref, wkv_ref, ws_ref, x_ref, encp_ref, got_ref, sum_ref, encall_ref,
    dosrc_ref, do_ref, g_ref, gall_ref, whole_ref, shared_ref, dkvall_ref, grad2_ref,
    dh1_ref, dx_ref, self_ref, column_ref, group_ref, plane_ref,
    red2_ref, red4_ref, red5_ref, r1_ref, r2_ref, r4_ref, r5_ref,
    give_ref, gots_ref, shsend, shrecv, load_sem, swap_sem, dosend, dorecv, gsend, grecv, kvsend, kvrecv, csend, crecv, psend, precv, zsend, zrecv, *more
):
    core, seq, rank = here()
    low = jnp.bfloat16
    count = cores * depth
    head = part // 3
    per_core = encg_ref.shape[0]
    mine, places = column_places(cores, depth)
    first = PlaneReduce(ranks, grad2_ref, *more[:6])
    second = PlaneReduce(ranks, grad2_ref, more[6], more[1], *more[7:11])
    deal_enc = Deal(cores, ranks, per_core, lambda target: sum_ref.at[target], encall_ref, *more[11:14])
    deal_in = Deal(cores, ranks, per_core, lambda target: dx_ref, in_ref, *more[14:17])
    hidden = PlaneSum(ranks, grad_ref, grad_ref.shape[2] - red5_ref.shape[2], *more[17:21])
    vectors = VectorSum(cores, depth, ranks, vout_ref, *more[21:])
    along = [
        SeqSum(depth, src, dst, zsend.at[n], zrecv.at[n])
        for n, (src, dst) in enumerate(
            ((red1_ref, r1_ref), (red2_ref, r2_ref), (red4_ref, r4_ref), (red5_ref, r5_ref))
        )
    ]
    loads = [
        pltpu.make_async_copy(src, dst, load_sem.at[n])
        for n, (src, dst) in enumerate(((wkv_in, wkv_ref), (enc_in, enc_ref), (x_in, x_ref), (ws_in, ws_ref)))
    ]
    squares = [
        pltpu.make_async_copy(
            w_in.at[half, of, pl.ds(0, 2 * part), :], w_ref.at[half, of], load_sem.at[4 + half * ranks + of]
        )
        for half in range(cores)
        for of in range(ranks)
    ]
    for load in squares + loads:
        load.start()
    peers = [column_peer(place, cores, rank) for place in places] + first.peers
    peers += [(1 - core, seq, peer[2]) for peer in first.peers]
    greet(peers)
    chain = Chain(depth, dkvall_ref, kvsend, kvrecv)
    dkvall_ref[seq] = dkv_ref[...]
    pl.semaphore_wait(pltpu.get_barrier_semaphore(), len(peers))
    chain.step(0)
    hidden.start()

    width = y1_ref.shape[1]
    lanes = width // cores
    dq2t = assembled(dq2_ref, depth)
    for load in squares:
        load.wait()
    dy1 = dh2_ref[...] + dot_nn(dq2t.T, late_square(w_ref, 1, part)) * SCALE
    z1, spread1 = centred_rows(h1_ref[...])
    dh1, gg1, gs1 = norm_back(z1, spread1, dy1, as_row(gain_ref))
    e1 = dh1.astype(low)
    dispersed(dot_nt(late_square(w_ref, 0, part), e1).astype(low), dosrc_ref, depth)
    ask = ColumnSend(cores, depth, dosrc_ref, do_ref, dosend, dorecv)
    for step in range(count - 1):
        ask.copy(step).start()
    do_ref[mine] = dosrc_ref[mine]
    dh1_ref[...] = dh1
    ones = jnp.ones((8, FULL), low)
    given = [vmid_ref[n : n + 1] for n in range(vmid_ref.shape[0])]
    given += [gg1, gs1, jnp.sum(e1.astype(jnp.float32), axis=0, keepdims=True), dot_nt(ones, dq2t)[0:1] * SCALE]
    given += [bv_ref[...], jnp.zeros_like(gg1)]
    vectors.start(given)
    o1t = assembled(oin_ref, depth)
    both = jnp.concatenate([y1_ref[...].T, e1.T], axis=1)
    blank = jnp.zeros((part, FULL), low)
    for to in range(ranks):
        rows = slice(to * part, (to + 1) * part)
        right = jnp.concatenate(
            [
                jnp.concatenate([dq2t[rows], blank], axis=1),
                jnp.concatenate([blank, o1t[rows]], axis=1),
            ],
            axis=0,
        )
        for half in range(cores):
            grad2_ref[half, to] = dot_nt(both[half * lanes : (half + 1) * lanes], right).astype(low)
    first.start()

    whole_ref[...] = jnp.zeros_like(whole_ref)
    shared_ref[...] = jnp.zeros_like(shared_ref)
    for step in range(count - 1):
        ask.wait_from(step)
    chain.step(1)
    back = ColumnSend(cores, depth, g_ref, gall_ref, gsend, grecv)

    def swap_shared(block):
        return remote_copy(
            give_ref.at[block], gots_ref.at[block], shsend.at[block], shrecv.at[block], (1 - core, seq, rank)
        )

    def go(block):
        g_ref[block, :, :WIDE] = back_block(
            block, True, core, count * FULL, q_ref[block], do_ref[block], o_ref[block], lse_ref[block],
            k_ref, kt_ref, v_ref, whole_ref, shared_ref,
        )
        start = pl.multiple_of(block * FULL, FULL)
        there = pl.ds(pl.multiple_of(start + (1 - core) * HALF, HALF), HALF)
        give_ref[block] = shared_ref[there, :].astype(low)
        swap_shared(block).start()

    def send_back(block):
        start = pl.multiple_of(block * FULL, FULL)
        whole = whole_ref[pl.ds(start, FULL), :].T.astype(low)
        here_rows = pl.ds(pl.multiple_of(start + core * HALF, HALF), HALF)
        swap_shared(block).wait_recv()
        shared = (shared_ref[here_rows, :] + gots_ref[block].astype(jnp.float32)).T.astype(low)
        g_ref[block, :, WIDE:] = jnp.concatenate([whole[:head], whole[head:], shared[:head], shared[head:]], axis=1)

        @pl.when(block != mine)
        def _():
            back.copy(lax.rem(block + 2 * count - mine - 1, count)).start()

        @pl.when(block == mine)
        def _():
            gall_ref[mine] = g_ref[mine]

    def step(n, carry):
        go(count - 1 - n)
        send_back(count - n)
        return carry

    go(count - 1)
    lax.fori_loop(1, 2, step, 0)
    first.middle()
    chain.step(2)
    vectors.second()
    lax.fori_loop(2, 4, step, 0)
    vectors.third()
    along[0].start()
    for load in loads:
        load.wait()
    for n in range(3, depth):
        chain.step(n)

    encoder_back(ranks, head, enc_ref, wkv_ref, idx_ref, dkvall_ref, encp_ref, grad2_ref)
    swap = remote_copy(encp_ref.at[1 - core], got_ref, swap_sem.at[0], swap_sem.at[1], (1 - core, seq, rank))
    swap.start()
    second.start()
    red2_ref[...] = first.finish().astype(low).reshape(red2_ref.shape)
    along[1].start()
    lax.fori_loop(4, 5, step, 0)
    swap.wait()
    sum_ref[...] = (encp_ref[core].astype(jnp.float32) + got_ref[...].astype(jnp.float32)).astype(low)
    deal_enc.start()
    second.middle()
    lax.fori_loop(5, count, step, 0)
    send_back(0)

    self_grads(count, cores, count, x_ref, g_ref, self_ref)
    column = [
        remote_copy(
            self_ref.at[place], column_ref.at[mine], csend.at[step], crecv.at[step], column_peer(place, cores, rank)
        )
        for step, place in enumerate(places)
    ]
    for copy in column:
        copy.start()

    for step in range(count - 1):
        back.wait_from(step)
    dx_ref[...] = input_rows(depth, gall_ref, dh1_ref, ws_ref)
    deal_in.start()

    red5_ref[...] = hidden.finish().astype(low).reshape(red5_ref.shape)
    along[3].start()
    vectors.finish()

    for copy in column:
        copy.wait()
    column_ref[mine] = self_ref[mine]
    merge_heads(depth, head, column_ref, group_ref)
    plane = [
        remote_copy(group_ref.at[peer[2]], plane_ref.at[rank], psend.at[step], precv.at[step], peer)
        for step, peer in enumerate(first.peers)
    ]
    for copy in plane:
        copy.start()
    red4_ref[...] = second.finish().astype(low).reshape(red4_ref.shape)
    along[2].start()

    deal_enc.finish()
    fold = encall_ref.shape[2]
    for item in range(per_core):
        for half in range(cores):
            for side in range(2):
                rows = slice((2 * half + side) * fold, (2 * half + side + 1) * fold)
                encg_ref[item, rows, :] = encall_ref[item, half, :, side * part : (side + 1) * part]
    w1_ref[...] = along[0].finish()
    squares_ref[...] = along[1].finish()
    for copy in plane:
        copy.wait()
    total = group_ref[rank].astype(jnp.float32)
    for step in range(1, ranks):
        total = total + plane_ref[lax.rem(rank + step, ranks)].astype(jnp.float32)
    total_ref[...] = total
    rest_ref[...] = along[3].finish()
    chain.finish()
    ask.finish_sends()
    back.finish_sends()
    for block in range(count):
        swap_shared(block).wait_send()
    deal_in.finish()
    pairs_ref[...] = along[2].finish()


def attend_self_back(per_core, *args):
    cores, depth, ranks = lax.axis_size(ITEM), lax.axis_size(SEQ), lax.axis_size(TENSOR)
    (
        dq2, dh2, h1, y1, o1, squares, gain, q, k, kt, v, o, lse, dkv, index, vec_mid, bv, red1, enc, wkv, ws, x_all, grad
    ) = args
    places, head, _ = q.shape
    rows, width = y1.shape
    low, full = jnp.bfloat16, jnp.float32
    part, lanes = 3 * head, width // cores
    all_rows = places * rows
    dma = pltpu.SemaphoreType.DMA
    grads = (cores, ranks, lanes, 2 * part)
    message = (places, head, WIDE + 2 * FULL + 2 * HALF)
    sums = pltpu.VMEM((all_rows, 2 * head), full)
    fold = enc.shape[0] // (2 * cores)
    rest = grad.shape[2] - width
    vec_shape = (places, (vec_mid.shape[0] + 6) // places, width)
    few = width // places
    high = few + 16
    red1 = red1.reshape(depth, few, width)
    along = [pltpu.VMEM((depth, few, columns), low) for columns in (2 * part, 2 * part, rest)]
    args = (*args[:17], red1, *args[18:])
    return call_kernel(
        functools.partial(self_back_kernel, cores, depth, ranks, part),
        "back_self",
        [
            ((per_core, cores, rows, width), low),
            ((per_core, enc.shape[0], part), low),
            ((high, 3 * part), full),
            ((few, 2 * part), full),
            ((few, 2 * part), full),
            ((few, rest), full),
            ((few, width), full),
            (vec_shape, full),
        ],
        list(args),
        scratch=[
            pltpu.VMEM((cores, ranks, 2 * part, lanes), low),
            pltpu.VMEM(enc.shape, low),
            pltpu.VMEM(wkv.shape, low),
            pltpu.VMEM(ws.shape, low),
            pltpu.VMEM(x_all.shape, low),
            pltpu.VMEM((cores, ranks, fold, 2 * part), low),
            pltpu.VMEM((ranks, fold, 2 * part), low),
            pltpu.VMEM((ranks, fold, 2 * part), low),
            pltpu.VMEM((per_core, cores, fold, 2 * part), low),
            pltpu.VMEM(q.shape, low),
            pltpu.VMEM(q.shape, low),
            pltpu.VMEM(message, low),
            pltpu.VMEM(message, low),
            sums,
            sums,
            pltpu.VMEM((depth,) + dkv.shape, low),
            pltpu.VMEM(grads, low),
            pltpu.VMEM((rows, width), full),
            pltpu.VMEM((rows, width), low),
            pltpu.VMEM((places, high, 6 * head), low),
            pltpu.VMEM((places, high, 6 * head), low),
            pltpu.VMEM((depth, high, 3 * part), low),
            pltpu.VMEM((ranks, high, 3 * part), low),
        ]
        + along
        + [pltpu.VMEM(red1.shape, low)]
        + along
        + [pltpu.VMEM((places, HALF, 2 * head), low), pltpu.VMEM((places, HALF, 2 * head), low)]
        + [dma((places,)), dma((places,)), dma((4 + cores * ranks,)), dma((2,))]
        + send_scratch(places)
        + send_scratch(places)
        + [dma((2, depth)), dma((depth,))]
        + send_scratch(places)
        + send_scratch(ranks)
        + [dma((4, depth - 1)), dma((4, depth - 1))]
        + reduce_scratch(ranks, lanes, 2 * part, low)
        + reduce_scratch(ranks, lanes, 2 * part, low)[1:]
        + deal_scratch(cores, ranks, per_core)
        + deal_scratch(cores, ranks, per_core)
        + sum_scratch(ranks, lanes, rest, low)
        + vector_scratch(vec_shape, places, ranks),
        collective_id=6,
        in_spaces=[pltpu.VMEM] * 5 + [pl.ANY] + [pltpu.VMEM] * 12 + [pl.ANY] * 5,
        us=100,
    )


def column_body(
    dec_input,
    encoder_states,
    retrieved,
    self_wq,
    self_bq,
    self_wk,
    self_wv,
    self_bv,
    self_wo,
    self_bo,
    norm1_gain,
    norm1_bias,
    cross_wq,
    cross_bq,
    cross_wk,
    cross_wv,
    cross_bv,
    cross_wo,
    cross_bo,
    norm2_gain,
    norm2_bias,
    ffn_w1,
    ffn_b1,
    ffn_w2,
    ffn_b2,
    norm3_gain,
    norm3_bias,
    out_grad,
):
    low, full = jnp.bfloat16, jnp.float32
    core, seq, rank = here()
    cores, depth, ranks = lax.axis_size(ITEM), lax.axis_size(SEQ), lax.axis_size(TENSOR)
    per_core, _, width = dec_input.shape
    slots = retrieved.shape[2]
    part = self_wq.shape[1]
    head = part // 3
    places = cores * depth
    lanes = width // cores
    hidden = ffn_w1.shape[1]

    short = jnp.stack([self_bq, self_bv, cross_bq, cross_bv])
    vectors = jnp.concatenate([jnp.pad(short, ((0, 0), (0, hidden - part))), ffn_b1.reshape(1, hidden)], axis=0)
    vectors = jnp.pad(vectors, ((0, 3), (0, 0)))
    (
        x_all, enc, weights_kv, weights_self, weights_square, weights_in, weights_out,
        grad_mine, index, vectors, q1, k1, k1t, v1, o1_parts, lse1, o1,
        h1, y1, q2, k2, k2t, v2, o2_parts, lse2, o2,
    ) = front(
        dec_input, out_grad, encoder_states, retrieved, vectors,
        [cross_wk.T, cross_wv.T], [self_wq.T, self_wk.T, self_wv.T], [self_wo, cross_wq.T, cross_wo],
        ffn_w1, ffn_w2, [self_bo, norm1_gain, norm1_bias],
    )
    x_all = x_all.reshape(places, FULL, width)
    layer_out, do2, dh2, vec_mid, grad_mid = middle(
        per_core,
        o2,
        y1,
        grad_mine,
        weights_square,
        weights_in,
        weights_out,
        [
            cross_bo,
            norm2_gain,
            norm2_bias,
            vectors,
            ffn_b2,
            norm3_gain,
            norm3_bias,
        ],
    )
    layer_out = layer_out.reshape(per_core, cores * FULL, width)
    dq2, dkv2, bv, first_sum = attend_cross_back(q2, k2, k2t, v2, o2_parts, lse2, do2, grad_mid, hidden)
    input_grad, encoder_grad, total, squares, pairs, rest, gffn_w1, vectors = attend_self_back(
        per_core,
        dq2, dh2, h1, y1, o1, weights_square, norm1_gain,
        q1, k1, k1t, v1, o1_parts, lse1, dkv2, index, vec_mid, bv, first_sum, enc, weights_kv, weights_self, x_all, grad_mid,
    )
    (
        gself_wq, gself_wk, gself_wv, gself_wo, gcross_wq, gcross_wk, gcross_wv, gcross_wo, gffn_w2,
        gself_bq, gself_bv, gself_bo, gnorm1_gain, gnorm1_bias,
        gcross_bq, gcross_bv, gcross_bo, gnorm2_gain, gnorm2_bias, gffn_b1, gffn_b2, gnorm3_gain, gnorm3_bias,
    ) = outputs(head, width, total, squares, pairs, rest, vectors)
    input_grad = input_grad.reshape(per_core, cores * FULL, width)
    gffn_w2 = gffn_w2.T
    return (
        layer_out,
        input_grad,
        encoder_grad,
        gself_wq,
        gself_bq,
        gself_wk,
        gself_wv,
        gself_bv,
        gself_wo,
        gself_bo,
        gnorm1_gain,
        gnorm1_bias,
        gcross_wq,
        gcross_bq,
        gcross_wk,
        gcross_wv,
        gcross_bv,
        gcross_wo,
        gcross_bo,
        gnorm2_gain,
        gnorm2_bias,
        gffn_w1,
        gffn_b1,
        gffn_w2,
        gffn_b2,
        gnorm3_gain,
        gnorm3_bias,
    )


def solution(mesh):
    placed = (
        P(ITEM, SEQ, None),
        P(ITEM, SEQ, None),
        P(ITEM, TENSOR, None),
        P(None, TENSOR),
        P(TENSOR),
        P(None, TENSOR),
        P(None, TENSOR),
        P(TENSOR),
        P(TENSOR, None),
        P(),
        P(),
        P(),
        P(None, TENSOR),
        P(TENSOR),
        P(None, TENSOR),
        P(None, TENSOR),
        P(TENSOR),
        P(TENSOR, None),
        P(),
        P(),
        P(),
        P(None, TENSOR),
        P(TENSOR),
        P(TENSOR, None),
        P(),
        P(),
        P(),
        P(ITEM, SEQ, None),
    )
    reduced = (
        P(ITEM, SEQ, None),
        P(ITEM, SEQ, None),
        P(ITEM, SEQ, TENSOR),
        P((ITEM, SEQ), TENSOR),
        P(TENSOR),
        P((ITEM, SEQ), TENSOR),
        P((ITEM, SEQ), TENSOR),
        P(TENSOR),
        P(TENSOR, (ITEM, SEQ)),
        P(),
        P(),
        P(),
        P((ITEM, SEQ), TENSOR),
        P(TENSOR),
        P((ITEM, SEQ), TENSOR),
        P((ITEM, SEQ), TENSOR),
        P(TENSOR),
        P(TENSOR, (ITEM, SEQ)),
        P(),
        P(),
        P(),
        P((ITEM, SEQ), TENSOR),
        P(TENSOR),
        P(TENSOR, (ITEM, SEQ)),
        P(),
        P(),
        P(),
    )

    def layer(*arrays):
        chosen = column_body if column_plan_fits(mesh, arrays) else general_body
        return jax.shard_map(
            chosen,
            mesh=mesh,
            in_specs=placed,
            out_specs=reduced,
            check_vma=False,
        )(*arrays)

    return layer
```

```python
import functools

import jax
import jax.numpy as jnp
from jax import lax
from jax.experimental import pallas as pl
from jax.experimental.pallas import tpu as pltpu
from jax.sharding import PartitionSpec as P

EPS = 1e-05
SCALE = 0.125
NEG = -1e30
MESH = pl.DeviceIdType.MESH
ITEM, SEQ, TENSOR = "item", "seq", "tensor"


def matmul(first_op, second_op):
    return jnp.dot(first_op, second_op, preferred_element_type=jnp.float32)


def layer_norm(rows_in, norm_gain, norm_shift):
    center = rows_in - jnp.mean(rows_in, axis=-1, keepdims=True)
    spread = jnp.mean(center * center, axis=-1, keepdims=True)
    return center * lax.rsqrt(spread + EPS) * norm_gain + norm_shift


def exact_gelu(values_in):
    return jax.nn.gelu(values_in, approximate=False)


def tensor_total(partial_rows):
    return lax.psum(partial_rows, TENSOR)


def row_total(values_in):
    return jnp.sum(values_in.astype(jnp.float32), axis=(0, 1))


def softmax_stats(scores):
    row_max = jnp.max(scores, axis=-1, keepdims=True)
    shifted = jnp.exp(scores - row_max)
    row_sum = jnp.sum(shifted, axis=-1, keepdims=True)
    return (shifted / row_sum, row_max + jnp.log(row_sum))


def owned_pick(encoder_states, kv_weights, kv_bias, flat_index, owned_mask):
    kv_table = (
        jnp.einsum("ind,dhf->inhf", encoder_states, kv_weights, preferred_element_type=jnp.float32)
        + kv_bias
    ).astype(jnp.bfloat16)
    flat_table = kv_table.reshape(-1, kv_table.shape[-1])
    picked = jnp.take(flat_table, flat_index, axis=0)
    return jnp.where(owned_mask, picked.astype(jnp.float32), 0.0)


def general_body(
    dec_input,
    encoder_states,
    retrieved,
    self_wq,
    self_bq,
    self_wk,
    self_wv,
    self_bv,
    self_wo,
    self_bo,
    norm1_gain,
    norm1_bias,
    cross_wq,
    cross_bq,
    cross_wk,
    cross_wv,
    cross_bv,
    cross_wo,
    cross_bo,
    norm2_gain,
    norm2_bias,
    ffn_w1,
    ffn_b1,
    ffn_w2,
    ffn_b2,
    norm3_gain,
    norm3_bias,
    out_grad,
):
    item_count, dec_rows, model_width = dec_input.shape
    local_heads = retrieved.shape[1]
    enc_rows = encoder_states.shape[1]
    head_cols = self_wq.shape[1]
    head_size = head_cols // local_heads
    seq_devices = lax.axis_size(SEQ)
    seq_rank = lax.axis_index(SEQ)
    seq_length = dec_rows * seq_devices
    queries = ((matmul(dec_input, self_wq) + self_bq) * SCALE).astype(jnp.bfloat16)
    keys_local = matmul(dec_input, self_wk).astype(jnp.bfloat16)
    values_local = (matmul(dec_input, self_wv) + self_bv).astype(jnp.bfloat16)
    kv_all = lax.all_gather(
        jnp.concatenate([keys_local, values_local], axis=-1), SEQ, axis=1, tiled=True
    )
    keys_all = kv_all[..., :head_cols].reshape(item_count, seq_length, local_heads, head_size)
    values_all = kv_all[..., head_cols:].reshape(item_count, seq_length, local_heads, head_size)
    query_heads = queries.reshape(item_count, dec_rows, local_heads, head_size)
    query_pos = seq_rank * dec_rows + jnp.arange(dec_rows)
    causal = query_pos[:, None] >= jnp.arange(seq_length)[None, :]

    def self_scores():
        raw_scores = jnp.einsum(
            "irhe,ilhe->ihrl", query_heads, keys_all, preferred_element_type=jnp.float32
        )
        return jnp.where(causal, raw_scores, NEG)

    prob_self, lse_self = softmax_stats(self_scores())
    attended = (
        jnp.einsum(
            "ihrl,ilhe->irhe",
            prob_self.astype(jnp.bfloat16),
            values_all,
            preferred_element_type=jnp.float32,
        )
        .astype(jnp.bfloat16)
        .reshape(item_count, dec_rows, head_cols)
    )
    branch_one = tensor_total(matmul(attended, self_wo)) + self_bo
    hidden_one = dec_input.astype(jnp.float32) + branch_one
    normed_one = layer_norm(hidden_one, norm1_gain, norm1_bias).astype(jnp.bfloat16)
    queries_x = (
        ((matmul(normed_one, cross_wq) + cross_bq) * SCALE)
        .astype(jnp.bfloat16)
        .reshape(item_count, dec_rows, local_heads, head_size)
    )
    kv_weights = jnp.concatenate(
        [
            cross_wk.reshape(model_width, local_heads, head_size),
            cross_wv.reshape(model_width, local_heads, head_size),
        ],
        axis=-1,
    )
    kv_bias = jnp.concatenate(
        [
            jnp.zeros((local_heads, head_size), jnp.float32),
            cross_bv.reshape(local_heads, head_size),
        ],
        axis=-1,
    )
    local_row = retrieved - seq_rank * enc_rows
    owned_mask = ((local_row >= 0) & (local_row < enc_rows))[..., None]
    flat_index = (
        jnp.arange(item_count, dtype=jnp.int32)[:, None, None] * enc_rows
        + jnp.clip(local_row, 0, enc_rows - 1)
    ) * local_heads + jnp.arange(local_heads, dtype=jnp.int32)[None, :, None]
    retrieved_kv = lax.psum(
        owned_pick(encoder_states, kv_weights, kv_bias, flat_index, owned_mask).astype(
            jnp.bfloat16
        ),
        SEQ,
    )

    def cross_scores(kv_pair):
        return jnp.einsum(
            "irhe,ihke->ihrk",
            queries_x,
            kv_pair[..., :head_size],
            preferred_element_type=jnp.float32,
        )

    prob_cross, lse_cross = softmax_stats(cross_scores(retrieved_kv))
    attended_x = (
        jnp.einsum(
            "ihrk,ihke->irhe",
            prob_cross.astype(jnp.bfloat16),
            retrieved_kv[..., head_size:],
            preferred_element_type=jnp.float32,
        )
        .astype(jnp.bfloat16)
        .reshape(item_count, dec_rows, head_cols)
    )
    branch_two = tensor_total(matmul(attended_x, cross_wo)) + cross_bo
    hidden_two = normed_one.astype(jnp.float32) + branch_two
    normed_two = layer_norm(hidden_two, norm2_gain, norm2_bias).astype(jnp.bfloat16)
    pre_act = matmul(normed_two, ffn_w1) + ffn_b1
    activated = exact_gelu(pre_act).astype(jnp.bfloat16)
    branch_three = tensor_total(matmul(activated, ffn_w2)) + ffn_b2
    hidden_three = normed_two.astype(jnp.float32) + branch_three
    layer_out = layer_norm(hidden_three, norm3_gain, norm3_bias)
    _, back_three = jax.vjp(layer_norm, hidden_three, norm3_gain, norm3_bias)
    d_hidden3, gnorm3_gain, gnorm3_bias = back_three(out_grad.astype(jnp.float32))
    d_branch3 = d_hidden3.astype(jnp.bfloat16)
    gffn_b2 = row_total(d_branch3)
    gffn_w2 = jnp.einsum("irf,ird->fd", activated, d_branch3, preferred_element_type=jnp.float32)
    d_activated = jnp.einsum("ird,fd->irf", d_branch3, ffn_w2, preferred_element_type=jnp.float32)
    _, gelu_back = jax.vjp(exact_gelu, pre_act)
    d_pre = gelu_back(d_activated)[0].astype(jnp.bfloat16)
    gffn_b1 = row_total(d_pre)
    gffn_w1 = jnp.einsum("ird,irf->df", normed_two, d_pre, preferred_element_type=jnp.float32)
    d_normed2 = d_hidden3 + tensor_total(
        jnp.einsum("irf,df->ird", d_pre, ffn_w1, preferred_element_type=jnp.float32)
    )
    _, back_two = jax.vjp(layer_norm, hidden_two, norm2_gain, norm2_bias)
    d_hidden2, gnorm2_gain, gnorm2_bias = back_two(d_normed2)
    d_branch2 = d_hidden2.astype(jnp.bfloat16)
    gcross_bo = row_total(d_branch2)
    gcross_wo = jnp.einsum("irc,ird->cd", attended_x, d_branch2, preferred_element_type=jnp.float32)
    d_attended2 = (
        jnp.einsum("ird,cd->irc", d_branch2, cross_wo, preferred_element_type=jnp.float32)
        .astype(jnp.bfloat16)
        .reshape(item_count, dec_rows, local_heads, head_size)
    )
    kv_back = lax.psum(
        owned_pick(encoder_states, kv_weights, kv_bias, flat_index, owned_mask).astype(
            jnp.bfloat16
        ),
        SEQ,
    )
    redo_cross = jnp.exp(cross_scores(kv_back) - lse_cross)
    dprob_cross = jnp.einsum(
        "irhe,ihke->ihrk", d_attended2, kv_back[..., head_size:], preferred_element_type=jnp.float32
    )
    d_scores2 = (
        redo_cross * (dprob_cross - jnp.sum(dprob_cross * redo_cross, axis=-1, keepdims=True))
    ).astype(jnp.bfloat16)
    d_query2 = (
        jnp.einsum(
            "ihrk,ihke->irhe",
            d_scores2,
            kv_back[..., :head_size],
            preferred_element_type=jnp.float32,
        )
        .astype(jnp.bfloat16)
        .reshape(item_count, dec_rows, head_cols)
    )
    kv_grad_part = jnp.concatenate(
        [
            jnp.einsum("ihrk,irhe->ihke", d_scores2, queries_x, preferred_element_type=jnp.float32),
            jnp.einsum(
                "ihrk,irhe->ihke",
                redo_cross.astype(jnp.bfloat16),
                d_attended2,
                preferred_element_type=jnp.float32,
            ),
        ],
        axis=-1,
    )
    kv_grad = lax.psum(kv_grad_part, SEQ).astype(jnp.bfloat16)
    kv_owned = jnp.where(owned_mask, kv_grad.astype(jnp.float32), 0.0)
    table_grad = (
        jnp.zeros((item_count * enc_rows * local_heads, 2 * head_size), jnp.float32)
        .at[flat_index.reshape(-1)]
        .add(kv_owned.reshape(-1, 2 * head_size))
    )
    table_low = table_grad.astype(jnp.bfloat16).reshape(
        item_count, enc_rows, local_heads, 2 * head_size
    )
    grad_kv_weights = jnp.einsum(
        "ind,inhf->dhf", encoder_states, table_low, preferred_element_type=jnp.float32
    )
    gcross_wk = grad_kv_weights[..., :head_size].reshape(model_width, head_cols)
    gcross_wv = grad_kv_weights[..., head_size:].reshape(model_width, head_cols)
    gcross_bv = row_total(table_low[..., head_size:]).reshape(head_cols)
    encoder_part = jnp.einsum(
        "inhf,dhf->ind", table_low, kv_weights, preferred_element_type=jnp.float32
    )
    encoder_grad = lax.psum_scatter(encoder_part, TENSOR, scatter_dimension=2, tiled=True).astype(
        jnp.bfloat16
    )
    gcross_bq = row_total(d_query2) * SCALE
    gcross_wq = (
        jnp.einsum("ird,irc->dc", normed_one, d_query2, preferred_element_type=jnp.float32) * SCALE
    )
    d_normed1 = d_hidden2 + tensor_total(
        jnp.einsum("irc,dc->ird", d_query2, cross_wq, preferred_element_type=jnp.float32) * SCALE
    )
    _, back_one = jax.vjp(layer_norm, hidden_one, norm1_gain, norm1_bias)
    d_hidden1, gnorm1_gain, gnorm1_bias = back_one(d_normed1)
    d_branch1 = d_hidden1.astype(jnp.bfloat16)
    gself_bo = row_total(d_branch1)
    gself_wo = jnp.einsum("irc,ird->cd", attended, d_branch1, preferred_element_type=jnp.float32)
    d_attended1 = (
        jnp.einsum("ird,cd->irc", d_branch1, self_wo, preferred_element_type=jnp.float32)
        .astype(jnp.bfloat16)
        .reshape(item_count, dec_rows, local_heads, head_size)
    )
    redo_self = jnp.exp(self_scores() - lse_self)
    dprob_self = jnp.einsum(
        "irhe,ilhe->ihrl", d_attended1, values_all, preferred_element_type=jnp.float32
    )
    d_scores1 = (
        redo_self * (dprob_self - jnp.sum(dprob_self * redo_self, axis=-1, keepdims=True))
    ).astype(jnp.bfloat16)
    probs_low = redo_self.astype(jnp.bfloat16)
    d_query1 = (
        jnp.einsum("ihrl,ilhe->irhe", d_scores1, keys_all, preferred_element_type=jnp.float32)
        .astype(jnp.bfloat16)
        .reshape(item_count, dec_rows, head_cols)
    )
    row_count = dec_rows * lax.axis_size(SEQ)
    key_grad = jnp.einsum(
        "ihrl,irhe->lihe", d_scores1, query_heads, preferred_element_type=jnp.float32
    ).reshape(row_count, item_count, head_cols)
    value_grad = jnp.einsum(
        "ihrl,irhe->lihe", probs_low, d_attended1, preferred_element_type=jnp.float32
    ).reshape(row_count, item_count, head_cols)
    kv_self = lax.psum_scatter(
        jnp.concatenate([key_grad, value_grad], axis=-1), SEQ, scatter_dimension=0, tiled=True
    ).astype(jnp.bfloat16)
    kv_self = jnp.swapaxes(kv_self, 0, 1)
    d_key1 = kv_self[..., :head_cols]
    d_value1 = kv_self[..., head_cols:]
    gself_bq = row_total(d_query1) * SCALE
    gself_wq = (
        jnp.einsum("ird,irc->dc", dec_input, d_query1, preferred_element_type=jnp.float32) * SCALE
    )
    gself_wk = jnp.einsum("ird,irc->dc", dec_input, d_key1, preferred_element_type=jnp.float32)
    gself_wv = jnp.einsum("ird,irc->dc", dec_input, d_value1, preferred_element_type=jnp.float32)
    gself_bv = row_total(d_value1)
    input_part = (
        jnp.einsum("irc,dc->ird", d_query1, self_wq, preferred_element_type=jnp.float32) * SCALE
        + jnp.einsum("irc,dc->ird", d_key1, self_wk, preferred_element_type=jnp.float32)
        + jnp.einsum("irc,dc->ird", d_value1, self_wv, preferred_element_type=jnp.float32)
    )
    input_grad = (d_hidden1 + tensor_total(input_part)).astype(jnp.bfloat16)
    matrices = (
        lax.psum_scatter(gself_wq, (ITEM, SEQ), scatter_dimension=0, tiled=True),
        lax.psum_scatter(gself_wk, (ITEM, SEQ), scatter_dimension=0, tiled=True),
        lax.psum_scatter(gself_wv, (ITEM, SEQ), scatter_dimension=0, tiled=True),
        lax.psum_scatter(gself_wo, (ITEM, SEQ), scatter_dimension=1, tiled=True),
        lax.psum_scatter(gcross_wq, (ITEM, SEQ), scatter_dimension=0, tiled=True),
        lax.psum_scatter(gcross_wk, (ITEM, SEQ), scatter_dimension=0, tiled=True),
        lax.psum_scatter(gcross_wv, (ITEM, SEQ), scatter_dimension=0, tiled=True),
        lax.psum_scatter(gcross_wo, (ITEM, SEQ), scatter_dimension=1, tiled=True),
        lax.psum_scatter(gffn_w1, (ITEM, SEQ), scatter_dimension=0, tiled=True),
        lax.psum_scatter(gffn_w2, (ITEM, SEQ), scatter_dimension=1, tiled=True),
    )
    vectors = lax.psum(
        (
            gself_bq,
            gself_bv,
            gself_bo,
            gnorm1_gain,
            gnorm1_bias,
            gcross_bq,
            gcross_bv,
            gcross_bo,
            gnorm2_gain,
            gnorm2_bias,
            gffn_b1,
            gffn_b2,
            gnorm3_gain,
            gnorm3_bias,
        ),
        (ITEM, SEQ),
    )
    return (
        layer_out.astype(jnp.bfloat16),
        input_grad,
        encoder_grad,
        matrices[0],
        vectors[0],
        matrices[1],
        matrices[2],
        vectors[1],
        matrices[3],
        vectors[2],
        vectors[3],
        vectors[4],
        matrices[4],
        vectors[5],
        matrices[5],
        matrices[6],
        vectors[6],
        matrices[7],
        vectors[7],
        vectors[8],
        vectors[9],
        matrices[8],
        vectors[10],
        matrices[9],
        vectors[11],
        vectors[12],
        vectors[13],
    )


VMEM_LIMIT = 58 * 1024 * 1024
FULL = 256
HALF = 128
WIDE = FULL + HALF
PAIR = 2 * FULL


def column_plan_fits(mesh, arrays):
    items, cores = arrays[0].shape[0], mesh.shape[ITEM]
    ranks, depth = mesh.shape[TENSOR], mesh.shape[SEQ]
    heads = arrays[2].shape[1]
    rows = arrays[0].shape[1] // depth
    width = arrays[0].shape[2]
    return (
        cores == 2
        and ranks == 4
        and items == ranks
        and ranks == depth
        and heads == 3 * depth
        and width == 64 * heads
        and rows == cores * FULL
        and arrays[2].shape[2] % PAIR == 0
    )


def here():
    return lax.axis_index(ITEM), lax.axis_index(SEQ), lax.axis_index(TENSOR)


def call_kernel(kernel, name, outs, args, scratch=(), collective_id=None, in_spaces=None, out_space=None, us=10):
    single = isinstance(outs, tuple)
    listed = [outs] if single else list(outs)
    out_spaces = [pltpu.VMEM] * len(listed) if out_space is None else out_space
    spaces = [pltpu.VMEM] * len(args) if in_spaces is None else in_spaces
    params = dict(vmem_limit_bytes=VMEM_LIMIT)
    if collective_id is not None:
        params.update(collective_id=collective_id, has_side_effects=True)
    out = pl.pallas_call(
        kernel,
        out_shape=[jax.ShapeDtypeStruct(s, d) for s, d in listed],
        in_specs=[pl.BlockSpec(memory_space=s) for s in spaces],
        out_specs=[pl.BlockSpec(memory_space=s) for s in out_spaces],
        scratch_shapes=list(scratch),
        compiler_params=pltpu.CompilerParams(**params),
        cost_estimate=pl.CostEstimate(flops=us * 10**9, bytes_accessed=us * 3 * 10**6, transcendentals=0),
        name=name,
    )(*args)
    return out[0] if single else out


def greet(peers):
    gate = pltpu.get_barrier_semaphore()
    for peer in peers:
        pl.semaphore_signal(gate, inc=1, device_id=peer, device_id_type=MESH)


def meet(peers):
    greet(peers)
    pl.semaphore_wait(pltpu.get_barrier_semaphore(), len(peers))


def column_peer(place, cores, rank):
    return (lax.rem(place, cores), place // cores, rank)


def remote_copy(src, dst, send, recv, device):
    return pltpu.make_async_remote_copy(
        src_ref=src, dst_ref=dst, send_sem=send, recv_sem=recv, device_id=device, device_id_type=MESH
    )


def plane_peers(cores, ranks):
    core, seq, rank = here()
    peers = []
    for step in range(1, cores * ranks):
        place = lax.rem(rank * cores + core + step, cores * ranks)
        peers.append((lax.rem(place, cores), seq, place // cores))
    return peers


class Deal:
    def __init__(self, cores, ranks, per_core, source, all_ref, send_sem, recv_sem, own_sem):
        self.cores, self.ranks, self.per_core = cores, ranks, per_core
        self.source, self.all_ref = source, all_ref
        self.send_sem, self.recv_sem, self.own_sem = send_sem, recv_sem, own_sem
        self.core, self.seq, self.rank = here()
        self.home = self.rank // per_core
        self.local = lax.rem(self.rank, per_core)

    def send(self, step):
        target = lax.rem(self.rank + step, self.ranks)
        return remote_copy(
            self.source(target),
            self.all_ref.at[self.local, self.core],
            self.send_sem.at[step],
            self.recv_sem.at[self.local, self.core],
            (self.home, self.seq, target),
        )

    def keep(self):
        return pltpu.make_async_copy(self.source(self.rank), self.all_ref.at[self.local, self.core], self.own_sem)

    def start(self):
        for step in range(1, self.ranks):
            self.send(step).start()

        @pl.when(self.core != self.home)
        def _():
            self.send(0).start()

        @pl.when(self.core == self.home)
        def _():
            self.keep().start()

    def finish(self):
        for item in range(self.per_core):
            for half in range(self.cores):
                inside = (half == self.core) & (self.core * self.per_core + item == self.rank)

                @pl.when(jnp.logical_not(inside))
                def _():
                    remote_copy(
                        self.source(0),
                        self.all_ref.at[item, half],
                        self.send_sem.at[0],
                        self.recv_sem.at[item, half],
                        (1 - self.core, self.seq, self.rank),
                    ).wait_recv()

        for step in range(1, self.ranks):
            self.send(step).wait_send()

        @pl.when(self.core != self.home)
        def _():
            self.send(0).wait_send()

        @pl.when(self.core == self.home)
        def _():
            self.keep().wait()


def deal_scratch(cores, ranks, per_core):
    dma = pltpu.SemaphoreType.DMA
    return [dma((ranks,)), dma((per_core, cores)), dma]


class PlaneGather:
    def __init__(self, all_ref, give_send, give_recv, far_send, far_recv, pass_send, pass_recv):
        self.all_ref = all_ref
        self.give_send, self.give_recv = give_send, give_recv
        self.far_send, self.far_recv = far_send, far_recv
        self.pass_send, self.pass_recv = pass_send, pass_recv
        self.core, self.seq, self.rank = here()
        low, high = lax.rem(self.rank, 2), self.rank // 2
        self.near = (2 * high + 1 - low, 2 * (1 - high) + low)
        self.far = 2 * (1 - high) + 1 - low
        self.half = all_ref.shape[2] // 2
        self.peers = [(self.core, self.seq, rank) for rank in self.near]

    def give(self, way):
        block = self.all_ref.at[self.core, self.rank]
        return remote_copy(block, block, self.give_send.at[way], self.give_recv.at[way], self.peers[way])

    def far_part(self, way, origin):
        return self.all_ref.at[self.core, origin, pl.ds(way * self.half, self.half), :]

    def onward(self, way):
        block = self.far_part(way, self.near[way])
        return remote_copy(
            block, block, self.far_send.at[way], self.far_recv.at[way], self.peers[1 - way]
        )

    def side(self, slot, block):
        return remote_copy(
            block, block, self.pass_send.at[slot], self.pass_recv.at[slot], (1 - self.core, self.seq, self.rank)
        )

    def sides(self):
        near = [self.side(way, self.all_ref.at[self.core, self.near[way]]) for way in range(2)]
        return near + [self.side(2 + way, self.far_part(way, self.far)) for way in range(2)]

    def start(self):
        for way in range(2):
            self.give(way).start()

    def forward(self):
        sides = self.sides()
        for way in range(2):
            self.give(way).wait_recv()
            self.onward(way).start()
            sides[way].start()

    def arrive(self):
        sides = self.sides()
        for way in range(2):
            self.onward(way).wait_recv()
            sides[2 + way].start()
        for side in sides:
            side.wait_recv()

    def finish(self):
        for way in range(2):
            self.give(way).wait_send()
            self.onward(way).wait_send()
        for side in self.sides():
            side.wait_send()


def own_weights(refs, all_ref, sem):
    cores, _, _, lanes = all_ref.shape
    rank = lax.axis_index(TENSOR)
    copies, first = [], 0
    for n, ref in enumerate(refs):
        rows = ref.shape[0]
        for half in range(cores):
            copies.append(
                pltpu.make_async_copy(
                    ref.at[:, pl.ds(half * lanes, lanes)],
                    all_ref.at[half, rank, pl.ds(first, rows), :],
                    sem.at[n, half],
                )
            )
        first += rows
    return copies


def gather_scratch():
    return [pltpu.SemaphoreType.DMA((n,)) for n in (2, 2, 2, 2, 4, 4)]


class PlaneReduce:
    def __init__(self, ranks, grad_ref, got_ref, sum_ref, all_ref, swap_sem, send_sem, recv_sem):
        self.ranks, self.grad_ref, self.got_ref = ranks, grad_ref, got_ref
        self.sum_ref, self.all_ref = sum_ref, all_ref
        self.swap_sem, self.send_sem, self.recv_sem = swap_sem, send_sem, recv_sem
        self.core, self.seq, self.rank = here()
        self.peers = [(self.core, self.seq, lax.rem(self.rank + step, ranks)) for step in range(1, ranks)]

    def swap(self):
        return remote_copy(
            self.grad_ref.at[1 - self.core],
            self.got_ref,
            self.swap_sem.at[0],
            self.swap_sem.at[1],
            (1 - self.core, self.seq, self.rank),
        )

    def copy(self, step):
        peer = self.peers[step]
        return remote_copy(
            self.sum_ref.at[peer[2]], self.all_ref.at[self.rank], self.send_sem.at[step], self.recv_sem.at[step], peer
        )

    def start(self):
        self.swap().start()

    def middle(self):
        self.swap().wait()
        for rank in range(self.ranks):
            self.sum_ref[rank] = (
                self.grad_ref[self.core, rank].astype(jnp.float32) + self.got_ref[rank].astype(jnp.float32)
            ).astype(self.sum_ref.dtype)
        for step in range(self.ranks - 1):
            self.copy(step).start()

    def finish(self):
        for step in range(self.ranks - 1):
            self.copy(step).wait()
        total = self.sum_ref[self.rank].astype(jnp.float32)
        for step in range(1, self.ranks):
            total = total + self.all_ref[lax.rem(self.rank + step, self.ranks)].astype(jnp.float32)
        return total


class PlaneSum:
    def __init__(self, ranks, src_ref, first, all_ref, own_sem, send_sem, recv_sem):
        self.ranks, self.src_ref, self.first = ranks, src_ref, first
        self.all_ref, self.own_sem, self.send_sem, self.recv_sem = all_ref, own_sem, send_sem, recv_sem
        self.core, self.seq, self.rank = here()
        self.peers = [(self.core, self.seq, lax.rem(self.rank + step, ranks)) for step in range(1, ranks)]

    def block(self, rank):
        return self.src_ref.at[rank, :, pl.ds(self.first, self.all_ref.shape[2])]

    def own(self):
        return pltpu.make_async_copy(self.block(self.rank), self.all_ref.at[self.rank], self.own_sem)

    def copy(self, step):
        peer = self.peers[step]
        return remote_copy(
            self.block(peer[2]), self.all_ref.at[self.rank], self.send_sem.at[step], self.recv_sem.at[step], peer
        )

    def start(self):
        self.own().start()
        for step in range(self.ranks - 1):
            self.copy(step).start()

    def finish(self):
        self.own().wait()
        for step in range(self.ranks - 1):
            self.copy(step).wait()
        total = self.all_ref[0].astype(jnp.float32)
        for origin in range(1, self.ranks):
            total = total + self.all_ref[origin].astype(jnp.float32)
        return total


def sum_scratch(ranks, rows, columns, dtype):
    dma = pltpu.SemaphoreType.DMA
    return [pltpu.VMEM((ranks, rows, columns), dtype), dma, dma((ranks - 1,)), dma((ranks - 1,))]


def reduce_scratch(ranks, rows, columns, dtype):
    dma = pltpu.SemaphoreType.DMA
    block = pltpu.VMEM((ranks, rows, columns), dtype)
    return [block, block, block, dma((2,)), dma((ranks - 1,)), dma((ranks - 1,))]


def column_places(cores, depth):
    core, seq, _ = here()
    mine = seq * cores + core
    return mine, [lax.rem(mine + step, cores * depth) for step in range(1, cores * depth)]


class ColumnSend:
    def __init__(self, cores, depth, source_ref, all_ref, send_sem, recv_sem):
        self.cores, self.count = cores, cores * depth
        self.source_ref, self.all_ref = source_ref, all_ref
        self.send_sem, self.recv_sem = send_sem, recv_sem
        core, seq, self.rank = here()
        self.mine = seq * cores + core

    def copy(self, step):
        place = lax.rem(self.mine + 1 + step, self.count)
        return remote_copy(
            self.source_ref.at[place],
            self.all_ref.at[self.mine],
            self.send_sem.at[step],
            self.recv_sem.at[step],
            column_peer(place, self.cores, self.rank),
        )

    def wait_from(self, step):
        self.copy(step).wait_recv()

    def finish_sends(self):
        for step in range(self.count - 1):
            self.copy(step).wait_send()

    def finish(self):
        for step in range(self.count - 1):
            self.copy(step).wait()


def send_scratch(count):
    return [pltpu.SemaphoreType.DMA((count - 1,)), pltpu.SemaphoreType.DMA((count - 1,))]


class Chain:
    def __init__(self, depth, all_ref, send_sem, recv_sem):
        self.depth, self.all_ref = depth, all_ref
        self.send_sem, self.recv_sem = send_sem, recv_sem
        core, self.seq, rank = here()
        self.above = (core, lax.rem(self.seq + 1, depth), rank)
        self.below = (core, lax.rem(self.seq + depth - 1, depth), rank)

    def copy(self, block, way):
        part = self.all_ref.at[block]
        target = self.above if way == 0 else self.below
        return remote_copy(part, part, self.send_sem.at[way, block], self.recv_sem.at[block], target)

    def step(self, n):
        up, down = self.seq - n, self.seq + n

        @pl.when(up >= 0)
        def _():
            if n > 0:
                self.copy(up, 0).wait_recv()

            @pl.when(self.seq + 1 < self.depth)
            def _():
                self.copy(up, 0).start()

        @pl.when(down < self.depth)
        def _():
            if n > 0:
                self.copy(down, 1).wait_recv()

            @pl.when(self.seq > 0)
            def _():
                self.copy(down, 1).start()

    def finish(self):
        for n in range(self.depth):
            up, down = self.seq - n, self.seq + n

            @pl.when((up >= 0) & (self.seq + 1 < self.depth))
            def _():
                self.copy(up, 0).wait_send()

            @pl.when((down < self.depth) & (self.seq > 0))
            def _():
                self.copy(down, 1).wait_send()


class VectorSum:
    def __init__(self, cores, depth, ranks, out_ref, src_ref, col_ref, sum_ref, plane_ref, a_send, a_recv, b_send, b_recv, c_send, c_recv):
        self.cores, self.depth, self.ranks = cores, depth, ranks
        self.out_ref, self.src_ref, self.col_ref = out_ref, src_ref, col_ref
        self.sum_ref, self.plane_ref = sum_ref, plane_ref
        self.sems = ((a_send, a_recv), (b_send, b_recv), (c_send, c_recv))
        core, seq, self.rank = here()
        self.mine, self.places = column_places(cores, depth)
        self.peers = [(core, seq, lax.rem(self.rank + step, ranks)) for step in range(1, ranks)]

    def copies(self, stage):
        send, recv = self.sems[stage]
        if stage == 1:
            return [
                remote_copy(self.sum_ref, self.plane_ref.at[self.rank], send.at[n], recv.at[n], peer)
                for n, peer in enumerate(self.peers)
            ]
        src = self.src_ref if stage == 0 else self.out_ref
        dst = self.col_ref if stage == 0 else self.out_ref
        return [
            remote_copy(
                src.at[place if stage == 0 else self.mine],
                dst.at[self.mine],
                send.at[n],
                recv.at[n],
                column_peer(place, self.cores, self.rank),
            )
            for n, place in enumerate(self.places)
        ]

    def start(self, rows):
        height = self.src_ref.shape[1]
        for n, row in enumerate(rows):
            self.src_ref[n // height, n % height : n % height + 1, :] = row
        for copy in self.copies(0):
            copy.start()

    def second(self):
        for copy in self.copies(0):
            copy.wait()
        total = self.src_ref[self.mine]
        for place in self.places:
            total = total + self.col_ref[place]
        self.sum_ref[...] = total
        for copy in self.copies(1):
            copy.start()

    def third(self):
        for copy in self.copies(1):
            copy.wait()
        self.plane_ref[self.rank] = self.sum_ref[...]
        total = self.plane_ref[0]
        for origin in range(1, self.ranks):
            total = total + self.plane_ref[origin]
        self.out_ref[self.mine] = total
        for copy in self.copies(2):
            copy.start()

    def finish(self):
        for copy in self.copies(2):
            copy.wait()


def vector_scratch(shape, places, ranks):
    full = jnp.float32
    return [
        pltpu.VMEM(shape, full),
        pltpu.VMEM(shape, full),
        pltpu.VMEM(shape[1:], full),
        pltpu.VMEM((ranks,) + shape[1:], full),
    ] + [pltpu.SemaphoreType.DMA((n - 1,)) for n in (places, places, ranks, ranks, places, places)]


class ChainSum:
    def __init__(self, depth, src_ref, in_ref, send_sem, recv_sem):
        self.depth, self.src_ref, self.in_ref = depth, src_ref, in_ref
        self.send_sem, self.recv_sem = send_sem, recv_sem
        core, self.seq, rank = here()
        self.above = (core, lax.rem(self.seq + 1, depth), rank)
        self.below = (core, lax.rem(self.seq + depth - 1, depth), rank)

    def up(self, block):
        return remote_copy(
            self.src_ref.at[block], self.in_ref.at[block], self.send_sem.at[block], self.recv_sem.at[block], self.above
        )

    def down(self, block):
        slot = jnp.where(block == self.seq - 1, self.depth, block)
        return remote_copy(
            self.src_ref.at[block], self.in_ref.at[slot], self.send_sem.at[block], self.recv_sem.at[slot], self.below
        )

    def start(self):
        @pl.when(self.seq == 0)
        def _():
            for block in range(self.depth - 1, 0, -1):
                self.up(block).start()

        @pl.when(self.seq == self.depth - 1)
        def _():
            for block in range(self.depth - 1):
                self.down(block).start()

    def add(self, block):
        here_sum = self.src_ref[block].astype(jnp.float32) + self.in_ref[block].astype(jnp.float32)
        self.src_ref[block] = here_sum.astype(self.src_ref.dtype)

    def relay(self, n):
        high = self.depth - 1 - n + self.seq

        @pl.when((self.seq >= 1) & (self.seq <= n) & (high > self.seq))
        def _():
            self.up(high).wait_recv()
            self.add(high)
            self.up(high).start()

        low = n - (self.depth - 1 - self.seq)

        @pl.when((self.seq <= self.depth - 2) & (low >= 0) & (low < self.seq))
        def _():
            self.into(low).wait_recv()
            self.add(low)
            self.down(low).start()

    def into(self, block):
        return remote_copy(
            self.src_ref.at[0], self.in_ref.at[block], self.send_sem.at[0], self.recv_sem.at[block], self.below
        )

    def finish(self):
        @pl.when(self.seq > 0)
        def _():
            self.into(self.seq).wait_recv()
            self.add(self.seq)

        @pl.when(self.seq < self.depth - 1)
        def _():
            self.into(self.depth).wait_recv()

        for block in range(self.depth):

            @pl.when(block > self.seq)
            def _():
                self.up(block).wait_send()

            @pl.when(block < self.seq)
            def _():
                self.down(block).wait_send()

        total = self.src_ref[self.seq].astype(jnp.float32)
        last = jnp.where(self.seq < self.depth - 1, self.in_ref[self.depth].astype(jnp.float32), 0.0)
        return total + last


def chain_scratch(depth):
    dma = pltpu.SemaphoreType.DMA
    return [dma((depth,)), dma((depth + 1,))]


def front_kernel(
    sizes,
    x_ref, g_ref, m_ref, idx_ref, vec_ref, ck_ref, cv_ref, wq_ref, wk_ref, wv_ref, wo1_ref, wq2_ref, wo2_ref, w1_ref, w2_ref,
    bo_ref, gain_ref, shift_ref,
    xout_ref, eout_ref, wkvout_ref, wsout_ref, sqout_ref, w1out_ref, w2out_ref,
    gmine_ref, iall_ref, vall_ref, q_ref, k_ref, kt_ref, v_ref, o_ref, lse_ref, oall_ref,
    h_ref, y_ref, q2_ref, k2_ref, k2t_ref, v2_ref, o2_ref, lse2_ref, o2all_ref,
    xall_ref, enc_ref, wkv_ref, ws_ref, sq_ref, w1all_ref, w2all_ref, piece_ref, got_ref, vt_ref, s_ref,
    qsrc_ref, half_ref, other_ref, v2t_ref,
    load_kv, load_s, load_sq, load_w1, load_w2,
    swap_send, swap_recv, chain_send, chain_recv, side_send, side_recv, own_sem,
    idx_send, idx_recv, vec_send, vec_recv, kvsend, kvrecv, osend, orecv, out_sem,
    half_sem, qsend, qrecv, o2send, o2recv, *wsems
):
    cores, depth, ranks, per_core = sizes
    low = jnp.bfloat16
    core, seq, rank = here()
    home = rank // per_core
    local = lax.rem(rank, per_core)
    blocks = cores * depth
    head = q_ref.shape[1]
    sibling = (1 - core, seq, rank)
    above = (core, lax.rem(seq + 1, depth), rank)
    below = (core, lax.rem(seq + depth - 1, depth), rank)
    mine, places = column_places(cores, depth)
    gathers = [PlaneGather(ref, *wsems[6 * n : 6 * n + 6]) for n, ref in enumerate((wkv_ref, ws_ref, sq_ref, w1all_ref, w2all_ref))]
    gather_kv, gather_s, gather_sq, gather_w1, gather_w2 = gathers
    loads = [
        own_weights((ck_ref, cv_ref), wkv_ref, load_kv),
        own_weights((wq_ref, wk_ref, wv_ref), ws_ref, load_s),
        own_weights((wo1_ref, wq2_ref, wo2_ref), sq_ref, load_sq),
        own_weights((w1_ref,), w1all_ref, load_w1),
        own_weights((w2_ref,), w2all_ref, load_w2),
    ]
    for group in loads:
        for copy in group:
            copy.start()
    plane = plane_peers(cores, ranks)
    peers = plane + [column_peer(place, cores, rank) for place in places]
    meet(peers)

    def remote(src, dst, send, recv, device):
        return remote_copy(src, dst, send, recv, device)

    there = pl.ds((1 - core) * FULL, FULL)
    half_rows = pl.ds(core * FULL, FULL)
    swap_x = remote(x_ref.at[local, there], xall_ref.at[seq, 1 - core], swap_send.at[0], swap_recv.at[0], sibling)
    swap_g = remote(g_ref.at[local, there], gmine_ref, swap_send.at[1], swap_recv.at[1], sibling)
    swap_e = remote(m_ref.at[local], enc_ref, swap_send.at[2], swap_recv.at[2], sibling)
    own_x = pltpu.make_async_copy(x_ref.at[local, half_rows], xall_ref.at[seq, core], own_sem.at[3])
    own_g = pltpu.make_async_copy(g_ref.at[local, half_rows], gmine_ref, own_sem.at[4])
    own_e = pltpu.make_async_copy(m_ref.at[local], enc_ref, own_sem.at[5])

    @pl.when(core == home)
    def _():
        swap_x.start()
        own_x.start()

    for copy in loads[0]:
        copy.wait()
    gather_kv.start()

    def chain(block, target, way):
        part = xall_ref.at[block, core]
        return remote(part, part, chain_send.at[way, block], chain_recv.at[block], target)

    def aside(block):
        part = xall_ref.at[block, core]
        return remote(part, part, side_send.at[block], side_recv.at[block], sibling)

    def chain_step(step):
        up, down = seq - step, seq + step

        @pl.when(up >= 0)
        def _():
            if step > 0:
                chain(up, above, 0).wait_recv()

            @pl.when(seq + 1 < depth)
            def _():
                chain(up, above, 0).start()

            aside(up).start()

        @pl.when(down < depth)
        def _():
            if step > 0:
                chain(down, below, 1).wait_recv()

            @pl.when(seq > 0)
            def _():
                chain(down, below, 1).start()

            if step > 0:
                aside(down).start()

    @pl.when(core == home)
    def _():
        own_x.wait()

    @pl.when(core != home)
    def _():
        swap_x.wait_recv()

    chain_step(0)

    @pl.when(core == home)
    def _():
        swap_e.start()
        own_e.start()
        swap_g.start()
        own_g.start()

    def give_index(item, half):
        return remote(
            idx_ref.at[item], iall_ref.at[rank], idx_send.at[item, half], idx_recv.at[rank],
            (half, seq, core * per_core + item),
        )

    def is_me(item, half):
        return (half == core) & (core * per_core + item == rank)

    for item in range(per_core):
        for half in range(cores):

            @pl.when(jnp.logical_not(is_me(item, half)))
            def _():
                give_index(item, half).start()

            @pl.when(is_me(item, half))
            def _():
                own = pltpu.make_async_copy(idx_ref.at[item], iall_ref.at[rank], own_sem.at[0])
                own.start()
                own.wait()

    across = [(core, seq, lax.rem(rank + step, ranks)) for step in range(1, ranks)]
    vecs = [
        remote(vec_ref, vall_ref.at[rank], vec_send.at[step], vec_recv.at[step], peer)
        for step, peer in enumerate(across)
    ]
    for copy in vecs:
        copy.start()
    own_vec = pltpu.make_async_copy(vec_ref, vall_ref.at[rank], own_sem.at[1])
    own_vec.start()

    gather_kv.forward()
    for copy in loads[1]:
        copy.wait()
    gather_s.start()
    chain_step(1)
    for copy in vecs:
        copy.wait()
    own_vec.wait()

    @pl.when(core == home)
    def _():
        own_e.wait()

    @pl.when(core != home)
    def _():
        swap_e.wait_recv()

    for origin in range(ranks):

        @pl.when(jnp.logical_not((core == home) & (rank == origin)))
        def _():
            remote(
                idx_ref.at[0], iall_ref.at[origin], idx_send.at[0, 0], idx_recv.at[origin], sibling
            ).wait_recv()

    gather_kv.arrive()

    kv_sum = ChainSum(depth, piece_ref, got_ref, kvsend, kvrecv)

    def pick(group):
        retrieve(group, enc_ref, wkv_ref, vall_ref, iall_ref, piece_ref)

    pick(0)
    gather_s.forward()
    for copy in loads[2]:
        copy.wait()
    gather_sq.start()
    pick(1)
    chain_step(2)
    pick(2)
    pick(3)
    for step in range(3, depth):
        chain_step(step)
    kv_sum.start()
    gather_s.arrive()
    for block in range(depth):
        aside(block).wait_recv()

    outs = [
        pltpu.make_async_copy(src, dst, out_sem.at[n])
        for n, (src, dst) in enumerate(
            (
                (xall_ref, xout_ref),
                (enc_ref, eout_ref),
                (wkv_ref, wkvout_ref),
                (ws_ref, wsout_ref),
                (sq_ref, sqout_ref),
                (w1all_ref, w1out_ref),
                (w2all_ref, w2out_ref),
            )
        )
    ]
    for copy in outs[:4]:
        copy.start()

    w = jnp.concatenate([head_rows(ws_ref, seq, n, which, head) for n in range(3) for which in (2 * core, 1)], axis=0)
    rows = [vall_ref[seq, n : n + 1, :] for n in range(2)]
    bias = column_of(
        jnp.concatenate(
            [
                piece
                for row in rows
                for piece in (jnp.where(core == 0, row[:, :head], row[:, 2 * head : 3 * head]), row[:, head : 2 * head])
            ],
            axis=1,
        )
    )

    def project(block, carry):
        lanes = pl.ds(pl.multiple_of(block * FULL, FULL), FULL)
        flat = dot_nt(w, xall_ref[block // cores, lax.rem(block, cores)])
        q = ((flat[: 2 * head] + bias[: 2 * head]) * SCALE).astype(low)
        shared = jnp.where(core == 0, q[head:, :HALF], q[head:, HALF:])
        q_ref[block] = jnp.concatenate([q[:head], shared], axis=1)
        k = flat[2 * head : 4 * head].astype(low)
        v = (flat[4 * head :] + bias[2 * head :]).astype(low)
        kt_ref[:, lanes] = k
        vt_ref[:, lanes] = v
        k_ref[lanes, :] = k.T
        v_ref[lanes, :] = v.T
        return carry

    lax.fori_loop(0, blocks, project, 0)
    gather_sq.forward()
    for copy in loads[3]:
        copy.wait()
    gather_w1.start()
    kv_sum.relay(1)

    back = ColumnSend(cores, depth, o_ref, oall_ref, osend, orecv)

    def attend(block):
        out, lse = attend_block(block, True, core, blocks * FULL, q_ref[block], k_ref, vt_ref, s_ref)
        o_ref[block] = out
        lse_ref[block] = lse
        return out

    def step(n, carry):
        attend(lax.rem(mine + 1 + n, blocks))
        back.copy(n).start()
        return carry

    lax.fori_loop(0, 4, step, 0)
    kv_sum.relay(2)
    lax.fori_loop(4, 6, step, 0)
    gather_w1.forward()
    for copy in loads[4]:
        copy.wait()
    gather_w2.start()
    lax.fori_loop(6, blocks - 1, step, 0)
    oall_ref[mine] = attend(mine)
    gather_sq.arrive()
    outs[4].start()
    for n in range(blocks - 1):
        back.wait_from(n)

    part = 3 * head
    o1 = assembled(oall_ref, depth).T
    h1 = xall_ref[seq, core].astype(jnp.float32) + dot_nn(o1, late_square(sq_ref, 0, part)) + as_row(bo_ref)
    z, _ = centred_rows(h1)
    y1 = (z * as_row(gain_ref) + as_row(shift_ref)).astype(low)
    h_ref[...] = h1
    y_ref[...] = y1
    bias2 = column_of(jnp.concatenate([vall_ref[of, 2:3, :part] for of in range(ranks)], axis=1))
    q2t = ((dot_nt(late_square(sq_ref, 1, part), y1) + bias2) * SCALE).astype(low)
    dispersed(q2t, qsrc_ref, depth)
    ask = ColumnSend(cores, depth, qsrc_ref, q2_ref, qsend, qrecv)
    for n in range(blocks - 1):
        ask.copy(n).start()
    q2_ref[mine] = qsrc_ref[mine]

    slots = k2_ref.shape[0]
    total = kv_sum.finish().astype(low)
    half_ref[...] = total[:, slots:]
    swap = remote(half_ref, other_ref, half_sem.at[0], half_sem.at[1], sibling)
    swap.start()
    gather_w1.arrive()
    outs[5].start()
    swap.wait()
    half, other = half_ref[...], other_ref[...]
    shared = jnp.concatenate([jnp.where(core == 0, half, other), jnp.where(core == 0, other, half)], axis=1)
    kt = jnp.concatenate([total[:head, :slots], shared[:head]], axis=0)
    vt = jnp.concatenate([total[head:, :slots], shared[head:]], axis=0)
    k2t_ref[...] = kt
    v2t_ref[...] = vt
    k2_ref[...] = kt.T
    v2_ref[...] = vt.T

    back2 = ColumnSend(cores, depth, o2_ref, o2all_ref, o2send, o2recv)

    def attend2(block):
        out, lse = attend_block(block, False, core, slots, q2_ref[block], k2_ref, v2t_ref, s_ref)
        o2_ref[block] = out
        lse2_ref[block] = lse
        return out

    o2all_ref[mine] = attend2(mine)

    def step2(n, carry):
        ask.wait_from(n)
        attend2(lax.rem(mine + blocks - 1 - n, blocks))
        back2.copy(blocks - 2 - n).start()
        return carry

    lax.fori_loop(0, 2, step2, 0)
    gather_w2.forward()
    lax.fori_loop(2, 5, step2, 0)
    gather_w2.arrive()
    outs[6].start()
    lax.fori_loop(5, blocks - 1, step2, 0)

    for n in range(depth):
        up, down = seq - n, seq + n

        @pl.when((up >= 0) & (seq + 1 < depth))
        def _():
            chain(up, above, 0).wait_send()

        @pl.when((down < depth) & (seq > 0))
        def _():
            chain(down, below, 1).wait_send()

        aside(n).wait_send()

    @pl.when(core == home)
    def _():
        for copy in (swap_x, swap_g, swap_e):
            copy.wait_send()
        own_g.wait()

    @pl.when(core != home)
    def _():
        swap_g.wait_recv()

    for item in range(per_core):
        for half in range(cores):

            @pl.when(jnp.logical_not(is_me(item, half)))
            def _():
                give_index(item, half).wait_send()

    ask.finish_sends()
    back.finish_sends()
    back2.finish()
    for gather in gathers:
        gather.finish()
    for copy in outs:
        copy.wait()


def front(dec_input, out_grad, encoder_states, retrieved, vectors, kv, selfs, squares, w1, w2, rows1):
    cores, depth, ranks = lax.axis_size(ITEM), lax.axis_size(SEQ), lax.axis_size(TENSOR)
    per_core, _, width = dec_input.shape
    enc_rows = encoder_states.shape[1]
    slots = retrieved.shape[2]
    part = kv[0].shape[0]
    head = part // 3
    places = cores * depth
    rows = places * FULL
    lanes = width // cores
    low, full = jnp.bfloat16, jnp.float32
    dma = pltpu.SemaphoreType.DMA

    def all_of(weights):
        return (cores, ranks, sum(w.shape[0] for w in weights), lanes)

    big = [(depth, cores, FULL, width), (enc_rows, width)] + [all_of(w) for w in (kv, selfs, squares, [w1], [w2])]
    kv_shape = (2 * head, slots + slots // 2)
    parts = (places, head, WIDE)
    small = [
        ((FULL, width), low),
        ((ranks,) + retrieved.shape[1:], retrieved.dtype),
        ((ranks,) + vectors.shape, vectors.dtype),
        ((places, head, WIDE), low),
        ((rows, 2 * head), low),
        ((2 * head, rows), low),
        ((rows, 2 * head), low),
        ((places, head, WIDE), low),
        ((places, 1, WIDE), full),
        (parts, low),
        ((FULL, width), full),
        ((FULL, width), low),
        (parts, low),
        ((slots, 2 * head), low),
        ((2 * head, slots), low),
        ((slots, 2 * head), low),
        (parts, low),
        ((places, 1, WIDE), full),
        (parts, low),
    ]
    return call_kernel(
        functools.partial(front_kernel, (cores, depth, ranks, per_core)),
        "front",
        [(shape, low) for shape in big] + small,
        [dec_input, out_grad, encoder_states, retrieved, vectors, *kv, *selfs, *squares, w1, w2, *rows1],
        scratch=[pltpu.VMEM(shape, low) for shape in big]
        + [
            pltpu.VMEM((depth,) + kv_shape, low),
            pltpu.VMEM((depth + 1,) + kv_shape, low),
            pltpu.VMEM((2 * head, rows), low),
            pltpu.VMEM((rows, WIDE), full),
            pltpu.VMEM(parts, low),
            pltpu.VMEM((2 * head, slots // 2), low),
            pltpu.VMEM((2 * head, slots // 2), low),
            pltpu.VMEM((2 * head, slots), low),
            dma((2, cores)),
            dma((3, cores)),
            dma((3, cores)),
            dma((1, cores)),
            dma((1, cores)),
            dma((3,)),
            dma((3,)),
            dma((2, depth)),
            dma((depth,)),
            dma((depth,)),
            dma((depth,)),
            dma((6,)),
            dma((per_core, cores)),
            dma((ranks,)),
        ]
        + send_scratch(ranks)
        + chain_scratch(depth)
        + send_scratch(places)
        + [dma((7,)), dma((2,))]
        + send_scratch(places)
        + send_scratch(places)
        + gather_scratch() * 5,
        collective_id=1,
        in_spaces=[pl.ANY] * 15 + [pltpu.VMEM] * 3,
        out_space=[pl.ANY] * 7 + [pltpu.VMEM] * len(small),
        us=90,
    )


def dot_nn(first_op, second_op):
    return lax.dot_general(first_op, second_op, (((1,), (0,)), ((), ())), preferred_element_type=jnp.float32)


def dot_nt(first_op, second_op):
    return lax.dot_general(first_op, second_op, (((1,), (1,)), ((), ())), preferred_element_type=jnp.float32)


def head_rows(ref, group, matrix, head_index, head):
    start = pl.multiple_of(matrix * 3 * head + head_index * head, head)
    rows = pl.ds(start, head)
    return jnp.concatenate([ref[half, group, rows, :] for half in range(ref.shape[0])], axis=1)


def as_row(ref):
    return ref[...].reshape(1, ref.shape[0])


def column_of(row):
    return jnp.broadcast_to(row, (8, row.shape[1])).T[:, :1]


def kv_rows(w_ref, group, head_index, head):
    return jnp.concatenate(
        [head_rows(w_ref, group, 0, head_index, head), head_rows(w_ref, group, 1, head_index, head)], axis=0
    )


def retrieve(group, enc_ref, w_ref, vec_ref, idx_ref, out_ref):
    core, seq, _ = here()
    enc_rows = enc_ref.shape[0]
    slots = idx_ref.shape[2]
    head = out_ref.shape[1] // 2
    low = jnp.bfloat16
    tall = enc_rows // 3

    def picked(table, index):
        total = jnp.zeros((table.shape[0], index.shape[1]), jnp.float32)
        for part in range(3):
            place = lax.broadcasted_iota(jnp.int32, (tall, index.shape[1]), 0) + (part * tall + seq * enc_rows)
            hot = jnp.where(place == index, 1.0, 0.0).astype(low)
            total = total + dot_nn(table[:, part * tall : (part + 1) * tall], hot)
        return total.astype(low)

    w = jnp.concatenate([kv_rows(w_ref, group, 2 * core, head), kv_rows(w_ref, group, 1, head)], axis=0)
    row = vec_ref[group, 3:4, :]
    blank = jnp.zeros((1, head), jnp.float32)
    first = jnp.where(core == 0, row[:, :head], row[:, 2 * head : 3 * head])
    bias = column_of(jnp.concatenate([blank, first, blank, row[:, head : 2 * head]], axis=1))
    table = (dot_nt(w, enc_ref[...]) + bias).astype(low)
    whole = idx_ref[group, pl.ds(2 * core, 1), :]
    shared = idx_ref[group, pl.ds(1, 1), :]
    half = jnp.where(core == 0, shared[:, : slots // 2], shared[:, slots // 2 :])
    out_ref[group] = jnp.concatenate([picked(table[: 2 * head], whole), picked(table[2 * head :], half)], axis=1)


def assembled(parts_ref, depth, columns=None):
    pieces = []
    for group in range(depth):
        first, second = parts_ref[2 * group], parts_ref[2 * group + 1]
        pieces += [
            first[:, :FULL],
            jnp.concatenate([first[:, FULL:WIDE], second[:, FULL:WIDE]], axis=1),
            second[:, :FULL],
        ]
    return jnp.concatenate(pieces, axis=0)


def dispersed(rows, parts_ref, depth):
    head = rows.shape[0] // (3 * depth)
    for group in range(depth):
        a = rows[3 * group * head : (3 * group + 1) * head]
        b = rows[(3 * group + 1) * head : (3 * group + 2) * head]
        c = rows[(3 * group + 2) * head : (3 * group + 3) * head]
        parts_ref[2 * group] = jnp.concatenate([a, b[:, :HALF]], axis=1)
        parts_ref[2 * group + 1] = jnp.concatenate([c, b[:, HALF:]], axis=1)


def late_square(ref, matrix, rows):
    cores, ranks = ref.shape[0], ref.shape[1]
    return jnp.concatenate(
        [
            jnp.concatenate([ref[half, rank, matrix * rows : (matrix + 1) * rows, :] for half in range(cores)], axis=1)
            for rank in range(ranks)
        ],
        axis=0,
    )


def centred_rows(h):
    center = h - jnp.mean(h, axis=-1, keepdims=True)
    spread = lax.rsqrt(jnp.mean(center * center, axis=-1, keepdims=True) + EPS)
    return center * spread, spread


def norm_back(z, spread, dy, gain):
    dz = dy * gain
    dh = spread * (
        dz - jnp.mean(dz, axis=-1, keepdims=True) - z * jnp.mean(dz * z, axis=-1, keepdims=True)
    )
    return dh, jnp.sum(dy * z, axis=0, keepdims=True), jnp.sum(dy, axis=0, keepdims=True)


def middle_kernel(
    cores, depth, ranks, per_core, part,
    o_ref, y1_ref, g_ref, w_ref, w1_in, w2_in, bo_ref, gain2_ref, shift2_ref, b1_ref, b2_ref, gain3_ref, shift3_ref,
    layer_ref, do_ref, dh2_ref, vec_ref, grad_ref,
    w1_ref, w2_ref, slope_ref, a_ref, df_ref, out_ref, dosrc_ref, turn_ref, give_ref, got_ref,
    ffn_sem, grad_sem, dosend, dorecv, *deal_sems
):
    low = jnp.bfloat16
    core, seq, rank = here()
    count = cores * depth
    mine, places = column_places(cores, depth)
    peers = [column_peer(place, cores, rank) for place in places]
    peers += [(half, seq, lax.rem(rank + step, ranks)) for step in range(1, ranks) for half in range(cores)]
    greet(peers)
    width = y1_ref.shape[1]
    lanes = width // cores
    loads = [
        pltpu.make_async_copy(src, dst, ffn_sem.at[n]) for n, (src, dst) in enumerate(((w1_in, w1_ref), (w2_in, w2_ref)))
    ]
    for load in loads:
        load.start()
    o2t = assembled(o_ref, depth)
    wo2 = late_square(w_ref, 2, part)
    h2 = y1_ref[...].astype(jnp.float32) + dot_nn(o2t.T, wo2) + as_row(bo_ref)
    z2, spread2 = centred_rows(h2)
    y2 = (z2 * as_row(gain2_ref) + as_row(shift2_ref)).astype(low)

    def hidden_in(of, half):
        return w1_ref[half, of]

    def hidden_out(of):
        return jnp.concatenate([w2_ref[half, of] for half in range(cores)], axis=1)

    root = 0.7071067811865476
    h3 = y2.astype(jnp.float32) + as_row(b2_ref)
    for load in loads:
        load.wait()
    for of in range(ranks):
        f = jnp.concatenate([dot_nn(y2, hidden_in(of, half)) for half in range(cores)], axis=1) + b1_ref[of, 4:5, :]
        cdf = 0.5 * (1.0 + lax.erf(f * root))
        a = (f * cdf).astype(low)
        slope_ref[of] = cdf + f * (0.3989422804014327 * jnp.exp(-0.5 * f * f))
        a_ref[of] = a
        h3 = h3 + dot_nn(a, hidden_out(of))
    z3, spread3 = centred_rows(h3)
    out_ref[...] = (z3 * as_row(gain3_ref) + as_row(shift3_ref)).astype(low)
    pl.semaphore_wait(pltpu.get_barrier_semaphore(), len(peers))
    deal = Deal(cores, ranks, per_core, lambda target: out_ref, layer_ref, *deal_sems)
    deal.start()

    dh3, gg3, gs3 = norm_back(z3, spread3, g_ref[...].astype(jnp.float32), as_row(gain3_ref))
    e3 = dh3.astype(low)
    dy2 = dh3
    for of in range(ranks):
        df = (dot_nt(e3, hidden_out(of)) * slope_ref[of]).astype(low)
        df_ref[of] = df
        for half in range(cores):
            dy2 = dy2 + dot_nt(df[:, half * lanes : (half + 1) * lanes], hidden_in(of, half))
    dh2, gg2, gs2 = norm_back(z2, spread2, dy2, as_row(gain2_ref))
    e2 = dh2.astype(low)
    dispersed(dot_nt(wo2, e2).astype(low), dosrc_ref, depth)
    ask = ColumnSend(cores, depth, dosrc_ref, do_ref, dosend, dorecv)
    for step in range(count - 1):
        ask.copy(step).start()
    do_ref[mine] = dosrc_ref[mine]

    dh2_ref[...] = dh2
    vec_ref[0:1] = gg3
    vec_ref[1:2] = gs3
    vec_ref[2:3] = jnp.sum(e3.astype(jnp.float32), axis=0, keepdims=True)
    vec_ref[3:4] = gg2
    vec_ref[4:5] = gs2
    vec_ref[5:6] = jnp.sum(e2.astype(jnp.float32), axis=0, keepdims=True)
    turn_ref[0] = y2.T
    turn_ref[1] = e3.T
    turn_ref[2] = e2.T
    pad = jnp.zeros((-part % 128, FULL), low)

    def grad_of(of, half):
        rows = pl.ds(pl.multiple_of(half * lanes, lanes), lanes)
        o2_part = jnp.concatenate([o2t[of * part : (of + 1) * part], pad], axis=0)
        return (
            dot_nn(turn_ref[0, rows, :], df_ref[of]),
            dot_nn(turn_ref[1, rows, :], a_ref[of]),
            dot_nt(turn_ref[2, rows, :], o2_part),
        )

    spans = (slice(0, width), slice(width, 2 * width), slice(2 * width, None))

    def swap(of):
        return remote_copy(
            give_ref.at[of], got_ref.at[of], grad_sem.at[0, of], grad_sem.at[1, of], (1 - core, seq, rank)
        )

    for of in range(ranks):
        vec_ref[6 + of : 7 + of] = jnp.sum(df_ref[of].astype(jnp.float32), axis=0, keepdims=True)
        for span, grad in zip(spans, grad_of(of, 1 - core)):
            give_ref[of, :, span] = grad.astype(low)
        swap(of).start()
    for of in range(ranks):
        grads = grad_of(of, core)
        swap(of).wait_recv()
        for span, grad in zip(spans, grads):
            grad_ref[of, :, span] = (grad + got_ref[of, :, span].astype(jnp.float32)).astype(low)
    for of in range(ranks):
        swap(of).wait_send()
    ask.finish()
    deal.finish()


def middle(per_core, o2, y1, grad_mine, squares, w1, w2, vectors):
    cores, depth, ranks = lax.axis_size(ITEM), lax.axis_size(SEQ), lax.axis_size(TENSOR)
    places, head, _ = o2.shape
    rows, width = y1.shape
    part, lanes, hidden = 3 * head, width // cores, width
    low, full = jnp.bfloat16, jnp.float32
    columns = 2 * hidden + part + (-part % 128)
    return call_kernel(
        functools.partial(middle_kernel, cores, depth, ranks, per_core, part),
        "middle",
        [
            ((per_core, cores, rows, width), low),
            (o2.shape, low),
            ((rows, width), full),
            ((6 + ranks, width), full),
            ((ranks, lanes, columns), low),
        ],
        [o2, y1, grad_mine, squares, w1, w2, *vectors],
        scratch=[
            pltpu.VMEM(w1.shape, low),
            pltpu.VMEM(w2.shape, low),
            pltpu.VMEM((ranks, rows, hidden), full),
            pltpu.VMEM((ranks, rows, hidden), low),
            pltpu.VMEM((ranks, rows, hidden), low),
            pltpu.VMEM((rows, width), low),
            pltpu.VMEM(o2.shape, low),
            pltpu.VMEM((3, width, rows), low),
            pltpu.VMEM((ranks, lanes, columns), low),
            pltpu.VMEM((ranks, lanes, columns), low),
            pltpu.SemaphoreType.DMA((2,)),
            pltpu.SemaphoreType.DMA((2, ranks)),
        ]
        + send_scratch(places)
        + deal_scratch(cores, ranks, per_core),
        collective_id=4,
        in_spaces=[pltpu.VMEM] * 4 + [pl.ANY] * 2 + [pltpu.VMEM] * len(vectors),
        us=22,
    )


def encoder_back(ranks, head, enc_ref, w_ref, idx_ref, dkv_ref, part_ref, grad_ref):
    core, seq, _ = here()
    low = jnp.bfloat16
    enc_rows, width = enc_ref.shape
    slots = idx_ref.shape[2]
    cores = w_ref.shape[0]
    lanes = width // cores
    part = width // ranks
    fold = enc_rows // (2 * cores)
    enc_t = enc_ref[...].T

    tables = []
    rows_w = []
    for group in range(ranks):
        heads = []
        shared = idx_ref[group, pl.ds(1, 1), :]
        shared = jnp.where(core == 0, shared[:, : slots // 2], shared[:, slots // 2 :])
        for which, index, rows in (
            (2 * core, idx_ref[group, pl.ds(2 * core, 1), :], slice(0, slots)),
            (1, shared, slice(slots, slots + slots // 2)),
        ):
            pieces = []
            for third in range(3):
                tall = enc_rows // 3
                place = lax.broadcasted_iota(jnp.int32, (tall, index.shape[1]), 0) + (third * tall + seq * enc_rows)
                hot = jnp.where(place == index, 1.0, 0.0).astype(low)
                pieces.append(dot_nn(hot, dkv_ref[group, rows, :]).astype(low))
            table = jnp.concatenate(pieces, axis=0)
            heads.append(table)
            tables.append(table)
            rows_w.append(kv_rows(w_ref, group, which, head))
        both = jnp.concatenate(heads, axis=1)
        grad = dot_nn(enc_t, both).astype(low)
        whole, shared = grad[:, : 2 * head], grad[:, 2 * head :]
        blank = jnp.zeros_like(whole)
        left = jnp.where(core == 0, whole, blank)
        right = jnp.where(core == 0, blank, whole)
        for half in range(cores):
            rows = slice(half * lanes, (half + 1) * lanes)
            grad_ref[half, group] = jnp.concatenate([left[rows], shared[rows], right[rows]], axis=1)
    table = jnp.concatenate(tables, axis=1)
    w = jnp.concatenate(rows_w, axis=0)
    for rank in range(ranks):
        cols = w[:, rank * part : (rank + 1) * part]
        flat = dot_nn(table, cols).astype(low)
        for half in range(cores):
            low_rows = flat[2 * half * fold : (2 * half + 1) * fold]
            high_rows = flat[(2 * half + 1) * fold : (2 * half + 2) * fold]
            part_ref[half, rank] = jnp.concatenate([low_rows, high_rows], axis=1)


def input_rows(depth, parts_ref, dh1_ref, w_ref):
    low = jnp.bfloat16
    part = 3 * parts_ref.shape[1]
    dqt = assembled(parts_ref, depth)
    stack_k, stack_v = [], []
    for group in range(depth):
        first, second = parts_ref[2 * group], parts_ref[2 * group + 1]
        for n, stack in ((0, stack_k), (1, stack_v)):
            whole = slice(WIDE + n * FULL, WIDE + (n + 1) * FULL)
            shared = slice(WIDE + 2 * FULL + n * HALF, WIDE + 2 * FULL + (n + 1) * HALF)
            both = jnp.concatenate([first[:, shared], second[:, shared]], axis=1)
            stack += [first[:, whole], both, second[:, whole]]
    dx = dh1_ref[...] + dot_nn(dqt.T, late_square(w_ref, 0, part)) * SCALE
    dx = dx + dot_nn(jnp.concatenate(stack_k, axis=0).T, late_square(w_ref, 1, part))
    dx = dx + dot_nn(jnp.concatenate(stack_v, axis=0).T, late_square(w_ref, 2, part))
    return dx.astype(low)


def merge_heads(depth, head, column_ref, group_ref):
    low = group_ref.dtype
    for group in range(depth):
        first, second = column_ref[2 * group], column_ref[2 * group + 1]
        pieces = []
        for n in range(3):
            whole = slice(2 * n * head, (2 * n + 1) * head)
            shared = slice((2 * n + 1) * head, (2 * n + 2) * head)
            both = (first[:, shared].astype(jnp.float32) + second[:, shared].astype(jnp.float32)).astype(low)
            pieces += [first[:, whole], both, second[:, whole]]
        group_ref[group] = jnp.concatenate(pieces, axis=1)


def outputs_kernel(
    ranks, part, head,
    total_ref, squares_ref, pairs_ref, rest_ref, vec_ref,
    wq1_ref, wk1_ref, wv1_ref, wo1_ref, wq2_ref, wk2_ref, wv2_ref, wo2_ref, w2_ref,
    bq1_ref, bv1_ref, bo1_ref, g1_ref, s1_ref, bq2_ref, bv2_ref, bo2_ref, g2_ref, s2_ref, b1_ref, b2_ref, g3_ref, s3_ref,
):
    rank = lax.axis_index(TENSOR)
    height = vec_ref.shape[1]

    def line(n):
        return vec_ref[n // height, n % height : n % height + 1, :]

    def whole(row):
        return row.reshape(row.shape[1])

    def rank_part(row):
        found = row[:, :part]
        for other in range(1, ranks):
            found = jnp.where(rank == other, row[:, other * part : (other + 1) * part], found)
        return whole(found)

    for ref, n in ((g3_ref, 0), (s3_ref, 1), (b2_ref, 2), (g2_ref, 3), (s2_ref, 4), (bo2_ref, 5)):
        ref[...] = whole(line(n))
    hidden = line(6)
    for other in range(1, ranks):
        hidden = jnp.where(rank == other, line(6 + other), hidden)
    b1_ref[...] = whole(hidden)
    for ref, n in ((g1_ref, 0), (s1_ref, 1), (bo1_ref, 2)):
        ref[...] = whole(line(6 + ranks + n))
    bq2_ref[...] = rank_part(line(9 + ranks))
    bv2_ref[...] = rank_part(line(10 + ranks))
    squares = squares_ref[...]
    wq2_ref[...] = squares[:, :part] * SCALE
    wo1_ref[...] = squares[:, part:].T
    pairs = pairs_ref[...]
    for n, ref in enumerate((wk2_ref, wv2_ref)):
        ref[...] = jnp.concatenate(
            [pairs[:, (2 * k + n) * head : (2 * k + n + 1) * head] for k in range(3)], axis=1
        )
    span = w2_ref.shape[1]
    w2_ref[...] = rest_ref[:, :span]
    wo2_ref[...] = rest_ref[:, span : span + part].T
    total = total_ref[...]
    rows = wq1_ref.shape[0]
    wq1_ref[...] = total[:rows, :part] * SCALE
    wk1_ref[...] = total[:rows, part : 2 * part]
    wv1_ref[...] = total[:rows, 2 * part :]
    bq1_ref[...] = whole(total[rows : rows + 1, :part] * SCALE)
    bv1_ref[...] = whole(total[rows : rows + 1, 2 * part :])


def outputs(head, width, total, squares, pairs, rest, vectors):
    ranks = lax.axis_size(TENSOR)
    few, part, full = squares.shape[0], 3 * head, jnp.float32
    square, turned = ((few, part), full), ((part, few), full)
    long, short = ((width,), full), ((part,), full)
    return call_kernel(
        functools.partial(outputs_kernel, ranks, part, head),
        "outputs",
        [square, square, square, turned, square, square, square, turned, ((few, width), full)]
        + [short, short, long, long, long, short, short, long, long, long, long, long, long, long],
        [total, squares, pairs, rest, vectors],
        us=2,
    )


def self_grads(blocks, cores, places, x_in, x_ref, x_sem, g_ref, out_ref):
    core, seq, rank = here()
    low = jnp.bfloat16
    head = g_ref.shape[1]
    width = x_ref.shape[2]
    rows = width // places

    def load(block):
        return pltpu.make_async_copy(x_in.at[block], x_ref.at[block % 2], x_sem.at[block % 2])

    load(0).start()
    load(1).start()
    total = jnp.zeros((width, 6 * head), jnp.float32)
    sums = jnp.zeros((16, 6 * head), jnp.float32)
    ones = jnp.ones((16, FULL), low)
    zero = jnp.zeros((head, HALF), low)
    for block in range(blocks):
        g = g_ref[block]

        def own_half(first):
            part = g[:, first : first + HALF]
            return jnp.where(
                core == 0, jnp.concatenate([part, zero], axis=1), jnp.concatenate([zero, part], axis=1)
            )

        whole = WIDE + 2 * FULL
        flat = jnp.concatenate(
            [
                g[:, :FULL],
                own_half(FULL),
                g[:, WIDE : WIDE + FULL],
                own_half(whole),
                g[:, WIDE + FULL : whole],
                own_half(whole + HALF),
            ],
            axis=0,
        )
        load(block).wait()
        total = total + dot_nt(x_ref[block % 2].T, flat)
        if block + 2 < blocks:
            load(block + 2).start()
        sums = sums + dot_nt(ones, flat)
    for place in range(places):
        start = ((place % cores) * (places // cores) + place // cores) * rows
        out_ref[place, :rows, :] = total[start : start + rows].astype(low)
        out_ref[place, rows:, :] = sums.astype(low)


def widen(block):
    lane = lax.broadcasted_iota(jnp.int32, block.shape, 1)
    zero = jnp.zeros_like(block)
    return jnp.concatenate([jnp.where(lane < FULL, block, zero), jnp.where(lane < FULL, zero, block)], axis=0)


def narrow(block):
    head = block.shape[0] // 2
    return jnp.concatenate([block[:head, :FULL], block[head:, FULL:]], axis=1)


def causal_pair(core, block):
    key = lax.broadcasted_iota(jnp.int32, (PAIR, WIDE), 0)
    lane = lax.broadcasted_iota(jnp.int32, (PAIR, WIDE), 1)
    token = jnp.where(lane < FULL, lane, lane - FULL + HALF * core)
    return key <= token + lax.rem(block, 2) * FULL


def pair_rows(pair):
    return pl.ds(pl.multiple_of(pair * PAIR, PAIR), PAIR)


def over_pairs(causal, block, slots, body, state):
    if causal:
        return lax.fori_loop(0, block // 2, body, state)
    for pair in range(slots // PAIR):
        state = body(pair, state)
    return state


def attend_block(block, causal, core, slots, q, k_ref, vt_ref, s_ref):
    low = jnp.bfloat16
    head = q.shape[0]
    wide = widen(q)

    def top_of(s):
        return jnp.max(s.reshape(PAIR // 8, 8, WIDE), axis=0)

    def look(pair, top):
        rows = pair_rows(pair)
        s = dot_nn(k_ref[rows, :], wide)
        s_ref[rows, :] = s
        return jnp.maximum(top, top_of(s))

    top = over_pairs(causal, block, slots, look, jnp.full((8, WIDE), NEG, jnp.float32))
    if causal:
        rows = pair_rows(block // 2)
        s = jnp.where(causal_pair(core, block), dot_nn(k_ref[rows, :], wide), NEG)
        s_ref[rows, :] = s
        top = jnp.maximum(top, top_of(s))
    top = jnp.max(top, axis=0, keepdims=True)

    def gather(pair, state):
        total, out = state
        rows = pair_rows(pair)
        p = jnp.exp(s_ref[rows, :] - top)
        total = total + jnp.sum(p.reshape(PAIR // 8, 8, WIDE), axis=0)
        out = out + dot_nn(vt_ref[:, rows], p.astype(low))
        return total, out

    state = (jnp.zeros((8, WIDE), jnp.float32), jnp.zeros((2 * head, WIDE), jnp.float32))
    state = over_pairs(causal, block, slots, gather, state)
    total, out = gather(block // 2, state) if causal else state
    total = jnp.sum(total, axis=0, keepdims=True)
    return (narrow(out) / total).astype(low), top + jnp.log(total)


def back_block(block, causal, core, slots, q, do, o, lse, k_ref, kt_ref, v_ref, whole_ref, shared_ref):
    low = jnp.bfloat16
    head = q.shape[0]
    wide_q, wide_do = widen(q), widen(do)
    delta = jnp.sum(do.astype(jnp.float32) * o.astype(jnp.float32), axis=0, keepdims=True)
    qd = jnp.concatenate([q, jnp.zeros_like(q)], axis=0).T
    dd = jnp.concatenate([jnp.zeros_like(do), do], axis=0).T
    mix_whole = jnp.concatenate([qd[:FULL], dd[:FULL]], axis=0)
    mix_shared = jnp.concatenate([qd[FULL:], dd[FULL:]], axis=0)

    def one(pair, dq, masked=False):
        rows = pair_rows(pair)
        s = dot_nn(k_ref[rows, :], wide_q)
        if masked:
            s = jnp.where(causal_pair(core, block), s, NEG)
        p = jnp.exp(s - lse)
        dp = dot_nn(v_ref[rows, :], wide_do)
        ds = (p * (dp - delta)).astype(low)
        p = p.astype(low)
        dq = dq + dot_nn(kt_ref[:, rows], ds)
        whole_ref[rows, :] += dot_nn(jnp.concatenate([ds[:, :FULL], p[:, :FULL]], axis=1), mix_whole)
        shared_ref[rows, :] += dot_nn(jnp.concatenate([ds[:, FULL:], p[:, FULL:]], axis=1), mix_shared)
        return dq

    dq = over_pairs(causal, block, slots, one, jnp.zeros((2 * head, WIDE), jnp.float32))
    if causal:
        dq = one(block // 2, dq, True)
    return narrow(dq).astype(low)


def cross_back_kernel(
    cores, depth,
    q_ref, k_ref, kt_ref, v_ref, o_ref, lse_ref, do_ref, grad_ref,
    dqall_ref, dkv_ref, bv_ref, sum_ref,
    dq_ref, whole_ref, shared_ref, give_ref, got_ref, swap_sem, send_sem, recv_sem, *sum_refs
):
    core, seq, rank = here()
    low = jnp.bfloat16
    count = cores * depth
    mine, places = column_places(cores, depth)
    hidden = PlaneSum(grad_ref.shape[0], grad_ref, 0, *sum_refs)
    peers = [column_peer(place, cores, rank) for place in places] + hidden.peers
    greet(peers)
    slots = k_ref.shape[0]
    whole_ref[...] = jnp.zeros_like(whole_ref)
    shared_ref[...] = jnp.zeros_like(shared_ref)
    back = ColumnSend(cores, depth, dq_ref, dqall_ref, send_sem, recv_sem)

    def go(block):
        return back_block(
            block, False, core, slots, q_ref[block], do_ref[block], o_ref[block], lse_ref[block],
            k_ref, kt_ref, v_ref, whole_ref, shared_ref,
        )

    pl.semaphore_wait(pltpu.get_barrier_semaphore(), len(peers))
    hidden.start()
    dq_ref[places[0]] = go(places[0])
    back.copy(0).start()

    def step(n, carry):
        block = lax.rem(mine + 1 + n, count)
        dq_ref[block] = go(block)
        back.copy(n).start()
        return carry

    lax.fori_loop(1, count - 1, step, 0)
    dqall_ref[mine] = go(mine)
    half = slots // 2
    give_ref[...] = shared_ref[pl.ds(pl.multiple_of((1 - core) * half, half), half), :].astype(low)
    swap = remote_copy(give_ref, got_ref, swap_sem.at[0], swap_sem.at[1], (1 - core, seq, rank))
    swap.start()
    dkv_ref[:slots] = whole_ref[...].astype(low)
    swap.wait()
    kept = shared_ref[pl.ds(pl.multiple_of(core * half, half), half), :]
    dkv_ref[slots:] = (kept + got_ref[...].astype(jnp.float32)).astype(low)
    head = q_ref.shape[1]
    first = jnp.sum(dkv_ref[:slots].astype(jnp.float32), axis=0, keepdims=True)[:, head:]
    second = jnp.sum(dkv_ref[slots:].astype(jnp.float32), axis=0, keepdims=True)[:, head:]
    bv_ref[...] = jnp.concatenate(
        [
            jnp.where(n == 3 * seq + 2 * core, first, jnp.where(n == 3 * seq + 1, second, 0.0))
            for n in range(3 * depth)
        ],
        axis=1,
    )
    back.finish()
    sum_ref[...] = hidden.finish().astype(low)


def attend_cross_back(q, k, kt, v, o, lse, do, grad, columns):
    cores, depth, ranks = lax.axis_size(ITEM), lax.axis_size(SEQ), lax.axis_size(TENSOR)
    lanes = grad.shape[1]
    places, head, _ = q.shape
    slots = k.shape[0]
    low = jnp.bfloat16
    sums = pltpu.VMEM((slots, 2 * head), jnp.float32)
    return call_kernel(
        functools.partial(cross_back_kernel, cores, depth),
        "back_cross",
        [
            (q.shape, low),
            ((slots + slots // 2, 2 * head), low),
            ((1, 3 * depth * head), jnp.float32),
            ((lanes, columns), low),
        ],
        [q, k, kt, v, o, lse, do, grad],
        scratch=[
            pltpu.VMEM(q.shape, low),
            sums,
            sums,
            pltpu.VMEM((slots // 2, 2 * head), low),
            pltpu.VMEM((slots // 2, 2 * head), low),
            pltpu.SemaphoreType.DMA((2,)),
        ]
        + send_scratch(places)
        + sum_scratch(ranks, lanes, columns, low),
        collective_id=5,
        in_spaces=[pltpu.VMEM] * 7 + [pl.ANY],
        us=24,
    )


def self_back_kernel(
    cores, depth, ranks, part,
    dq2_ref, dh2_ref, h1_ref, y1_ref, oin_ref, w_in, gain_ref,
    q_ref, k_ref, kt_ref, v_ref, o_ref, lse_ref, dkv_ref, idx_ref, vmid_ref, bv_ref, red1_in,
    enc_in, wkv_in, ws_in, x_in, grad_ref,
    in_ref, encg_ref, total_ref, squares_ref, pairs_ref, rest_ref, w1_ref, vout_ref,
    w_ref, enc_ref, wkv_ref, ws_ref, x_ref, encp_ref, got_ref, sum_ref, encall_ref,
    dosrc_ref, do_ref, g_ref, gall_ref, whole_ref, shared_ref, dkvall_ref, grad2_ref,
    dh1_ref, dx_ref, self_ref, column_ref, group_ref, plane_ref,
    red1_ref, red2_ref, red4_ref, red5_ref, r1_ref, r2_ref, r4_ref, r5_ref,
    give_ref, gots_ref, shsend, shrecv, load_sem, x_sem, swap_sem, dosend, dorecv, gsend, grecv, kvsend, kvrecv, csend, crecv, psend, precv, zsend, zrecv, *more
):
    core, seq, rank = here()
    low = jnp.bfloat16
    count = cores * depth
    head = part // 3
    per_core = encg_ref.shape[0]
    mine, places = column_places(cores, depth)
    first = PlaneReduce(ranks, grad2_ref, *more[:6])
    second = PlaneReduce(ranks, grad2_ref, more[6], more[1], *more[7:11])
    deal_enc = Deal(cores, ranks, per_core, lambda target: sum_ref.at[target], encall_ref, *more[11:14])
    deal_in = Deal(cores, ranks, per_core, lambda target: dx_ref, in_ref, *more[14:17])
    hidden = PlaneSum(ranks, grad_ref, grad_ref.shape[2] - red5_ref.shape[2], *more[17:21])
    vectors = VectorSum(cores, depth, ranks, vout_ref, *more[21:])
    along = [
        ChainSum(depth, src, dst, zsend.at[n], zrecv.at[n])
        for n, (src, dst) in enumerate(
            ((red1_ref, r1_ref), (red2_ref, r2_ref), (red4_ref, r4_ref), (red5_ref, r5_ref))
        )
    ]
    loads = [
        pltpu.make_async_copy(src, dst, load_sem.at[n])
        for n, (src, dst) in enumerate(((wkv_in, wkv_ref), (enc_in, enc_ref), (ws_in, ws_ref)))
    ]
    squares = [
        pltpu.make_async_copy(
            w_in.at[half, of, pl.ds(0, 2 * part), :], w_ref.at[half, of], load_sem.at[3 + half * ranks + of]
        )
        for half in range(cores)
        for of in range(ranks)
    ]
    for load in squares + loads:
        load.start()
    peers = [column_peer(place, cores, rank) for place in places] + first.peers
    peers += [(1 - core, seq, peer[2]) for peer in first.peers]
    greet(peers)
    chain = Chain(depth, dkvall_ref, kvsend, kvrecv)
    dkvall_ref[seq] = dkv_ref[...]
    pl.semaphore_wait(pltpu.get_barrier_semaphore(), len(peers))
    chain.step(0)
    hidden.start()
    red1_ref[...] = red1_in[...]

    width = y1_ref.shape[1]
    lanes = width // cores
    dq2t = assembled(dq2_ref, depth)
    for load in squares:
        load.wait()
    dy1 = dh2_ref[...] + dot_nn(dq2t.T, late_square(w_ref, 1, part)) * SCALE
    z1, spread1 = centred_rows(h1_ref[...])
    dh1, gg1, gs1 = norm_back(z1, spread1, dy1, as_row(gain_ref))
    e1 = dh1.astype(low)
    dispersed(dot_nt(late_square(w_ref, 0, part), e1).astype(low), dosrc_ref, depth)
    ask = ColumnSend(cores, depth, dosrc_ref, do_ref, dosend, dorecv)
    for step in range(count - 1):
        ask.copy(step).start()
    do_ref[mine] = dosrc_ref[mine]
    dh1_ref[...] = dh1
    ones = jnp.ones((8, FULL), low)
    given = [vmid_ref[n : n + 1] for n in range(vmid_ref.shape[0])]
    given += [gg1, gs1, jnp.sum(e1.astype(jnp.float32), axis=0, keepdims=True), dot_nt(ones, dq2t)[0:1] * SCALE]
    given += [bv_ref[...], jnp.zeros_like(gg1)]
    vectors.start(given)
    o1t = assembled(oin_ref, depth)
    both = jnp.concatenate([y1_ref[...].T, e1.T], axis=1)
    blank = jnp.zeros((part, FULL), low)
    for to in range(ranks):
        rows = slice(to * part, (to + 1) * part)
        right = jnp.concatenate(
            [
                jnp.concatenate([dq2t[rows], blank], axis=1),
                jnp.concatenate([blank, o1t[rows]], axis=1),
            ],
            axis=0,
        )
        for half in range(cores):
            grad2_ref[half, to] = dot_nt(both[half * lanes : (half + 1) * lanes], right).astype(low)
    first.start()

    whole_ref[...] = jnp.zeros_like(whole_ref)
    shared_ref[...] = jnp.zeros_like(shared_ref)
    for step in range(count - 1):
        ask.wait_from(step)
    chain.step(1)
    back = ColumnSend(cores, depth, g_ref, gall_ref, gsend, grecv)

    def swap_shared(block):
        return remote_copy(
            give_ref.at[block], gots_ref.at[block], shsend.at[block], shrecv.at[block], (1 - core, seq, rank)
        )

    def go(block):
        g_ref[block, :, :WIDE] = back_block(
            block, True, core, count * FULL, q_ref[block], do_ref[block], o_ref[block], lse_ref[block],
            k_ref, kt_ref, v_ref, whole_ref, shared_ref,
        )
        start = pl.multiple_of(block * FULL, FULL)
        there = pl.ds(pl.multiple_of(start + (1 - core) * HALF, HALF), HALF)
        give_ref[block] = shared_ref[there, :].astype(low)
        swap_shared(block).start()

    def send_back(block):
        start = pl.multiple_of(block * FULL, FULL)
        whole = whole_ref[pl.ds(start, FULL), :].T.astype(low)
        here_rows = pl.ds(pl.multiple_of(start + core * HALF, HALF), HALF)
        swap_shared(block).wait_recv()
        shared = (shared_ref[here_rows, :] + gots_ref[block].astype(jnp.float32)).T.astype(low)
        g_ref[block, :, WIDE:] = jnp.concatenate([whole[:head], whole[head:], shared[:head], shared[head:]], axis=1)

        @pl.when(block != mine)
        def _():
            back.copy(lax.rem(block + 2 * count - mine - 1, count)).start()

        @pl.when(block == mine)
        def _():
            gall_ref[mine] = g_ref[mine]

    def step(n, carry):
        go(count - 1 - n)
        send_back(count - n)
        return carry

    go(count - 1)
    lax.fori_loop(1, 2, step, 0)
    first.middle()
    chain.step(2)
    lax.fori_loop(2, 4, step, 0)
    along[0].start()
    lax.fori_loop(4, count, step, 0)
    send_back(0)

    self_grads(count, cores, count, x_in, x_ref, x_sem, g_ref, self_ref)
    column = [
        remote_copy(
            self_ref.at[place], column_ref.at[mine], csend.at[step], crecv.at[step], column_peer(place, cores, rank)
        )
        for step, place in enumerate(places)
    ]
    for copy in column:
        copy.start()

    vectors.second()
    for load in loads:
        load.wait()
    for n in range(3, depth):
        chain.step(n)

    encoder_back(ranks, head, enc_ref, wkv_ref, idx_ref, dkvall_ref, encp_ref, grad2_ref)
    swap = remote_copy(encp_ref.at[1 - core], got_ref, swap_sem.at[0], swap_sem.at[1], (1 - core, seq, rank))
    swap.start()
    second.start()
    red2_ref[...] = first.finish().astype(low).reshape(red2_ref.shape)
    along[1].start()
    along[0].relay(1)
    red5_ref[...] = hidden.finish().astype(low).reshape(red5_ref.shape)
    along[3].start()
    swap.wait()
    sum_ref[...] = (encp_ref[core].astype(jnp.float32) + got_ref[...].astype(jnp.float32)).astype(low)
    deal_enc.start()
    second.middle()

    for step in range(count - 1):
        back.wait_from(step)
    dx_ref[...] = input_rows(depth, gall_ref, dh1_ref, ws_ref)
    deal_in.start()
    along[0].relay(2)
    along[1].relay(1)
    along[3].relay(1)

    for copy in column:
        copy.wait()
    column_ref[mine] = self_ref[mine]
    merge_heads(depth, head, column_ref, group_ref)
    plane = [
        remote_copy(group_ref.at[peer[2]], plane_ref.at[rank], psend.at[step], precv.at[step], peer)
        for step, peer in enumerate(first.peers)
    ]
    for copy in plane:
        copy.start()
    red4_ref[...] = second.finish().astype(low).reshape(red4_ref.shape)
    along[2].start()
    along[1].relay(2)
    along[3].relay(2)
    vectors.third()
    along[2].relay(1)

    deal_enc.finish()
    fold = encall_ref.shape[2]
    for item in range(per_core):
        for half in range(cores):
            for side in range(2):
                rows = slice((2 * half + side) * fold, (2 * half + side + 1) * fold)
                encg_ref[item, rows, :] = encall_ref[item, half, :, side * part : (side + 1) * part]
    w1_ref[...] = along[0].finish()
    squares_ref[...] = along[1].finish()
    along[2].relay(2)
    rest_ref[...] = along[3].finish()
    for copy in plane:
        copy.wait()
    total = group_ref[rank].astype(jnp.float32)
    for step in range(1, ranks):
        total = total + plane_ref[lax.rem(rank + step, ranks)].astype(jnp.float32)
    total_ref[...] = total
    vectors.finish()
    chain.finish()
    ask.finish_sends()
    back.finish_sends()
    for block in range(count):
        swap_shared(block).wait_send()
    deal_in.finish()
    pairs_ref[...] = along[2].finish()


def attend_self_back(per_core, *args):
    cores, depth, ranks = lax.axis_size(ITEM), lax.axis_size(SEQ), lax.axis_size(TENSOR)
    (
        dq2, dh2, h1, y1, o1, squares, gain, q, k, kt, v, o, lse, dkv, index, vec_mid, bv, red1, enc, wkv, ws, x_all, grad
    ) = args
    places, head, _ = q.shape
    rows, width = y1.shape
    low, full = jnp.bfloat16, jnp.float32
    part, lanes = 3 * head, width // cores
    all_rows = places * rows
    dma = pltpu.SemaphoreType.DMA
    grads = (cores, ranks, lanes, 2 * part)
    message = (places, head, WIDE + 2 * FULL + 2 * HALF)
    sums = pltpu.VMEM((all_rows, 2 * head), full)
    fold = enc.shape[0] // (2 * cores)
    rest = grad.shape[2] - width
    vec_shape = (places, (vec_mid.shape[0] + 6) // places, width)
    few = width // places
    high = few + 16
    red1 = red1.reshape(depth, few, width)
    along = [pltpu.VMEM((depth, few, columns), low) for columns in (2 * part, 2 * part, rest)]
    into = [pltpu.VMEM((depth + 1, few, columns), low) for columns in (width, 2 * part, 2 * part, rest)]
    args = (*args[:17], red1, *args[18:])
    return call_kernel(
        functools.partial(self_back_kernel, cores, depth, ranks, part),
        "back_self",
        [
            ((per_core, cores, rows, width), low),
            ((per_core, enc.shape[0], part), low),
            ((high, 3 * part), full),
            ((few, 2 * part), full),
            ((few, 2 * part), full),
            ((few, rest), full),
            ((few, width), full),
            (vec_shape, full),
        ],
        list(args),
        scratch=[
            pltpu.VMEM((cores, ranks, 2 * part, lanes), low),
            pltpu.VMEM(enc.shape, low),
            pltpu.VMEM(wkv.shape, low),
            pltpu.VMEM(ws.shape, low),
            pltpu.VMEM((2,) + x_all.shape[1:], low),
            pltpu.VMEM((cores, ranks, fold, 2 * part), low),
            pltpu.VMEM((ranks, fold, 2 * part), low),
            pltpu.VMEM((ranks, fold, 2 * part), low),
            pltpu.VMEM((per_core, cores, fold, 2 * part), low),
            pltpu.VMEM(q.shape, low),
            pltpu.VMEM(q.shape, low),
            pltpu.VMEM(message, low),
            pltpu.VMEM(message, low),
            sums,
            sums,
            pltpu.VMEM((depth,) + dkv.shape, low),
            pltpu.VMEM(grads, low),
            pltpu.VMEM((rows, width), full),
            pltpu.VMEM((rows, width), low),
            pltpu.VMEM((places, high, 6 * head), low),
            pltpu.VMEM((places, high, 6 * head), low),
            pltpu.VMEM((depth, high, 3 * part), low),
            pltpu.VMEM((ranks, high, 3 * part), low),
        ]
        + [pltpu.VMEM(red1.shape, low)]
        + along
        + into
        + [pltpu.VMEM((places, HALF, 2 * head), low), pltpu.VMEM((places, HALF, 2 * head), low)]
        + [dma((places,)), dma((places,)), dma((3 + cores * ranks,)), dma((2,)), dma((2,))]
        + send_scratch(places)
        + send_scratch(places)
        + [dma((2, depth)), dma((depth,))]
        + send_scratch(places)
        + send_scratch(ranks)
        + [dma((4, depth)), dma((4, depth + 1))]
        + reduce_scratch(ranks, lanes, 2 * part, low)
        + reduce_scratch(ranks, lanes, 2 * part, low)[1:]
        + deal_scratch(cores, ranks, per_core)
        + deal_scratch(cores, ranks, per_core)
        + sum_scratch(ranks, lanes, rest, low)
        + vector_scratch(vec_shape, places, ranks),
        collective_id=6,
        in_spaces=[pltpu.VMEM] * 5 + [pl.ANY] + [pltpu.VMEM] * 12 + [pl.ANY] * 5,
        us=100,
    )


def column_body(
    dec_input,
    encoder_states,
    retrieved,
    self_wq,
    self_bq,
    self_wk,
    self_wv,
    self_bv,
    self_wo,
    self_bo,
    norm1_gain,
    norm1_bias,
    cross_wq,
    cross_bq,
    cross_wk,
    cross_wv,
    cross_bv,
    cross_wo,
    cross_bo,
    norm2_gain,
    norm2_bias,
    ffn_w1,
    ffn_b1,
    ffn_w2,
    ffn_b2,
    norm3_gain,
    norm3_bias,
    out_grad,
):
    low, full = jnp.bfloat16, jnp.float32
    core, seq, rank = here()
    cores, depth, ranks = lax.axis_size(ITEM), lax.axis_size(SEQ), lax.axis_size(TENSOR)
    per_core, _, width = dec_input.shape
    slots = retrieved.shape[2]
    part = self_wq.shape[1]
    head = part // 3
    places = cores * depth
    lanes = width // cores
    hidden = ffn_w1.shape[1]

    short = jnp.stack([self_bq, self_bv, cross_bq, cross_bv])
    vectors = jnp.concatenate([jnp.pad(short, ((0, 0), (0, hidden - part))), ffn_b1.reshape(1, hidden)], axis=0)
    vectors = jnp.pad(vectors, ((0, 3), (0, 0)))
    (
        x_all, enc, weights_kv, weights_self, weights_square, weights_in, weights_out,
        grad_mine, index, vectors, q1, k1, k1t, v1, o1_parts, lse1, o1,
        h1, y1, q2, k2, k2t, v2, o2_parts, lse2, o2,
    ) = front(
        dec_input, out_grad, encoder_states, retrieved, vectors,
        [cross_wk.T, cross_wv.T], [self_wq.T, self_wk.T, self_wv.T], [self_wo, cross_wq.T, cross_wo],
        ffn_w1, ffn_w2, [self_bo, norm1_gain, norm1_bias],
    )
    x_all = x_all.reshape(places, FULL, width)
    layer_out, do2, dh2, vec_mid, grad_mid = middle(
        per_core,
        o2,
        y1,
        grad_mine,
        weights_square,
        weights_in,
        weights_out,
        [
            cross_bo,
            norm2_gain,
            norm2_bias,
            vectors,
            ffn_b2,
            norm3_gain,
            norm3_bias,
        ],
    )
    layer_out = layer_out.reshape(per_core, cores * FULL, width)
    dq2, dkv2, bv, first_sum = attend_cross_back(q2, k2, k2t, v2, o2_parts, lse2, do2, grad_mid, hidden)
    input_grad, encoder_grad, total, squares, pairs, rest, gffn_w1, vectors = attend_self_back(
        per_core,
        dq2, dh2, h1, y1, o1, weights_square, norm1_gain,
        q1, k1, k1t, v1, o1_parts, lse1, dkv2, index, vec_mid, bv, first_sum, enc, weights_kv, weights_self, x_all, grad_mid,
    )
    (
        gself_wq, gself_wk, gself_wv, gself_wo, gcross_wq, gcross_wk, gcross_wv, gcross_wo, gffn_w2,
        gself_bq, gself_bv, gself_bo, gnorm1_gain, gnorm1_bias,
        gcross_bq, gcross_bv, gcross_bo, gnorm2_gain, gnorm2_bias, gffn_b1, gffn_b2, gnorm3_gain, gnorm3_bias,
    ) = outputs(head, width, total, squares, pairs, rest, vectors)
    input_grad = input_grad.reshape(per_core, cores * FULL, width)
    gffn_w2 = gffn_w2.T
    return (
        layer_out,
        input_grad,
        encoder_grad,
        gself_wq,
        gself_bq,
        gself_wk,
        gself_wv,
        gself_bv,
        gself_wo,
        gself_bo,
        gnorm1_gain,
        gnorm1_bias,
        gcross_wq,
        gcross_bq,
        gcross_wk,
        gcross_wv,
        gcross_bv,
        gcross_wo,
        gcross_bo,
        gnorm2_gain,
        gnorm2_bias,
        gffn_w1,
        gffn_b1,
        gffn_w2,
        gffn_b2,
        gnorm3_gain,
        gnorm3_bias,
    )


def solution(mesh):
    placed = (
        P(ITEM, SEQ, None),
        P(ITEM, SEQ, None),
        P(ITEM, TENSOR, None),
        P(None, TENSOR),
        P(TENSOR),
        P(None, TENSOR),
        P(None, TENSOR),
        P(TENSOR),
        P(TENSOR, None),
        P(),
        P(),
        P(),
        P(None, TENSOR),
        P(TENSOR),
        P(None, TENSOR),
        P(None, TENSOR),
        P(TENSOR),
        P(TENSOR, None),
        P(),
        P(),
        P(),
        P(None, TENSOR),
        P(TENSOR),
        P(TENSOR, None),
        P(),
        P(),
        P(),
        P(ITEM, SEQ, None),
    )
    reduced = (
        P(ITEM, SEQ, None),
        P(ITEM, SEQ, None),
        P(ITEM, SEQ, TENSOR),
        P((ITEM, SEQ), TENSOR),
        P(TENSOR),
        P((ITEM, SEQ), TENSOR),
        P((ITEM, SEQ), TENSOR),
        P(TENSOR),
        P(TENSOR, (ITEM, SEQ)),
        P(),
        P(),
        P(),
        P((ITEM, SEQ), TENSOR),
        P(TENSOR),
        P((ITEM, SEQ), TENSOR),
        P((ITEM, SEQ), TENSOR),
        P(TENSOR),
        P(TENSOR, (ITEM, SEQ)),
        P(),
        P(),
        P(),
        P((ITEM, SEQ), TENSOR),
        P(TENSOR),
        P(TENSOR, (ITEM, SEQ)),
        P(),
        P(),
        P(),
    )

    def layer(*arrays):
        chosen = column_body if column_plan_fits(mesh, arrays) else general_body
        return jax.shard_map(
            chosen,
            mesh=mesh,
            in_specs=placed,
            out_specs=reduced,
            check_vma=False,
        )(*arrays)

    return layer
```

```python
import functools

import jax
import jax.numpy as jnp
from jax import lax
from jax.experimental import pallas as pl
from jax.experimental.pallas import tpu as pltpu
from jax.sharding import PartitionSpec as P

EPS = 1e-05
SCALE = 0.125
NEG = -1e30
MESH = pl.DeviceIdType.MESH
ITEM, SEQ, TENSOR = "item", "seq", "tensor"


def matmul(first_op, second_op):
    return jnp.dot(first_op, second_op, preferred_element_type=jnp.float32)


def layer_norm(rows_in, norm_gain, norm_shift):
    center = rows_in - jnp.mean(rows_in, axis=-1, keepdims=True)
    spread = jnp.mean(center * center, axis=-1, keepdims=True)
    return center * lax.rsqrt(spread + EPS) * norm_gain + norm_shift


def exact_gelu(values_in):
    return jax.nn.gelu(values_in, approximate=False)


def tensor_total(partial_rows):
    return lax.psum(partial_rows, TENSOR)


def row_total(values_in):
    return jnp.sum(values_in.astype(jnp.float32), axis=(0, 1))


def softmax_stats(scores):
    row_max = jnp.max(scores, axis=-1, keepdims=True)
    shifted = jnp.exp(scores - row_max)
    row_sum = jnp.sum(shifted, axis=-1, keepdims=True)
    return (shifted / row_sum, row_max + jnp.log(row_sum))


def owned_pick(encoder_states, kv_weights, kv_bias, flat_index, owned_mask):
    kv_table = (
        jnp.einsum("ind,dhf->inhf", encoder_states, kv_weights, preferred_element_type=jnp.float32)
        + kv_bias
    ).astype(jnp.bfloat16)
    flat_table = kv_table.reshape(-1, kv_table.shape[-1])
    picked = jnp.take(flat_table, flat_index, axis=0)
    return jnp.where(owned_mask, picked.astype(jnp.float32), 0.0)


def general_body(
    dec_input,
    encoder_states,
    retrieved,
    self_wq,
    self_bq,
    self_wk,
    self_wv,
    self_bv,
    self_wo,
    self_bo,
    norm1_gain,
    norm1_bias,
    cross_wq,
    cross_bq,
    cross_wk,
    cross_wv,
    cross_bv,
    cross_wo,
    cross_bo,
    norm2_gain,
    norm2_bias,
    ffn_w1,
    ffn_b1,
    ffn_w2,
    ffn_b2,
    norm3_gain,
    norm3_bias,
    out_grad,
):
    item_count, dec_rows, model_width = dec_input.shape
    local_heads = retrieved.shape[1]
    enc_rows = encoder_states.shape[1]
    head_cols = self_wq.shape[1]
    head_size = head_cols // local_heads
    seq_devices = lax.axis_size(SEQ)
    seq_rank = lax.axis_index(SEQ)
    seq_length = dec_rows * seq_devices
    queries = ((matmul(dec_input, self_wq) + self_bq) * SCALE).astype(jnp.bfloat16)
    keys_local = matmul(dec_input, self_wk).astype(jnp.bfloat16)
    values_local = (matmul(dec_input, self_wv) + self_bv).astype(jnp.bfloat16)
    kv_all = lax.all_gather(
        jnp.concatenate([keys_local, values_local], axis=-1), SEQ, axis=1, tiled=True
    )
    keys_all = kv_all[..., :head_cols].reshape(item_count, seq_length, local_heads, head_size)
    values_all = kv_all[..., head_cols:].reshape(item_count, seq_length, local_heads, head_size)
    query_heads = queries.reshape(item_count, dec_rows, local_heads, head_size)
    query_pos = seq_rank * dec_rows + jnp.arange(dec_rows)
    causal = query_pos[:, None] >= jnp.arange(seq_length)[None, :]

    def self_scores():
        raw_scores = jnp.einsum(
            "irhe,ilhe->ihrl", query_heads, keys_all, preferred_element_type=jnp.float32
        )
        return jnp.where(causal, raw_scores, NEG)

    prob_self, lse_self = softmax_stats(self_scores())
    attended = (
        jnp.einsum(
            "ihrl,ilhe->irhe",
            prob_self.astype(jnp.bfloat16),
            values_all,
            preferred_element_type=jnp.float32,
        )
        .astype(jnp.bfloat16)
        .reshape(item_count, dec_rows, head_cols)
    )
    branch_one = tensor_total(matmul(attended, self_wo)) + self_bo
    hidden_one = dec_input.astype(jnp.float32) + branch_one
    normed_one = layer_norm(hidden_one, norm1_gain, norm1_bias).astype(jnp.bfloat16)
    queries_x = (
        ((matmul(normed_one, cross_wq) + cross_bq) * SCALE)
        .astype(jnp.bfloat16)
        .reshape(item_count, dec_rows, local_heads, head_size)
    )
    kv_weights = jnp.concatenate(
        [
            cross_wk.reshape(model_width, local_heads, head_size),
            cross_wv.reshape(model_width, local_heads, head_size),
        ],
        axis=-1,
    )
    kv_bias = jnp.concatenate(
        [
            jnp.zeros((local_heads, head_size), jnp.float32),
            cross_bv.reshape(local_heads, head_size),
        ],
        axis=-1,
    )
    local_row = retrieved - seq_rank * enc_rows
    owned_mask = ((local_row >= 0) & (local_row < enc_rows))[..., None]
    flat_index = (
        jnp.arange(item_count, dtype=jnp.int32)[:, None, None] * enc_rows
        + jnp.clip(local_row, 0, enc_rows - 1)
    ) * local_heads + jnp.arange(local_heads, dtype=jnp.int32)[None, :, None]
    retrieved_kv = lax.psum(
        owned_pick(encoder_states, kv_weights, kv_bias, flat_index, owned_mask).astype(
            jnp.bfloat16
        ),
        SEQ,
    )

    def cross_scores(kv_pair):
        return jnp.einsum(
            "irhe,ihke->ihrk",
            queries_x,
            kv_pair[..., :head_size],
            preferred_element_type=jnp.float32,
        )

    prob_cross, lse_cross = softmax_stats(cross_scores(retrieved_kv))
    attended_x = (
        jnp.einsum(
            "ihrk,ihke->irhe",
            prob_cross.astype(jnp.bfloat16),
            retrieved_kv[..., head_size:],
            preferred_element_type=jnp.float32,
        )
        .astype(jnp.bfloat16)
        .reshape(item_count, dec_rows, head_cols)
    )
    branch_two = tensor_total(matmul(attended_x, cross_wo)) + cross_bo
    hidden_two = normed_one.astype(jnp.float32) + branch_two
    normed_two = layer_norm(hidden_two, norm2_gain, norm2_bias).astype(jnp.bfloat16)
    pre_act = matmul(normed_two, ffn_w1) + ffn_b1
    activated = exact_gelu(pre_act).astype(jnp.bfloat16)
    branch_three = tensor_total(matmul(activated, ffn_w2)) + ffn_b2
    hidden_three = normed_two.astype(jnp.float32) + branch_three
    layer_out = layer_norm(hidden_three, norm3_gain, norm3_bias)
    _, back_three = jax.vjp(layer_norm, hidden_three, norm3_gain, norm3_bias)
    d_hidden3, gnorm3_gain, gnorm3_bias = back_three(out_grad.astype(jnp.float32))
    d_branch3 = d_hidden3.astype(jnp.bfloat16)
    gffn_b2 = row_total(d_branch3)
    gffn_w2 = jnp.einsum("irf,ird->fd", activated, d_branch3, preferred_element_type=jnp.float32)
    d_activated = jnp.einsum("ird,fd->irf", d_branch3, ffn_w2, preferred_element_type=jnp.float32)
    _, gelu_back = jax.vjp(exact_gelu, pre_act)
    d_pre = gelu_back(d_activated)[0].astype(jnp.bfloat16)
    gffn_b1 = row_total(d_pre)
    gffn_w1 = jnp.einsum("ird,irf->df", normed_two, d_pre, preferred_element_type=jnp.float32)
    d_normed2 = d_hidden3 + tensor_total(
        jnp.einsum("irf,df->ird", d_pre, ffn_w1, preferred_element_type=jnp.float32)
    )
    _, back_two = jax.vjp(layer_norm, hidden_two, norm2_gain, norm2_bias)
    d_hidden2, gnorm2_gain, gnorm2_bias = back_two(d_normed2)
    d_branch2 = d_hidden2.astype(jnp.bfloat16)
    gcross_bo = row_total(d_branch2)
    gcross_wo = jnp.einsum("irc,ird->cd", attended_x, d_branch2, preferred_element_type=jnp.float32)
    d_attended2 = (
        jnp.einsum("ird,cd->irc", d_branch2, cross_wo, preferred_element_type=jnp.float32)
        .astype(jnp.bfloat16)
        .reshape(item_count, dec_rows, local_heads, head_size)
    )
    kv_back = lax.psum(
        owned_pick(encoder_states, kv_weights, kv_bias, flat_index, owned_mask).astype(
            jnp.bfloat16
        ),
        SEQ,
    )
    redo_cross = jnp.exp(cross_scores(kv_back) - lse_cross)
    dprob_cross = jnp.einsum(
        "irhe,ihke->ihrk", d_attended2, kv_back[..., head_size:], preferred_element_type=jnp.float32
    )
    d_scores2 = (
        redo_cross * (dprob_cross - jnp.sum(dprob_cross * redo_cross, axis=-1, keepdims=True))
    ).astype(jnp.bfloat16)
    d_query2 = (
        jnp.einsum(
            "ihrk,ihke->irhe",
            d_scores2,
            kv_back[..., :head_size],
            preferred_element_type=jnp.float32,
        )
        .astype(jnp.bfloat16)
        .reshape(item_count, dec_rows, head_cols)
    )
    kv_grad_part = jnp.concatenate(
        [
            jnp.einsum("ihrk,irhe->ihke", d_scores2, queries_x, preferred_element_type=jnp.float32),
            jnp.einsum(
                "ihrk,irhe->ihke",
                redo_cross.astype(jnp.bfloat16),
                d_attended2,
                preferred_element_type=jnp.float32,
            ),
        ],
        axis=-1,
    )
    kv_grad = lax.psum(kv_grad_part, SEQ).astype(jnp.bfloat16)
    kv_owned = jnp.where(owned_mask, kv_grad.astype(jnp.float32), 0.0)
    table_grad = (
        jnp.zeros((item_count * enc_rows * local_heads, 2 * head_size), jnp.float32)
        .at[flat_index.reshape(-1)]
        .add(kv_owned.reshape(-1, 2 * head_size))
    )
    table_low = table_grad.astype(jnp.bfloat16).reshape(
        item_count, enc_rows, local_heads, 2 * head_size
    )
    grad_kv_weights = jnp.einsum(
        "ind,inhf->dhf", encoder_states, table_low, preferred_element_type=jnp.float32
    )
    gcross_wk = grad_kv_weights[..., :head_size].reshape(model_width, head_cols)
    gcross_wv = grad_kv_weights[..., head_size:].reshape(model_width, head_cols)
    gcross_bv = row_total(table_low[..., head_size:]).reshape(head_cols)
    encoder_part = jnp.einsum(
        "inhf,dhf->ind", table_low, kv_weights, preferred_element_type=jnp.float32
    )
    encoder_grad = lax.psum_scatter(encoder_part, TENSOR, scatter_dimension=2, tiled=True).astype(
        jnp.bfloat16
    )
    gcross_bq = row_total(d_query2) * SCALE
    gcross_wq = (
        jnp.einsum("ird,irc->dc", normed_one, d_query2, preferred_element_type=jnp.float32) * SCALE
    )
    d_normed1 = d_hidden2 + tensor_total(
        jnp.einsum("irc,dc->ird", d_query2, cross_wq, preferred_element_type=jnp.float32) * SCALE
    )
    _, back_one = jax.vjp(layer_norm, hidden_one, norm1_gain, norm1_bias)
    d_hidden1, gnorm1_gain, gnorm1_bias = back_one(d_normed1)
    d_branch1 = d_hidden1.astype(jnp.bfloat16)
    gself_bo = row_total(d_branch1)
    gself_wo = jnp.einsum("irc,ird->cd", attended, d_branch1, preferred_element_type=jnp.float32)
    d_attended1 = (
        jnp.einsum("ird,cd->irc", d_branch1, self_wo, preferred_element_type=jnp.float32)
        .astype(jnp.bfloat16)
        .reshape(item_count, dec_rows, local_heads, head_size)
    )
    redo_self = jnp.exp(self_scores() - lse_self)
    dprob_self = jnp.einsum(
        "irhe,ilhe->ihrl", d_attended1, values_all, preferred_element_type=jnp.float32
    )
    d_scores1 = (
        redo_self * (dprob_self - jnp.sum(dprob_self * redo_self, axis=-1, keepdims=True))
    ).astype(jnp.bfloat16)
    probs_low = redo_self.astype(jnp.bfloat16)
    d_query1 = (
        jnp.einsum("ihrl,ilhe->irhe", d_scores1, keys_all, preferred_element_type=jnp.float32)
        .astype(jnp.bfloat16)
        .reshape(item_count, dec_rows, head_cols)
    )
    row_count = dec_rows * lax.axis_size(SEQ)
    key_grad = jnp.einsum(
        "ihrl,irhe->lihe", d_scores1, query_heads, preferred_element_type=jnp.float32
    ).reshape(row_count, item_count, head_cols)
    value_grad = jnp.einsum(
        "ihrl,irhe->lihe", probs_low, d_attended1, preferred_element_type=jnp.float32
    ).reshape(row_count, item_count, head_cols)
    kv_self = lax.psum_scatter(
        jnp.concatenate([key_grad, value_grad], axis=-1), SEQ, scatter_dimension=0, tiled=True
    ).astype(jnp.bfloat16)
    kv_self = jnp.swapaxes(kv_self, 0, 1)
    d_key1 = kv_self[..., :head_cols]
    d_value1 = kv_self[..., head_cols:]
    gself_bq = row_total(d_query1) * SCALE
    gself_wq = (
        jnp.einsum("ird,irc->dc", dec_input, d_query1, preferred_element_type=jnp.float32) * SCALE
    )
    gself_wk = jnp.einsum("ird,irc->dc", dec_input, d_key1, preferred_element_type=jnp.float32)
    gself_wv = jnp.einsum("ird,irc->dc", dec_input, d_value1, preferred_element_type=jnp.float32)
    gself_bv = row_total(d_value1)
    input_part = (
        jnp.einsum("irc,dc->ird", d_query1, self_wq, preferred_element_type=jnp.float32) * SCALE
        + jnp.einsum("irc,dc->ird", d_key1, self_wk, preferred_element_type=jnp.float32)
        + jnp.einsum("irc,dc->ird", d_value1, self_wv, preferred_element_type=jnp.float32)
    )
    input_grad = (d_hidden1 + tensor_total(input_part)).astype(jnp.bfloat16)
    matrices = (
        lax.psum_scatter(gself_wq, (ITEM, SEQ), scatter_dimension=0, tiled=True),
        lax.psum_scatter(gself_wk, (ITEM, SEQ), scatter_dimension=0, tiled=True),
        lax.psum_scatter(gself_wv, (ITEM, SEQ), scatter_dimension=0, tiled=True),
        lax.psum_scatter(gself_wo, (ITEM, SEQ), scatter_dimension=1, tiled=True),
        lax.psum_scatter(gcross_wq, (ITEM, SEQ), scatter_dimension=0, tiled=True),
        lax.psum_scatter(gcross_wk, (ITEM, SEQ), scatter_dimension=0, tiled=True),
        lax.psum_scatter(gcross_wv, (ITEM, SEQ), scatter_dimension=0, tiled=True),
        lax.psum_scatter(gcross_wo, (ITEM, SEQ), scatter_dimension=1, tiled=True),
        lax.psum_scatter(gffn_w1, (ITEM, SEQ), scatter_dimension=0, tiled=True),
        lax.psum_scatter(gffn_w2, (ITEM, SEQ), scatter_dimension=1, tiled=True),
    )
    vectors = lax.psum(
        (
            gself_bq,
            gself_bv,
            gself_bo,
            gnorm1_gain,
            gnorm1_bias,
            gcross_bq,
            gcross_bv,
            gcross_bo,
            gnorm2_gain,
            gnorm2_bias,
            gffn_b1,
            gffn_b2,
            gnorm3_gain,
            gnorm3_bias,
        ),
        (ITEM, SEQ),
    )
    return (
        layer_out.astype(jnp.bfloat16),
        input_grad,
        encoder_grad,
        matrices[0],
        vectors[0],
        matrices[1],
        matrices[2],
        vectors[1],
        matrices[3],
        vectors[2],
        vectors[3],
        vectors[4],
        matrices[4],
        vectors[5],
        matrices[5],
        matrices[6],
        vectors[6],
        matrices[7],
        vectors[7],
        vectors[8],
        vectors[9],
        matrices[8],
        vectors[10],
        matrices[9],
        vectors[11],
        vectors[12],
        vectors[13],
    )


VMEM_LIMIT = 58 * 1024 * 1024
FULL = 256
HALF = 128
WIDE = FULL + HALF
PAIR = 2 * FULL


def column_plan_fits(mesh, arrays):
    items, cores = arrays[0].shape[0], mesh.shape[ITEM]
    ranks, depth = mesh.shape[TENSOR], mesh.shape[SEQ]
    heads = arrays[2].shape[1]
    rows = arrays[0].shape[1] // depth
    width = arrays[0].shape[2]
    return (
        cores == 2
        and ranks == 4
        and items == ranks
        and ranks == depth
        and heads == 3 * depth
        and width == 64 * heads
        and rows == cores * FULL
        and arrays[2].shape[2] % PAIR == 0
    )


def here():
    return lax.axis_index(ITEM), lax.axis_index(SEQ), lax.axis_index(TENSOR)


def call_kernel(kernel, name, outs, args, scratch=(), collective_id=None, in_spaces=None, out_space=None, us=10):
    single = isinstance(outs, tuple)
    listed = [outs] if single else list(outs)
    out_spaces = [pltpu.VMEM] * len(listed) if out_space is None else out_space
    spaces = [pltpu.VMEM] * len(args) if in_spaces is None else in_spaces
    params = dict(vmem_limit_bytes=VMEM_LIMIT)
    if collective_id is not None:
        params.update(collective_id=collective_id, has_side_effects=True)
    out = pl.pallas_call(
        kernel,
        out_shape=[jax.ShapeDtypeStruct(s, d) for s, d in listed],
        in_specs=[pl.BlockSpec(memory_space=s) for s in spaces],
        out_specs=[pl.BlockSpec(memory_space=s) for s in out_spaces],
        scratch_shapes=list(scratch),
        compiler_params=pltpu.CompilerParams(**params),
        cost_estimate=pl.CostEstimate(flops=us * 10**9, bytes_accessed=us * 3 * 10**6, transcendentals=0),
        name=name,
    )(*args)
    return out[0] if single else out


def greet(peers):
    gate = pltpu.get_barrier_semaphore()
    for peer in peers:
        pl.semaphore_signal(gate, inc=1, device_id=peer, device_id_type=MESH)


def meet(peers):
    greet(peers)
    pl.semaphore_wait(pltpu.get_barrier_semaphore(), len(peers))


def column_peer(place, cores, rank):
    return (lax.rem(place, cores), place // cores, rank)


def remote_copy(src, dst, send, recv, device):
    return pltpu.make_async_remote_copy(
        src_ref=src, dst_ref=dst, send_sem=send, recv_sem=recv, device_id=device, device_id_type=MESH
    )


def plane_peers(cores, ranks):
    core, seq, rank = here()
    peers = []
    for step in range(1, cores * ranks):
        place = lax.rem(rank * cores + core + step, cores * ranks)
        peers.append((lax.rem(place, cores), seq, place // cores))
    return peers


class Deal:
    def __init__(self, cores, ranks, per_core, source, all_ref, send_sem, recv_sem, own_sem):
        self.cores, self.ranks, self.per_core = cores, ranks, per_core
        self.source, self.all_ref = source, all_ref
        self.send_sem, self.recv_sem, self.own_sem = send_sem, recv_sem, own_sem
        self.core, self.seq, self.rank = here()
        self.home = self.rank // per_core
        self.local = lax.rem(self.rank, per_core)

    def send(self, step):
        target = lax.rem(self.rank + step, self.ranks)
        return remote_copy(
            self.source(target),
            self.all_ref.at[self.local, self.core],
            self.send_sem.at[step],
            self.recv_sem.at[self.local, self.core],
            (self.home, self.seq, target),
        )

    def keep(self):
        return pltpu.make_async_copy(self.source(self.rank), self.all_ref.at[self.local, self.core], self.own_sem)

    def start(self):
        for step in range(1, self.ranks):
            self.send(step).start()

        @pl.when(self.core != self.home)
        def _():
            self.send(0).start()

        @pl.when(self.core == self.home)
        def _():
            self.keep().start()

    def finish(self):
        for item in range(self.per_core):
            for half in range(self.cores):
                inside = (half == self.core) & (self.core * self.per_core + item == self.rank)

                @pl.when(jnp.logical_not(inside))
                def _():
                    remote_copy(
                        self.source(0),
                        self.all_ref.at[item, half],
                        self.send_sem.at[0],
                        self.recv_sem.at[item, half],
                        (1 - self.core, self.seq, self.rank),
                    ).wait_recv()

        for step in range(1, self.ranks):
            self.send(step).wait_send()

        @pl.when(self.core != self.home)
        def _():
            self.send(0).wait_send()

        @pl.when(self.core == self.home)
        def _():
            self.keep().wait()


def deal_scratch(cores, ranks, per_core):
    dma = pltpu.SemaphoreType.DMA
    return [dma((ranks,)), dma((per_core, cores)), dma]


class PlaneGather:
    def __init__(self, all_ref, give_send, give_recv, far_send, far_recv, pass_send, pass_recv):
        self.all_ref = all_ref
        self.give_send, self.give_recv = give_send, give_recv
        self.far_send, self.far_recv = far_send, far_recv
        self.pass_send, self.pass_recv = pass_send, pass_recv
        self.core, self.seq, self.rank = here()
        low, high = lax.rem(self.rank, 2), self.rank // 2
        self.near = (2 * high + 1 - low, 2 * (1 - high) + low)
        self.far = 2 * (1 - high) + 1 - low
        self.half = all_ref.shape[2] // 2
        self.peers = [(self.core, self.seq, rank) for rank in self.near]

    def give(self, way):
        block = self.all_ref.at[self.core, self.rank]
        return remote_copy(block, block, self.give_send.at[way], self.give_recv.at[way], self.peers[way])

    def far_part(self, way, origin):
        return self.all_ref.at[self.core, origin, pl.ds(way * self.half, self.half), :]

    def onward(self, way):
        block = self.far_part(way, self.near[way])
        return remote_copy(
            block, block, self.far_send.at[way], self.far_recv.at[way], self.peers[1 - way]
        )

    def side(self, slot, block):
        return remote_copy(
            block, block, self.pass_send.at[slot], self.pass_recv.at[slot], (1 - self.core, self.seq, self.rank)
        )

    def sides(self):
        near = [self.side(way, self.all_ref.at[self.core, self.near[way]]) for way in range(2)]
        return near + [self.side(2 + way, self.far_part(way, self.far)) for way in range(2)]

    def start(self):
        for way in range(2):
            self.give(way).start()

    def forward(self):
        sides = self.sides()
        for way in range(2):
            self.give(way).wait_recv()
            self.onward(way).start()
            sides[way].start()

    def arrive(self):
        sides = self.sides()
        for way in range(2):
            self.onward(way).wait_recv()
            sides[2 + way].start()
        for side in sides:
            side.wait_recv()

    def finish(self):
        for way in range(2):
            self.give(way).wait_send()
            self.onward(way).wait_send()
        for side in self.sides():
            side.wait_send()


def own_weights(refs, all_ref, sem):
    cores, _, _, lanes = all_ref.shape
    rank = lax.axis_index(TENSOR)
    copies, first = [], 0
    for n, ref in enumerate(refs):
        rows = ref.shape[0]
        for half in range(cores):
            copies.append(
                pltpu.make_async_copy(
                    ref.at[:, pl.ds(half * lanes, lanes)],
                    all_ref.at[half, rank, pl.ds(first, rows), :],
                    sem.at[n, half],
                )
            )
        first += rows
    return copies


def gather_scratch():
    return [pltpu.SemaphoreType.DMA((n,)) for n in (2, 2, 2, 2, 4, 4)]


class PlaneReduce:
    def __init__(self, ranks, grad_ref, got_ref, sum_ref, all_ref, swap_sem, send_sem, recv_sem):
        self.ranks, self.grad_ref, self.got_ref = ranks, grad_ref, got_ref
        self.sum_ref, self.all_ref = sum_ref, all_ref
        self.swap_sem, self.send_sem, self.recv_sem = swap_sem, send_sem, recv_sem
        self.core, self.seq, self.rank = here()
        self.peers = [(self.core, self.seq, lax.rem(self.rank + step, ranks)) for step in range(1, ranks)]

    def swap(self):
        return remote_copy(
            self.grad_ref.at[1 - self.core],
            self.got_ref,
            self.swap_sem.at[0],
            self.swap_sem.at[1],
            (1 - self.core, self.seq, self.rank),
        )

    def copy(self, step):
        peer = self.peers[step]
        return remote_copy(
            self.sum_ref.at[peer[2]], self.all_ref.at[self.rank], self.send_sem.at[step], self.recv_sem.at[step], peer
        )

    def start(self):
        self.swap().start()

    def middle(self):
        self.swap().wait()
        for rank in range(self.ranks):
            self.sum_ref[rank] = (
                self.grad_ref[self.core, rank].astype(jnp.float32) + self.got_ref[rank].astype(jnp.float32)
            ).astype(self.sum_ref.dtype)
        for step in range(self.ranks - 1):
            self.copy(step).start()

    def finish(self):
        for step in range(self.ranks - 1):
            self.copy(step).wait()
        total = self.sum_ref[self.rank].astype(jnp.float32)
        for step in range(1, self.ranks):
            total = total + self.all_ref[lax.rem(self.rank + step, self.ranks)].astype(jnp.float32)
        return total


class PlaneSum:
    def __init__(self, ranks, src_ref, first, all_ref, own_sem, send_sem, recv_sem):
        self.ranks, self.src_ref, self.first = ranks, src_ref, first
        self.all_ref, self.own_sem, self.send_sem, self.recv_sem = all_ref, own_sem, send_sem, recv_sem
        self.core, self.seq, self.rank = here()
        self.peers = [(self.core, self.seq, lax.rem(self.rank + step, ranks)) for step in range(1, ranks)]

    def block(self, rank):
        return self.src_ref.at[rank, :, pl.ds(self.first, self.all_ref.shape[2])]

    def own(self):
        return pltpu.make_async_copy(self.block(self.rank), self.all_ref.at[self.rank], self.own_sem)

    def copy(self, step):
        peer = self.peers[step]
        return remote_copy(
            self.block(peer[2]), self.all_ref.at[self.rank], self.send_sem.at[step], self.recv_sem.at[step], peer
        )

    def start(self):
        self.own().start()
        for step in range(self.ranks - 1):
            self.copy(step).start()

    def finish(self):
        self.own().wait()
        for step in range(self.ranks - 1):
            self.copy(step).wait()
        total = self.all_ref[0].astype(jnp.float32)
        for origin in range(1, self.ranks):
            total = total + self.all_ref[origin].astype(jnp.float32)
        return total


def sum_scratch(ranks, rows, columns, dtype):
    dma = pltpu.SemaphoreType.DMA
    return [pltpu.VMEM((ranks, rows, columns), dtype), dma, dma((ranks - 1,)), dma((ranks - 1,))]


def reduce_scratch(ranks, rows, columns, dtype):
    dma = pltpu.SemaphoreType.DMA
    block = pltpu.VMEM((ranks, rows, columns), dtype)
    return [block, block, block, dma((2,)), dma((ranks - 1,)), dma((ranks - 1,))]


def column_places(cores, depth):
    core, seq, _ = here()
    mine = seq * cores + core
    return mine, [lax.rem(mine + step, cores * depth) for step in range(1, cores * depth)]


class ColumnSend:
    def __init__(self, cores, depth, source_ref, all_ref, send_sem, recv_sem):
        self.cores, self.count = cores, cores * depth
        self.source_ref, self.all_ref = source_ref, all_ref
        self.send_sem, self.recv_sem = send_sem, recv_sem
        core, seq, self.rank = here()
        self.mine = seq * cores + core

    def copy(self, step):
        place = lax.rem(self.mine + 1 + step, self.count)
        return remote_copy(
            self.source_ref.at[place],
            self.all_ref.at[self.mine],
            self.send_sem.at[step],
            self.recv_sem.at[step],
            column_peer(place, self.cores, self.rank),
        )

    def wait_from(self, step):
        self.copy(step).wait_recv()

    def finish_sends(self):
        for step in range(self.count - 1):
            self.copy(step).wait_send()

    def finish(self):
        for step in range(self.count - 1):
            self.copy(step).wait()


def send_scratch(count):
    return [pltpu.SemaphoreType.DMA((count - 1,)), pltpu.SemaphoreType.DMA((count - 1,))]


class Chain:
    def __init__(self, depth, all_ref, send_sem, recv_sem):
        self.depth, self.all_ref = depth, all_ref
        self.send_sem, self.recv_sem = send_sem, recv_sem
        core, self.seq, rank = here()
        self.above = (core, lax.rem(self.seq + 1, depth), rank)
        self.below = (core, lax.rem(self.seq + depth - 1, depth), rank)

    def copy(self, block, way):
        part = self.all_ref.at[block]
        target = self.above if way == 0 else self.below
        return remote_copy(part, part, self.send_sem.at[way, block], self.recv_sem.at[block], target)

    def step(self, n):
        up, down = self.seq - n, self.seq + n

        @pl.when(up >= 0)
        def _():
            if n > 0:
                self.copy(up, 0).wait_recv()

            @pl.when(self.seq + 1 < self.depth)
            def _():
                self.copy(up, 0).start()

        @pl.when(down < self.depth)
        def _():
            if n > 0:
                self.copy(down, 1).wait_recv()

            @pl.when(self.seq > 0)
            def _():
                self.copy(down, 1).start()

    def finish(self):
        for n in range(self.depth):
            up, down = self.seq - n, self.seq + n

            @pl.when((up >= 0) & (self.seq + 1 < self.depth))
            def _():
                self.copy(up, 0).wait_send()

            @pl.when((down < self.depth) & (self.seq > 0))
            def _():
                self.copy(down, 1).wait_send()


class VectorSum:
    def __init__(self, cores, depth, ranks, out_ref, src_ref, col_ref, sum_ref, plane_ref, a_send, a_recv, b_send, b_recv, c_send, c_recv):
        self.cores, self.depth, self.ranks = cores, depth, ranks
        self.out_ref, self.src_ref, self.col_ref = out_ref, src_ref, col_ref
        self.sum_ref, self.plane_ref = sum_ref, plane_ref
        self.sems = ((a_send, a_recv), (b_send, b_recv), (c_send, c_recv))
        core, seq, self.rank = here()
        self.mine, self.places = column_places(cores, depth)
        self.peers = [(core, seq, lax.rem(self.rank + step, ranks)) for step in range(1, ranks)]

    def copies(self, stage):
        send, recv = self.sems[stage]
        if stage == 1:
            return [
                remote_copy(self.sum_ref, self.plane_ref.at[self.rank], send.at[n], recv.at[n], peer)
                for n, peer in enumerate(self.peers)
            ]
        src = self.src_ref if stage == 0 else self.out_ref
        dst = self.col_ref if stage == 0 else self.out_ref
        return [
            remote_copy(
                src.at[place if stage == 0 else self.mine],
                dst.at[self.mine],
                send.at[n],
                recv.at[n],
                column_peer(place, self.cores, self.rank),
            )
            for n, place in enumerate(self.places)
        ]

    def start(self, rows):
        height = self.src_ref.shape[1]
        for n, row in enumerate(rows):
            self.src_ref[n // height, n % height : n % height + 1, :] = row
        for copy in self.copies(0):
            copy.start()

    def second(self):
        for copy in self.copies(0):
            copy.wait()
        total = self.src_ref[self.mine]
        for place in self.places:
            total = total + self.col_ref[place]
        self.sum_ref[...] = total
        for copy in self.copies(1):
            copy.start()

    def third(self):
        for copy in self.copies(1):
            copy.wait()
        self.plane_ref[self.rank] = self.sum_ref[...]
        total = self.plane_ref[0]
        for origin in range(1, self.ranks):
            total = total + self.plane_ref[origin]
        self.out_ref[self.mine] = total
        for copy in self.copies(2):
            copy.start()

    def finish(self):
        for copy in self.copies(2):
            copy.wait()


def vector_scratch(shape, places, ranks):
    full = jnp.float32
    return [
        pltpu.VMEM(shape, full),
        pltpu.VMEM(shape, full),
        pltpu.VMEM(shape[1:], full),
        pltpu.VMEM((ranks,) + shape[1:], full),
    ] + [pltpu.SemaphoreType.DMA((n - 1,)) for n in (places, places, ranks, ranks, places, places)]


class ChainSum:
    def __init__(self, depth, src_ref, in_ref, send_sem, recv_sem):
        self.depth, self.src_ref, self.in_ref = depth, src_ref, in_ref
        self.send_sem, self.recv_sem = send_sem, recv_sem
        core, self.seq, rank = here()
        self.above = (core, lax.rem(self.seq + 1, depth), rank)
        self.below = (core, lax.rem(self.seq + depth - 1, depth), rank)

    def up(self, block):
        return remote_copy(
            self.src_ref.at[block], self.in_ref.at[block], self.send_sem.at[block], self.recv_sem.at[block], self.above
        )

    def down(self, block):
        slot = jnp.where(block == self.seq - 1, self.depth, block)
        return remote_copy(
            self.src_ref.at[block], self.in_ref.at[slot], self.send_sem.at[block], self.recv_sem.at[slot], self.below
        )

    def start(self):
        @pl.when(self.seq == 0)
        def _():
            for block in range(self.depth - 1, 0, -1):
                self.up(block).start()

        @pl.when(self.seq == self.depth - 1)
        def _():
            for block in range(self.depth - 1):
                self.down(block).start()

    def add(self, block):
        here_sum = self.src_ref[block].astype(jnp.float32) + self.in_ref[block].astype(jnp.float32)
        self.src_ref[block] = here_sum.astype(self.src_ref.dtype)

    def relay(self, n):
        high = self.depth - 1 - n + self.seq

        @pl.when((self.seq >= 1) & (self.seq <= n) & (high > self.seq))
        def _():
            self.up(high).wait_recv()
            self.add(high)
            self.up(high).start()

        low = n - (self.depth - 1 - self.seq)

        @pl.when((self.seq <= self.depth - 2) & (low >= 0) & (low < self.seq))
        def _():
            self.into(low).wait_recv()
            self.add(low)
            self.down(low).start()

    def into(self, block):
        return remote_copy(
            self.src_ref.at[0], self.in_ref.at[block], self.send_sem.at[0], self.recv_sem.at[block], self.below
        )

    def finish(self):
        @pl.when(self.seq > 0)
        def _():
            self.into(self.seq).wait_recv()
            self.add(self.seq)

        @pl.when(self.seq < self.depth - 1)
        def _():
            self.into(self.depth).wait_recv()

        for block in range(self.depth):

            @pl.when(block > self.seq)
            def _():
                self.up(block).wait_send()

            @pl.when(block < self.seq)
            def _():
                self.down(block).wait_send()

        total = self.src_ref[self.seq].astype(jnp.float32)
        last = jnp.where(self.seq < self.depth - 1, self.in_ref[self.depth].astype(jnp.float32), 0.0)
        return total + last


def chain_scratch(depth):
    dma = pltpu.SemaphoreType.DMA
    return [dma((depth,)), dma((depth + 1,))]


def front_kernel(
    sizes,
    x_ref, g_ref, m_ref, idx_ref, bq1_ref, bv1_ref, bq2_ref, bv2_ref, b1_ref, ck_ref, cv_ref, wq_ref, wk_ref, wv_ref, wo1_ref, wq2_ref, wo2_ref, w1_ref, w2_ref,
    bo_ref, gain_ref, shift_ref,
    xout_ref, eout_ref, wkvout_ref, wsout_ref, sqout_ref, w1out_ref, w2out_ref,
    gmine_ref, iall_ref, vall_ref, q_ref, k_ref, kt_ref, v_ref, o_ref, lse_ref, oall_ref,
    h_ref, y_ref, q2_ref, k2_ref, k2t_ref, v2_ref, o2_ref, lse2_ref, o2all_ref,
    xall_ref, enc_ref, wkv_ref, ws_ref, sq_ref, w1all_ref, w2all_ref, piece_ref, got_ref, vt_ref, s_ref,
    qsrc_ref, half_ref, other_ref, v2t_ref, vec_ref,
    load_kv, load_s, load_sq, load_w1, load_w2,
    swap_send, swap_recv, chain_send, chain_recv, side_send, side_recv, own_sem,
    idx_send, idx_recv, vec_send, vec_recv, kvsend, kvrecv, osend, orecv, out_sem,
    half_sem, qsend, qrecv, o2send, o2recv, *wsems
):
    cores, depth, ranks, per_core = sizes
    low = jnp.bfloat16
    core, seq, rank = here()
    home = rank // per_core
    local = lax.rem(rank, per_core)
    blocks = cores * depth
    head = q_ref.shape[1]
    sibling = (1 - core, seq, rank)
    above = (core, lax.rem(seq + 1, depth), rank)
    below = (core, lax.rem(seq + depth - 1, depth), rank)
    mine, places = column_places(cores, depth)
    gathers = [PlaneGather(ref, *wsems[6 * n : 6 * n + 6]) for n, ref in enumerate((wkv_ref, ws_ref, sq_ref, w1all_ref, w2all_ref))]
    gather_kv, gather_s, gather_sq, gather_w1, gather_w2 = gathers
    loads = [
        own_weights((ck_ref, cv_ref), wkv_ref, load_kv),
        own_weights((wq_ref, wk_ref, wv_ref), ws_ref, load_s),
        own_weights((wo1_ref, wq2_ref, wo2_ref), sq_ref, load_sq),
        own_weights((w1_ref,), w1all_ref, load_w1),
        own_weights((w2_ref,), w2all_ref, load_w2),
    ]
    for group in loads:
        for copy in group:
            copy.start()
    vec_ref[...] = jnp.zeros_like(vec_ref)
    for n, ref in enumerate((bq1_ref, bv1_ref, bq2_ref, bv2_ref, b1_ref)):
        vec_ref[n : n + 1, : ref.shape[0]] = as_row(ref)
    plane = plane_peers(cores, ranks)
    peers = plane + [column_peer(place, cores, rank) for place in places]
    meet(peers)

    def remote(src, dst, send, recv, device):
        return remote_copy(src, dst, send, recv, device)

    there = pl.ds((1 - core) * FULL, FULL)
    half_rows = pl.ds(core * FULL, FULL)
    swap_x = remote(x_ref.at[local, there], xall_ref.at[seq, 1 - core], swap_send.at[0], swap_recv.at[0], sibling)
    swap_g = remote(g_ref.at[local, there], gmine_ref, swap_send.at[1], swap_recv.at[1], sibling)
    swap_e = remote(m_ref.at[local], enc_ref, swap_send.at[2], swap_recv.at[2], sibling)
    own_x = pltpu.make_async_copy(x_ref.at[local, half_rows], xall_ref.at[seq, core], own_sem.at[3])
    own_g = pltpu.make_async_copy(g_ref.at[local, half_rows], gmine_ref, own_sem.at[4])
    own_e = pltpu.make_async_copy(m_ref.at[local], enc_ref, own_sem.at[5])

    @pl.when(core == home)
    def _():
        swap_x.start()
        own_x.start()

    for copy in loads[0]:
        copy.wait()
    gather_kv.start()

    def chain(block, target, way):
        part = xall_ref.at[block, core]
        return remote(part, part, chain_send.at[way, block], chain_recv.at[block], target)

    def aside(block):
        part = xall_ref.at[block, core]
        return remote(part, part, side_send.at[block], side_recv.at[block], sibling)

    def chain_step(step):
        up, down = seq - step, seq + step

        @pl.when(up >= 0)
        def _():
            if step > 0:
                chain(up, above, 0).wait_recv()

            @pl.when(seq + 1 < depth)
            def _():
                chain(up, above, 0).start()

            aside(up).start()

        @pl.when(down < depth)
        def _():
            if step > 0:
                chain(down, below, 1).wait_recv()

            @pl.when(seq > 0)
            def _():
                chain(down, below, 1).start()

            if step > 0:
                aside(down).start()

    @pl.when(core == home)
    def _():
        own_x.wait()

    @pl.when(core != home)
    def _():
        swap_x.wait_recv()

    chain_step(0)

    @pl.when(core == home)
    def _():
        swap_e.start()
        own_e.start()
        swap_g.start()
        own_g.start()

    def give_index(item, half):
        return remote(
            idx_ref.at[item], iall_ref.at[rank], idx_send.at[item, half], idx_recv.at[rank],
            (half, seq, core * per_core + item),
        )

    def is_me(item, half):
        return (half == core) & (core * per_core + item == rank)

    for item in range(per_core):
        for half in range(cores):

            @pl.when(jnp.logical_not(is_me(item, half)))
            def _():
                give_index(item, half).start()

            @pl.when(is_me(item, half))
            def _():
                own = pltpu.make_async_copy(idx_ref.at[item], iall_ref.at[rank], own_sem.at[0])
                own.start()
                own.wait()

    across = [(core, seq, lax.rem(rank + step, ranks)) for step in range(1, ranks)]
    vecs = [
        remote(vec_ref, vall_ref.at[rank], vec_send.at[step], vec_recv.at[step], peer)
        for step, peer in enumerate(across)
    ]
    for copy in vecs:
        copy.start()
    own_vec = pltpu.make_async_copy(vec_ref, vall_ref.at[rank], own_sem.at[1])
    own_vec.start()

    gather_kv.forward()
    for copy in loads[1]:
        copy.wait()
    gather_s.start()
    chain_step(1)
    for copy in vecs:
        copy.wait()
    own_vec.wait()

    @pl.when(core == home)
    def _():
        own_e.wait()

    @pl.when(core != home)
    def _():
        swap_e.wait_recv()

    for origin in range(ranks):

        @pl.when(jnp.logical_not((core == home) & (rank == origin)))
        def _():
            remote(
                idx_ref.at[0], iall_ref.at[origin], idx_send.at[0, 0], idx_recv.at[origin], sibling
            ).wait_recv()

    gather_kv.arrive()

    kv_sum = ChainSum(depth, piece_ref, got_ref, kvsend, kvrecv)

    def pick(group):
        retrieve(group, enc_ref, wkv_ref, vall_ref, iall_ref, piece_ref)

    pick(0)
    gather_s.forward()
    for copy in loads[2]:
        copy.wait()
    gather_sq.start()
    pick(1)
    chain_step(2)
    pick(2)
    pick(3)
    for step in range(3, depth):
        chain_step(step)
    kv_sum.start()
    gather_s.arrive()
    for block in range(depth):
        aside(block).wait_recv()

    outs = [
        pltpu.make_async_copy(src, dst, out_sem.at[n])
        for n, (src, dst) in enumerate(
            (
                (xall_ref, xout_ref),
                (enc_ref, eout_ref),
                (wkv_ref, wkvout_ref),
                (ws_ref, wsout_ref),
                (sq_ref, sqout_ref),
                (w1all_ref, w1out_ref),
                (w2all_ref, w2out_ref),
            )
        )
    ]
    for copy in outs[:4]:
        copy.start()

    w = jnp.concatenate([head_rows(ws_ref, seq, n, which, head) for n in range(3) for which in (2 * core, 1)], axis=0)
    rows = [vall_ref[seq, n : n + 1, :] for n in range(2)]
    bias = column_of(
        jnp.concatenate(
            [
                piece
                for row in rows
                for piece in (jnp.where(core == 0, row[:, :head], row[:, 2 * head : 3 * head]), row[:, head : 2 * head])
            ],
            axis=1,
        )
    )

    def project(block, carry):
        lanes = pl.ds(pl.multiple_of(block * FULL, FULL), FULL)
        flat = dot_nt(w, xall_ref[block // cores, lax.rem(block, cores)])
        q = ((flat[: 2 * head] + bias[: 2 * head]) * SCALE).astype(low)
        shared = jnp.where(core == 0, q[head:, :HALF], q[head:, HALF:])
        q_ref[block] = jnp.concatenate([q[:head], shared], axis=1)
        k = flat[2 * head : 4 * head].astype(low)
        v = (flat[4 * head :] + bias[2 * head :]).astype(low)
        kt_ref[:, lanes] = k
        vt_ref[:, lanes] = v
        k_ref[lanes, :] = k.T
        v_ref[lanes, :] = v.T
        return carry

    lax.fori_loop(0, blocks, project, 0)
    gather_sq.forward()
    for copy in loads[3]:
        copy.wait()
    gather_w1.start()
    kv_sum.relay(1)

    back = ColumnSend(cores, depth, o_ref, oall_ref, osend, orecv)

    def attend(block):
        out, lse = attend_block(block, True, core, blocks * FULL, q_ref[block], k_ref, vt_ref, s_ref)
        o_ref[block] = out
        lse_ref[block] = lse
        return out

    def step(n, carry):
        attend(lax.rem(mine + 1 + n, blocks))
        back.copy(n).start()
        return carry

    lax.fori_loop(0, 4, step, 0)
    kv_sum.relay(2)
    lax.fori_loop(4, 6, step, 0)
    gather_w1.forward()
    for copy in loads[4]:
        copy.wait()
    gather_w2.start()
    lax.fori_loop(6, blocks - 1, step, 0)
    oall_ref[mine] = attend(mine)
    gather_sq.arrive()
    outs[4].start()
    for n in range(blocks - 1):
        back.wait_from(n)

    part = 3 * head
    o1 = assembled(oall_ref, depth).T
    h1 = xall_ref[seq, core].astype(jnp.float32) + dot_nn(o1, late_square(sq_ref, 0, part)) + as_row(bo_ref)
    z, _ = centred_rows(h1)
    y1 = (z * as_row(gain_ref) + as_row(shift_ref)).astype(low)
    h_ref[...] = h1
    y_ref[...] = y1
    bias2 = column_of(jnp.concatenate([vall_ref[of, 2:3, :part] for of in range(ranks)], axis=1))
    q2t = ((dot_nt(late_square(sq_ref, 1, part), y1) + bias2) * SCALE).astype(low)
    dispersed(q2t, qsrc_ref, depth)
    ask = ColumnSend(cores, depth, qsrc_ref, q2_ref, qsend, qrecv)
    for n in range(blocks - 1):
        ask.copy(n).start()
    q2_ref[mine] = qsrc_ref[mine]

    slots = k2_ref.shape[0]
    total = kv_sum.finish().astype(low)
    half_ref[...] = total[:, slots:]
    swap = remote(half_ref, other_ref, half_sem.at[0], half_sem.at[1], sibling)
    swap.start()
    gather_w1.arrive()
    outs[5].start()
    swap.wait()
    half, other = half_ref[...], other_ref[...]
    shared = jnp.concatenate([jnp.where(core == 0, half, other), jnp.where(core == 0, other, half)], axis=1)
    kt = jnp.concatenate([total[:head, :slots], shared[:head]], axis=0)
    vt = jnp.concatenate([total[head:, :slots], shared[head:]], axis=0)
    k2t_ref[...] = kt
    v2t_ref[...] = vt
    k2_ref[...] = kt.T
    v2_ref[...] = vt.T

    back2 = ColumnSend(cores, depth, o2_ref, o2all_ref, o2send, o2recv)

    def attend2(block):
        out, lse = attend_block(block, False, core, slots, q2_ref[block], k2_ref, v2t_ref, s_ref)
        o2_ref[block] = out
        lse2_ref[block] = lse
        return out

    o2all_ref[mine] = attend2(mine)

    def step2(n, carry):
        ask.wait_from(n)
        attend2(lax.rem(mine + blocks - 1 - n, blocks))
        back2.copy(blocks - 2 - n).start()
        return carry

    lax.fori_loop(0, 2, step2, 0)
    gather_w2.forward()
    lax.fori_loop(2, 5, step2, 0)
    gather_w2.arrive()
    outs[6].start()
    lax.fori_loop(5, blocks - 1, step2, 0)

    for n in range(depth):
        up, down = seq - n, seq + n

        @pl.when((up >= 0) & (seq + 1 < depth))
        def _():
            chain(up, above, 0).wait_send()

        @pl.when((down < depth) & (seq > 0))
        def _():
            chain(down, below, 1).wait_send()

        aside(n).wait_send()

    @pl.when(core == home)
    def _():
        for copy in (swap_x, swap_g, swap_e):
            copy.wait_send()
        own_g.wait()

    @pl.when(core != home)
    def _():
        swap_g.wait_recv()

    for item in range(per_core):
        for half in range(cores):

            @pl.when(jnp.logical_not(is_me(item, half)))
            def _():
                give_index(item, half).wait_send()

    ask.finish_sends()
    back.finish_sends()
    back2.finish()
    for gather in gathers:
        gather.finish()
    for copy in outs:
        copy.wait()


def front(dec_input, out_grad, encoder_states, retrieved, vectors, kv, selfs, squares, w1, w2, rows1):
    cores, depth, ranks = lax.axis_size(ITEM), lax.axis_size(SEQ), lax.axis_size(TENSOR)
    per_core, _, width = dec_input.shape
    enc_rows = encoder_states.shape[1]
    slots = retrieved.shape[2]
    part = kv[0].shape[0]
    head = part // 3
    places = cores * depth
    rows = places * FULL
    lanes = width // cores
    low, full = jnp.bfloat16, jnp.float32
    dma = pltpu.SemaphoreType.DMA

    def all_of(weights):
        return (cores, ranks, sum(w.shape[0] for w in weights), lanes)

    big = [(depth, cores, FULL, width), (enc_rows, width)] + [all_of(w) for w in (kv, selfs, squares, [w1], [w2])]
    kv_shape = (2 * head, slots + slots // 2)
    parts = (places, head, WIDE)
    vec_shape = (8, vectors[-1].shape[0])
    small = [
        ((FULL, width), low),
        ((ranks,) + retrieved.shape[1:], retrieved.dtype),
        ((ranks,) + vec_shape, full),
        ((places, head, WIDE), low),
        ((rows, 2 * head), low),
        ((2 * head, rows), low),
        ((rows, 2 * head), low),
        ((places, head, WIDE), low),
        ((places, 1, WIDE), full),
        (parts, low),
        ((FULL, width), full),
        ((FULL, width), low),
        (parts, low),
        ((slots, 2 * head), low),
        ((2 * head, slots), low),
        ((slots, 2 * head), low),
        (parts, low),
        ((places, 1, WIDE), full),
        (parts, low),
    ]
    return call_kernel(
        functools.partial(front_kernel, (cores, depth, ranks, per_core)),
        "front",
        [(shape, low) for shape in big] + small,
        [dec_input, out_grad, encoder_states, retrieved, *vectors, *kv, *selfs, *squares, w1, w2, *rows1],
        scratch=[pltpu.VMEM(shape, low) for shape in big]
        + [
            pltpu.VMEM((depth,) + kv_shape, low),
            pltpu.VMEM((depth + 1,) + kv_shape, low),
            pltpu.VMEM((2 * head, rows), low),
            pltpu.VMEM((rows, WIDE), full),
            pltpu.VMEM(parts, low),
            pltpu.VMEM((2 * head, slots // 2), low),
            pltpu.VMEM((2 * head, slots // 2), low),
            pltpu.VMEM((2 * head, slots), low),
            pltpu.VMEM(vec_shape, full),
            dma((2, cores)),
            dma((3, cores)),
            dma((3, cores)),
            dma((1, cores)),
            dma((1, cores)),
            dma((3,)),
            dma((3,)),
            dma((2, depth)),
            dma((depth,)),
            dma((depth,)),
            dma((depth,)),
            dma((6,)),
            dma((per_core, cores)),
            dma((ranks,)),
        ]
        + send_scratch(ranks)
        + chain_scratch(depth)
        + send_scratch(places)
        + [dma((7,)), dma((2,))]
        + send_scratch(places)
        + send_scratch(places)
        + gather_scratch() * 5,
        collective_id=1,
        in_spaces=[pl.ANY] * 4 + [pltpu.VMEM] * len(vectors) + [pl.ANY] * 10 + [pltpu.VMEM] * 3,
        out_space=[pl.ANY] * 7 + [pltpu.VMEM] * len(small),
        us=90,
    )


def dot_nn(first_op, second_op):
    return lax.dot_general(first_op, second_op, (((1,), (0,)), ((), ())), preferred_element_type=jnp.float32)


def dot_nt(first_op, second_op):
    return lax.dot_general(first_op, second_op, (((1,), (1,)), ((), ())), preferred_element_type=jnp.float32)


def head_rows(ref, group, matrix, head_index, head):
    start = pl.multiple_of(matrix * 3 * head + head_index * head, head)
    rows = pl.ds(start, head)
    return jnp.concatenate([ref[half, group, rows, :] for half in range(ref.shape[0])], axis=1)


def as_row(ref):
    return ref[...].reshape(1, ref.shape[0])


def column_of(row):
    return jnp.broadcast_to(row, (8, row.shape[1])).T[:, :1]


def kv_rows(w_ref, group, head_index, head):
    return jnp.concatenate(
        [head_rows(w_ref, group, 0, head_index, head), head_rows(w_ref, group, 1, head_index, head)], axis=0
    )


def retrieve(group, enc_ref, w_ref, vec_ref, idx_ref, out_ref):
    core, seq, _ = here()
    enc_rows = enc_ref.shape[0]
    slots = idx_ref.shape[2]
    head = out_ref.shape[1] // 2
    low = jnp.bfloat16
    tall = enc_rows // 3

    def picked(table, index):
        total = jnp.zeros((table.shape[0], index.shape[1]), jnp.float32)
        for part in range(3):
            place = lax.broadcasted_iota(jnp.int32, (tall, index.shape[1]), 0) + (part * tall + seq * enc_rows)
            hot = jnp.where(place == index, 1.0, 0.0).astype(low)
            total = total + dot_nn(table[:, part * tall : (part + 1) * tall], hot)
        return total.astype(low)

    w = jnp.concatenate([kv_rows(w_ref, group, 2 * core, head), kv_rows(w_ref, group, 1, head)], axis=0)
    row = vec_ref[group, 3:4, :]
    blank = jnp.zeros((1, head), jnp.float32)
    first = jnp.where(core == 0, row[:, :head], row[:, 2 * head : 3 * head])
    bias = column_of(jnp.concatenate([blank, first, blank, row[:, head : 2 * head]], axis=1))
    table = (dot_nt(w, enc_ref[...]) + bias).astype(low)
    whole = idx_ref[group, pl.ds(2 * core, 1), :]
    shared = idx_ref[group, pl.ds(1, 1), :]
    half = jnp.where(core == 0, shared[:, : slots // 2], shared[:, slots // 2 :])
    out_ref[group] = jnp.concatenate([picked(table[: 2 * head], whole), picked(table[2 * head :], half)], axis=1)


def assembled(parts_ref, depth, columns=None):
    pieces = []
    for group in range(depth):
        first, second = parts_ref[2 * group], parts_ref[2 * group + 1]
        pieces += [
            first[:, :FULL],
            jnp.concatenate([first[:, FULL:WIDE], second[:, FULL:WIDE]], axis=1),
            second[:, :FULL],
        ]
    return jnp.concatenate(pieces, axis=0)


def dispersed(rows, parts_ref, depth):
    head = rows.shape[0] // (3 * depth)
    for group in range(depth):
        a = rows[3 * group * head : (3 * group + 1) * head]
        b = rows[(3 * group + 1) * head : (3 * group + 2) * head]
        c = rows[(3 * group + 2) * head : (3 * group + 3) * head]
        parts_ref[2 * group] = jnp.concatenate([a, b[:, :HALF]], axis=1)
        parts_ref[2 * group + 1] = jnp.concatenate([c, b[:, HALF:]], axis=1)


def late_square(ref, matrix, rows):
    cores, ranks = ref.shape[0], ref.shape[1]
    return jnp.concatenate(
        [
            jnp.concatenate([ref[half, rank, matrix * rows : (matrix + 1) * rows, :] for half in range(cores)], axis=1)
            for rank in range(ranks)
        ],
        axis=0,
    )


def centred_rows(h):
    center = h - jnp.mean(h, axis=-1, keepdims=True)
    spread = lax.rsqrt(jnp.mean(center * center, axis=-1, keepdims=True) + EPS)
    return center * spread, spread


def norm_back(z, spread, dy, gain):
    dz = dy * gain
    dh = spread * (
        dz - jnp.mean(dz, axis=-1, keepdims=True) - z * jnp.mean(dz * z, axis=-1, keepdims=True)
    )
    return dh, jnp.sum(dy * z, axis=0, keepdims=True), jnp.sum(dy, axis=0, keepdims=True)


def middle_kernel(
    cores, depth, ranks, per_core, part,
    o_ref, y1_ref, g_ref, w_ref, w1_in, w2_in, bo_ref, gain2_ref, shift2_ref, b1_ref, b2_ref, gain3_ref, shift3_ref,
    layer_ref, do_ref, dh2_ref, vec_ref, grad_ref,
    w1_ref, w2_ref, slope_ref, a_ref, df_ref, out_ref, dosrc_ref, turn_ref, give_ref, got_ref,
    ffn_sem, grad_sem, dosend, dorecv, *deal_sems
):
    low = jnp.bfloat16
    core, seq, rank = here()
    count = cores * depth
    mine, places = column_places(cores, depth)
    peers = [column_peer(place, cores, rank) for place in places]
    peers += [(half, seq, lax.rem(rank + step, ranks)) for step in range(1, ranks) for half in range(cores)]
    greet(peers)
    width = y1_ref.shape[1]
    lanes = width // cores
    loads = [
        pltpu.make_async_copy(src, dst, ffn_sem.at[n]) for n, (src, dst) in enumerate(((w1_in, w1_ref), (w2_in, w2_ref)))
    ]
    for load in loads:
        load.start()
    o2t = assembled(o_ref, depth)
    wo2 = late_square(w_ref, 2, part)
    h2 = y1_ref[...].astype(jnp.float32) + dot_nn(o2t.T, wo2) + as_row(bo_ref)
    z2, spread2 = centred_rows(h2)
    y2 = (z2 * as_row(gain2_ref) + as_row(shift2_ref)).astype(low)

    def hidden_in(of, half):
        return w1_ref[half, of]

    def hidden_out(of):
        return jnp.concatenate([w2_ref[half, of] for half in range(cores)], axis=1)

    root = 0.7071067811865476
    h3 = y2.astype(jnp.float32) + as_row(b2_ref)
    for load in loads:
        load.wait()
    for of in range(ranks):
        f = jnp.concatenate([dot_nn(y2, hidden_in(of, half)) for half in range(cores)], axis=1) + b1_ref[of, 4:5, :]
        cdf = 0.5 * (1.0 + lax.erf(f * root))
        a = (f * cdf).astype(low)
        slope_ref[of] = cdf + f * (0.3989422804014327 * jnp.exp(-0.5 * f * f))
        a_ref[of] = a
        h3 = h3 + dot_nn(a, hidden_out(of))
    z3, spread3 = centred_rows(h3)
    out_ref[...] = (z3 * as_row(gain3_ref) + as_row(shift3_ref)).astype(low)
    pl.semaphore_wait(pltpu.get_barrier_semaphore(), len(peers))
    deal = Deal(cores, ranks, per_core, lambda target: out_ref, layer_ref, *deal_sems)
    deal.start()

    dh3, gg3, gs3 = norm_back(z3, spread3, g_ref[...].astype(jnp.float32), as_row(gain3_ref))
    e3 = dh3.astype(low)
    dy2 = dh3
    for of in range(ranks):
        df = (dot_nt(e3, hidden_out(of)) * slope_ref[of]).astype(low)
        df_ref[of] = df
        for half in range(cores):
            dy2 = dy2 + dot_nt(df[:, half * lanes : (half + 1) * lanes], hidden_in(of, half))
    dh2, gg2, gs2 = norm_back(z2, spread2, dy2, as_row(gain2_ref))
    e2 = dh2.astype(low)
    dispersed(dot_nt(wo2, e2).astype(low), dosrc_ref, depth)
    ask = ColumnSend(cores, depth, dosrc_ref, do_ref, dosend, dorecv)
    for step in range(count - 1):
        ask.copy(step).start()
    do_ref[mine] = dosrc_ref[mine]

    dh2_ref[...] = dh2
    vec_ref[0:1] = gg3
    vec_ref[1:2] = gs3
    vec_ref[2:3] = jnp.sum(e3.astype(jnp.float32), axis=0, keepdims=True)
    vec_ref[3:4] = gg2
    vec_ref[4:5] = gs2
    vec_ref[5:6] = jnp.sum(e2.astype(jnp.float32), axis=0, keepdims=True)
    turn_ref[0] = y2.T
    turn_ref[1] = e3.T
    turn_ref[2] = e2.T
    pad = jnp.zeros((-part % 128, FULL), low)

    def grad_of(of, half):
        rows = pl.ds(pl.multiple_of(half * lanes, lanes), lanes)
        o2_part = jnp.concatenate([o2t[of * part : (of + 1) * part], pad], axis=0)
        return (
            dot_nn(turn_ref[0, rows, :], df_ref[of]),
            dot_nn(turn_ref[1, rows, :], a_ref[of]),
            dot_nt(turn_ref[2, rows, :], o2_part),
        )

    spans = (slice(0, width), slice(width, 2 * width), slice(2 * width, None))

    def swap(of):
        return remote_copy(
            give_ref.at[of], got_ref.at[of], grad_sem.at[0, of], grad_sem.at[1, of], (1 - core, seq, rank)
        )

    for of in range(ranks):
        vec_ref[6 + of : 7 + of] = jnp.sum(df_ref[of].astype(jnp.float32), axis=0, keepdims=True)
        for span, grad in zip(spans, grad_of(of, 1 - core)):
            give_ref[of, :, span] = grad.astype(low)
        swap(of).start()
    for of in range(ranks):
        grads = grad_of(of, core)
        swap(of).wait_recv()
        for span, grad in zip(spans, grads):
            grad_ref[of, :, span] = (grad + got_ref[of, :, span].astype(jnp.float32)).astype(low)
    for of in range(ranks):
        swap(of).wait_send()
    ask.finish()
    deal.finish()


def middle(per_core, o2, y1, grad_mine, squares, w1, w2, vectors):
    cores, depth, ranks = lax.axis_size(ITEM), lax.axis_size(SEQ), lax.axis_size(TENSOR)
    places, head, _ = o2.shape
    rows, width = y1.shape
    part, lanes, hidden = 3 * head, width // cores, width
    low, full = jnp.bfloat16, jnp.float32
    columns = 2 * hidden + part + (-part % 128)
    return call_kernel(
        functools.partial(middle_kernel, cores, depth, ranks, per_core, part),
        "middle",
        [
            ((per_core, cores, rows, width), low),
            (o2.shape, low),
            ((rows, width), full),
            ((6 + ranks, width), full),
            ((ranks, lanes, columns), low),
        ],
        [o2, y1, grad_mine, squares, w1, w2, *vectors],
        scratch=[
            pltpu.VMEM(w1.shape, low),
            pltpu.VMEM(w2.shape, low),
            pltpu.VMEM((ranks, rows, hidden), full),
            pltpu.VMEM((ranks, rows, hidden), low),
            pltpu.VMEM((ranks, rows, hidden), low),
            pltpu.VMEM((rows, width), low),
            pltpu.VMEM(o2.shape, low),
            pltpu.VMEM((3, width, rows), low),
            pltpu.VMEM((ranks, lanes, columns), low),
            pltpu.VMEM((ranks, lanes, columns), low),
            pltpu.SemaphoreType.DMA((2,)),
            pltpu.SemaphoreType.DMA((2, ranks)),
        ]
        + send_scratch(places)
        + deal_scratch(cores, ranks, per_core),
        collective_id=4,
        in_spaces=[pltpu.VMEM] * 4 + [pl.ANY] * 2 + [pltpu.VMEM] * len(vectors),
        us=22,
    )


def encoder_back(ranks, head, enc_ref, w_ref, idx_ref, dkv_ref, part_ref, grad_ref):
    core, seq, _ = here()
    low = jnp.bfloat16
    enc_rows, width = enc_ref.shape
    slots = idx_ref.shape[2]
    cores = w_ref.shape[0]
    lanes = width // cores
    part = width // ranks
    fold = enc_rows // (2 * cores)
    enc_t = enc_ref[...].T

    tables = []
    rows_w = []
    for group in range(ranks):
        heads = []
        shared = idx_ref[group, pl.ds(1, 1), :]
        shared = jnp.where(core == 0, shared[:, : slots // 2], shared[:, slots // 2 :])
        for which, index, rows in (
            (2 * core, idx_ref[group, pl.ds(2 * core, 1), :], slice(0, slots)),
            (1, shared, slice(slots, slots + slots // 2)),
        ):
            pieces = []
            for third in range(3):
                tall = enc_rows // 3
                place = lax.broadcasted_iota(jnp.int32, (tall, index.shape[1]), 0) + (third * tall + seq * enc_rows)
                hot = jnp.where(place == index, 1.0, 0.0).astype(low)
                pieces.append(dot_nn(hot, dkv_ref[group, rows, :]).astype(low))
            table = jnp.concatenate(pieces, axis=0)
            heads.append(table)
            tables.append(table)
            rows_w.append(kv_rows(w_ref, group, which, head))
        both = jnp.concatenate(heads, axis=1)
        grad = dot_nn(enc_t, both).astype(low)
        whole, shared = grad[:, : 2 * head], grad[:, 2 * head :]
        blank = jnp.zeros_like(whole)
        left = jnp.where(core == 0, whole, blank)
        right = jnp.where(core == 0, blank, whole)
        for half in range(cores):
            rows = slice(half * lanes, (half + 1) * lanes)
            grad_ref[half, group] = jnp.concatenate([left[rows], shared[rows], right[rows]], axis=1)
    table = jnp.concatenate(tables, axis=1)
    w = jnp.concatenate(rows_w, axis=0)
    for rank in range(ranks):
        cols = w[:, rank * part : (rank + 1) * part]
        flat = dot_nn(table, cols).astype(low)
        for half in range(cores):
            low_rows = flat[2 * half * fold : (2 * half + 1) * fold]
            high_rows = flat[(2 * half + 1) * fold : (2 * half + 2) * fold]
            part_ref[half, rank] = jnp.concatenate([low_rows, high_rows], axis=1)


def input_rows(depth, parts_ref, dh1_ref, w_ref):
    low = jnp.bfloat16
    part = 3 * parts_ref.shape[1]
    dqt = assembled(parts_ref, depth)
    stack_k, stack_v = [], []
    for group in range(depth):
        first, second = parts_ref[2 * group], parts_ref[2 * group + 1]
        for n, stack in ((0, stack_k), (1, stack_v)):
            whole = slice(WIDE + n * FULL, WIDE + (n + 1) * FULL)
            shared = slice(WIDE + 2 * FULL + n * HALF, WIDE + 2 * FULL + (n + 1) * HALF)
            both = jnp.concatenate([first[:, shared], second[:, shared]], axis=1)
            stack += [first[:, whole], both, second[:, whole]]
    dx = dh1_ref[...] + dot_nn(dqt.T, late_square(w_ref, 0, part)) * SCALE
    dx = dx + dot_nn(jnp.concatenate(stack_k, axis=0).T, late_square(w_ref, 1, part))
    dx = dx + dot_nn(jnp.concatenate(stack_v, axis=0).T, late_square(w_ref, 2, part))
    return dx.astype(low)


def merge_heads(depth, head, column_ref, group_ref):
    low = group_ref.dtype
    for group in range(depth):
        first, second = column_ref[2 * group], column_ref[2 * group + 1]
        pieces = []
        for n in range(3):
            whole = slice(2 * n * head, (2 * n + 1) * head)
            shared = slice((2 * n + 1) * head, (2 * n + 2) * head)
            both = (first[:, shared].astype(jnp.float32) + second[:, shared].astype(jnp.float32)).astype(low)
            pieces += [first[:, whole], both, second[:, whole]]
        group_ref[group] = jnp.concatenate(pieces, axis=1)


def outputs_kernel(
    ranks, part, head,
    total_ref, squares_ref, pairs_ref, rest_ref, vec_ref, layer_in, input_in, enc_in,
    layer_out, input_out, enc_out, wq1_ref, wk1_ref, wv1_ref, wo1_ref, wq2_ref, wk2_ref, wv2_ref, wo2_ref, w2_ref,
    bq1_ref, bv1_ref, bo1_ref, g1_ref, s1_ref, bq2_ref, bv2_ref, bo2_ref, g2_ref, s2_ref, b1_ref, b2_ref, g3_ref, s3_ref,
    layer_ref, input_ref, enc_ref, in_sem, out_sem,
):
    large = ((layer_in, layer_ref, layer_out), (input_in, input_ref, input_out), (enc_in, enc_ref, enc_out))
    loads = [pltpu.make_async_copy(src, mid, in_sem.at[n]) for n, (src, mid, _) in enumerate(large)]
    stores = [pltpu.make_async_copy(mid, dst, out_sem.at[n]) for n, (_, mid, dst) in enumerate(large)]
    for load in loads:
        load.start()
    for load, store in zip(loads, stores):
        load.wait()
        store.start()
    rank = lax.axis_index(TENSOR)
    height = vec_ref.shape[1]

    def line(n):
        return vec_ref[n // height, n % height : n % height + 1, :]

    def whole(row):
        return row.reshape(row.shape[1])

    def rank_part(row):
        found = row[:, :part]
        for other in range(1, ranks):
            found = jnp.where(rank == other, row[:, other * part : (other + 1) * part], found)
        return whole(found)

    for ref, n in ((g3_ref, 0), (s3_ref, 1), (b2_ref, 2), (g2_ref, 3), (s2_ref, 4), (bo2_ref, 5)):
        ref[...] = whole(line(n))
    hidden = line(6)
    for other in range(1, ranks):
        hidden = jnp.where(rank == other, line(6 + other), hidden)
    b1_ref[...] = whole(hidden)
    for ref, n in ((g1_ref, 0), (s1_ref, 1), (bo1_ref, 2)):
        ref[...] = whole(line(6 + ranks + n))
    bq2_ref[...] = rank_part(line(9 + ranks))
    bv2_ref[...] = rank_part(line(10 + ranks))
    squares = squares_ref[...]
    wq2_ref[...] = squares[:, :part] * SCALE
    wo1_ref[...] = squares[:, part:].T
    pairs = pairs_ref[...]
    for n, ref in enumerate((wk2_ref, wv2_ref)):
        ref[...] = jnp.concatenate(
            [pairs[:, (2 * k + n) * head : (2 * k + n + 1) * head] for k in range(3)], axis=1
        )
    span = w2_ref.shape[1]
    w2_ref[...] = rest_ref[:, :span]
    wo2_ref[...] = rest_ref[:, span : span + part].T
    total = total_ref[...]
    rows = wq1_ref.shape[0]
    wq1_ref[...] = total[:rows, :part] * SCALE
    wk1_ref[...] = total[:rows, part : 2 * part]
    wv1_ref[...] = total[:rows, 2 * part :]
    bq1_ref[...] = whole(total[rows : rows + 1, :part] * SCALE)
    bv1_ref[...] = whole(total[rows : rows + 1, 2 * part :])
    for store in stores:
        store.wait()


def outputs(head, width, total, squares, pairs, rest, vectors, large):
    ranks = lax.axis_size(TENSOR)
    few, part, full = squares.shape[0], 3 * head, jnp.float32
    square, turned = ((few, part), full), ((part, few), full)
    long, short = ((width,), full), ((part,), full)
    return call_kernel(
        functools.partial(outputs_kernel, ranks, part, head),
        "outputs",
        [(x.shape, x.dtype) for x in large]
        + [square, square, square, turned, square, square, square, turned, ((few, width), full)]
        + [short, short, long, long, long, short, short, long, long, long, long, long, long, long],
        [total, squares, pairs, rest, vectors, *large],
        scratch=[pltpu.VMEM(x.shape, x.dtype) for x in large]
        + [pltpu.SemaphoreType.DMA((len(large),)), pltpu.SemaphoreType.DMA((len(large),))],
        in_spaces=[pltpu.VMEM] * 5 + [pl.ANY] * len(large),
        out_space=[pl.ANY] * len(large) + [pltpu.VMEM] * 23,
        us=4,
    )


def self_grads(blocks, cores, places, x_in, x_ref, x_sem, g_ref, out_ref):
    core, seq, rank = here()
    low = jnp.bfloat16
    head = g_ref.shape[1]
    width = x_ref.shape[2]
    rows = width // places

    def load(block):
        return pltpu.make_async_copy(x_in.at[block], x_ref.at[block % 2], x_sem.at[block % 2])

    load(0).start()
    load(1).start()
    total = jnp.zeros((width, 6 * head), jnp.float32)
    sums = jnp.zeros((16, 6 * head), jnp.float32)
    ones = jnp.ones((16, FULL), low)
    zero = jnp.zeros((head, HALF), low)
    for block in range(blocks):
        g = g_ref[block]

        def own_half(first):
            part = g[:, first : first + HALF]
            return jnp.where(
                core == 0, jnp.concatenate([part, zero], axis=1), jnp.concatenate([zero, part], axis=1)
            )

        whole = WIDE + 2 * FULL
        flat = jnp.concatenate(
            [
                g[:, :FULL],
                own_half(FULL),
                g[:, WIDE : WIDE + FULL],
                own_half(whole),
                g[:, WIDE + FULL : whole],
                own_half(whole + HALF),
            ],
            axis=0,
        )
        load(block).wait()
        total = total + dot_nt(x_ref[block % 2].T, flat)
        if block + 2 < blocks:
            load(block + 2).start()
        sums = sums + dot_nt(ones, flat)
    for place in range(places):
        start = ((place % cores) * (places // cores) + place // cores) * rows
        out_ref[place, :rows, :] = total[start : start + rows].astype(low)
        out_ref[place, rows:, :] = sums.astype(low)


def widen(block):
    lane = lax.broadcasted_iota(jnp.int32, block.shape, 1)
    zero = jnp.zeros_like(block)
    return jnp.concatenate([jnp.where(lane < FULL, block, zero), jnp.where(lane < FULL, zero, block)], axis=0)


def narrow(block):
    head = block.shape[0] // 2
    return jnp.concatenate([block[:head, :FULL], block[head:, FULL:]], axis=1)


def causal_pair(core, block):
    key = lax.broadcasted_iota(jnp.int32, (PAIR, WIDE), 0)
    lane = lax.broadcasted_iota(jnp.int32, (PAIR, WIDE), 1)
    token = jnp.where(lane < FULL, lane, lane - FULL + HALF * core)
    return key <= token + lax.rem(block, 2) * FULL


def pair_rows(pair):
    return pl.ds(pl.multiple_of(pair * PAIR, PAIR), PAIR)


def over_pairs(causal, block, slots, body, state):
    if causal:
        return lax.fori_loop(0, block // 2, body, state)
    for pair in range(slots // PAIR):
        state = body(pair, state)
    return state


def attend_block(block, causal, core, slots, q, k_ref, vt_ref, s_ref):
    low = jnp.bfloat16
    head = q.shape[0]
    wide = widen(q)

    def top_of(s):
        return jnp.max(s.reshape(PAIR // 8, 8, WIDE), axis=0)

    def look(pair, top):
        rows = pair_rows(pair)
        s = dot_nn(k_ref[rows, :], wide)
        s_ref[rows, :] = s
        return jnp.maximum(top, top_of(s))

    top = over_pairs(causal, block, slots, look, jnp.full((8, WIDE), NEG, jnp.float32))
    if causal:
        rows = pair_rows(block // 2)
        s = jnp.where(causal_pair(core, block), dot_nn(k_ref[rows, :], wide), NEG)
        s_ref[rows, :] = s
        top = jnp.maximum(top, top_of(s))
    top = jnp.max(top, axis=0, keepdims=True)

    def gather(pair, state):
        total, out = state
        rows = pair_rows(pair)
        p = jnp.exp(s_ref[rows, :] - top)
        total = total + jnp.sum(p.reshape(PAIR // 8, 8, WIDE), axis=0)
        out = out + dot_nn(vt_ref[:, rows], p.astype(low))
        return total, out

    state = (jnp.zeros((8, WIDE), jnp.float32), jnp.zeros((2 * head, WIDE), jnp.float32))
    state = over_pairs(causal, block, slots, gather, state)
    total, out = gather(block // 2, state) if causal else state
    total = jnp.sum(total, axis=0, keepdims=True)
    return (narrow(out) / total).astype(low), top + jnp.log(total)


def back_block(block, causal, core, slots, q, do, o, lse, k_ref, kt_ref, v_ref, whole_ref, shared_ref):
    low = jnp.bfloat16
    head = q.shape[0]
    wide_q, wide_do = widen(q), widen(do)
    delta = jnp.sum(do.astype(jnp.float32) * o.astype(jnp.float32), axis=0, keepdims=True)
    qd = jnp.concatenate([q, jnp.zeros_like(q)], axis=0).T
    dd = jnp.concatenate([jnp.zeros_like(do), do], axis=0).T
    mix_whole = jnp.concatenate([qd[:FULL], dd[:FULL]], axis=0)
    mix_shared = jnp.concatenate([qd[FULL:], dd[FULL:]], axis=0)

    def one(pair, dq, masked=False):
        rows = pair_rows(pair)
        s = dot_nn(k_ref[rows, :], wide_q)
        if masked:
            s = jnp.where(causal_pair(core, block), s, NEG)
        p = jnp.exp(s - lse)
        dp = dot_nn(v_ref[rows, :], wide_do)
        ds = (p * (dp - delta)).astype(low)
        p = p.astype(low)
        dq = dq + dot_nn(kt_ref[:, rows], ds)
        whole_ref[rows, :] += dot_nn(jnp.concatenate([ds[:, :FULL], p[:, :FULL]], axis=1), mix_whole)
        shared_ref[rows, :] += dot_nn(jnp.concatenate([ds[:, FULL:], p[:, FULL:]], axis=1), mix_shared)
        return dq

    dq = over_pairs(causal, block, slots, one, jnp.zeros((2 * head, WIDE), jnp.float32))
    if causal:
        dq = one(block // 2, dq, True)
    return narrow(dq).astype(low)


def cross_back_kernel(
    cores, depth,
    q_ref, k_ref, kt_ref, v_ref, o_ref, lse_ref, do_ref, grad_ref,
    dqall_ref, dkv_ref, bv_ref, sum_ref,
    dq_ref, whole_ref, shared_ref, give_ref, got_ref, swap_sem, send_sem, recv_sem, *sum_refs
):
    core, seq, rank = here()
    low = jnp.bfloat16
    count = cores * depth
    mine, places = column_places(cores, depth)
    hidden = PlaneSum(grad_ref.shape[0], grad_ref, 0, *sum_refs)
    peers = [column_peer(place, cores, rank) for place in places] + hidden.peers
    greet(peers)
    slots = k_ref.shape[0]
    whole_ref[...] = jnp.zeros_like(whole_ref)
    shared_ref[...] = jnp.zeros_like(shared_ref)
    back = ColumnSend(cores, depth, dq_ref, dqall_ref, send_sem, recv_sem)

    def go(block):
        return back_block(
            block, False, core, slots, q_ref[block], do_ref[block], o_ref[block], lse_ref[block],
            k_ref, kt_ref, v_ref, whole_ref, shared_ref,
        )

    pl.semaphore_wait(pltpu.get_barrier_semaphore(), len(peers))
    hidden.start()
    dq_ref[places[0]] = go(places[0])
    back.copy(0).start()

    def step(n, carry):
        block = lax.rem(mine + 1 + n, count)
        dq_ref[block] = go(block)
        back.copy(n).start()
        return carry

    lax.fori_loop(1, count - 1, step, 0)
    dqall_ref[mine] = go(mine)
    half = slots // 2
    give_ref[...] = shared_ref[pl.ds(pl.multiple_of((1 - core) * half, half), half), :].astype(low)
    swap = remote_copy(give_ref, got_ref, swap_sem.at[0], swap_sem.at[1], (1 - core, seq, rank))
    swap.start()
    dkv_ref[:slots] = whole_ref[...].astype(low)
    swap.wait()
    kept = shared_ref[pl.ds(pl.multiple_of(core * half, half), half), :]
    dkv_ref[slots:] = (kept + got_ref[...].astype(jnp.float32)).astype(low)
    head = q_ref.shape[1]
    first = jnp.sum(dkv_ref[:slots].astype(jnp.float32), axis=0, keepdims=True)[:, head:]
    second = jnp.sum(dkv_ref[slots:].astype(jnp.float32), axis=0, keepdims=True)[:, head:]
    bv_ref[...] = jnp.concatenate(
        [
            jnp.where(n == 3 * seq + 2 * core, first, jnp.where(n == 3 * seq + 1, second, 0.0))
            for n in range(3 * depth)
        ],
        axis=1,
    )
    back.finish()
    sum_ref[...] = hidden.finish().astype(low)


def attend_cross_back(q, k, kt, v, o, lse, do, grad, columns):
    cores, depth, ranks = lax.axis_size(ITEM), lax.axis_size(SEQ), lax.axis_size(TENSOR)
    lanes = grad.shape[1]
    places, head, _ = q.shape
    slots = k.shape[0]
    low = jnp.bfloat16
    sums = pltpu.VMEM((slots, 2 * head), jnp.float32)
    return call_kernel(
        functools.partial(cross_back_kernel, cores, depth),
        "back_cross",
        [
            (q.shape, low),
            ((slots + slots // 2, 2 * head), low),
            ((1, 3 * depth * head), jnp.float32),
            ((lanes, columns), low),
        ],
        [q, k, kt, v, o, lse, do, grad],
        scratch=[
            pltpu.VMEM(q.shape, low),
            sums,
            sums,
            pltpu.VMEM((slots // 2, 2 * head), low),
            pltpu.VMEM((slots // 2, 2 * head), low),
            pltpu.SemaphoreType.DMA((2,)),
        ]
        + send_scratch(places)
        + sum_scratch(ranks, lanes, columns, low),
        collective_id=5,
        in_spaces=[pltpu.VMEM] * 7 + [pl.ANY],
        us=24,
    )


def self_back_kernel(
    cores, depth, ranks, part,
    dq2_ref, dh2_ref, h1_ref, y1_ref, oin_ref, w_in, gain_ref,
    q_ref, k_ref, kt_ref, v_ref, o_ref, lse_ref, dkv_ref, idx_ref, vmid_ref, bv_ref, red1_in,
    enc_in, wkv_in, ws_in, x_in, grad_ref,
    in_ref, encg_ref, total_ref, squares_ref, pairs_ref, rest_ref, w1_ref, vout_ref,
    w_ref, enc_ref, wkv_ref, ws_ref, x_ref, encp_ref, got_ref, sum_ref, encall_ref,
    dosrc_ref, do_ref, g_ref, gall_ref, whole_ref, shared_ref, dkvall_ref, grad2_ref,
    dh1_ref, dx_ref, self_ref, column_ref, group_ref, plane_ref,
    red1_ref, red2_ref, red4_ref, red5_ref, r1_ref, r2_ref, r4_ref, r5_ref,
    give_ref, gots_ref, shsend, shrecv, load_sem, x_sem, swap_sem, dosend, dorecv, gsend, grecv, kvsend, kvrecv, csend, crecv, psend, precv, zsend, zrecv, *more
):
    core, seq, rank = here()
    low = jnp.bfloat16
    count = cores * depth
    head = part // 3
    per_core = encg_ref.shape[0]
    mine, places = column_places(cores, depth)
    first = PlaneReduce(ranks, grad2_ref, *more[:6])
    second = PlaneReduce(ranks, grad2_ref, more[6], more[1], *more[7:11])
    deal_enc = Deal(cores, ranks, per_core, lambda target: sum_ref.at[target], encall_ref, *more[11:14])
    deal_in = Deal(cores, ranks, per_core, lambda target: dx_ref, in_ref, *more[14:17])
    hidden = PlaneSum(ranks, grad_ref, grad_ref.shape[2] - red5_ref.shape[2], *more[17:21])
    vectors = VectorSum(cores, depth, ranks, vout_ref, *more[21:])
    along = [
        ChainSum(depth, src, dst, zsend.at[n], zrecv.at[n])
        for n, (src, dst) in enumerate(
            ((red1_ref, r1_ref), (red2_ref, r2_ref), (red4_ref, r4_ref), (red5_ref, r5_ref))
        )
    ]
    loads = [
        pltpu.make_async_copy(src, dst, load_sem.at[n])
        for n, (src, dst) in enumerate(((wkv_in, wkv_ref), (enc_in, enc_ref), (ws_in, ws_ref)))
    ]
    squares = [
        pltpu.make_async_copy(
            w_in.at[half, of, pl.ds(0, 2 * part), :], w_ref.at[half, of], load_sem.at[3 + half * ranks + of]
        )
        for half in range(cores)
        for of in range(ranks)
    ]
    for load in squares + loads:
        load.start()
    peers = [column_peer(place, cores, rank) for place in places] + first.peers
    peers += [(1 - core, seq, peer[2]) for peer in first.peers]
    greet(peers)
    chain = Chain(depth, dkvall_ref, kvsend, kvrecv)
    dkvall_ref[seq] = dkv_ref[...]
    pl.semaphore_wait(pltpu.get_barrier_semaphore(), len(peers))
    chain.step(0)
    hidden.start()
    red1_ref[...] = red1_in[...]

    width = y1_ref.shape[1]
    lanes = width // cores
    dq2t = assembled(dq2_ref, depth)
    for load in squares:
        load.wait()
    dy1 = dh2_ref[...] + dot_nn(dq2t.T, late_square(w_ref, 1, part)) * SCALE
    z1, spread1 = centred_rows(h1_ref[...])
    dh1, gg1, gs1 = norm_back(z1, spread1, dy1, as_row(gain_ref))
    e1 = dh1.astype(low)
    dispersed(dot_nt(late_square(w_ref, 0, part), e1).astype(low), dosrc_ref, depth)
    ask = ColumnSend(cores, depth, dosrc_ref, do_ref, dosend, dorecv)
    for step in range(count - 1):
        ask.copy(step).start()
    do_ref[mine] = dosrc_ref[mine]
    dh1_ref[...] = dh1
    ones = jnp.ones((8, FULL), low)
    given = [vmid_ref[n : n + 1] for n in range(vmid_ref.shape[0])]
    given += [gg1, gs1, jnp.sum(e1.astype(jnp.float32), axis=0, keepdims=True), dot_nt(ones, dq2t)[0:1] * SCALE]
    given += [bv_ref[...], jnp.zeros_like(gg1)]
    vectors.start(given)
    o1t = assembled(oin_ref, depth)
    both = jnp.concatenate([y1_ref[...].T, e1.T], axis=1)
    blank = jnp.zeros((part, FULL), low)
    for to in range(ranks):
        rows = slice(to * part, (to + 1) * part)
        right = jnp.concatenate(
            [
                jnp.concatenate([dq2t[rows], blank], axis=1),
                jnp.concatenate([blank, o1t[rows]], axis=1),
            ],
            axis=0,
        )
        for half in range(cores):
            grad2_ref[half, to] = dot_nt(both[half * lanes : (half + 1) * lanes], right).astype(low)
    first.start()

    whole_ref[...] = jnp.zeros_like(whole_ref)
    shared_ref[...] = jnp.zeros_like(shared_ref)
    for step in range(count - 1):
        ask.wait_from(step)
    chain.step(1)
    back = ColumnSend(cores, depth, g_ref, gall_ref, gsend, grecv)

    def swap_shared(block):
        return remote_copy(
            give_ref.at[block], gots_ref.at[block], shsend.at[block], shrecv.at[block], (1 - core, seq, rank)
        )

    def go(block):
        g_ref[block, :, :WIDE] = back_block(
            block, True, core, count * FULL, q_ref[block], do_ref[block], o_ref[block], lse_ref[block],
            k_ref, kt_ref, v_ref, whole_ref, shared_ref,
        )
        start = pl.multiple_of(block * FULL, FULL)
        there = pl.ds(pl.multiple_of(start + (1 - core) * HALF, HALF), HALF)
        give_ref[block] = shared_ref[there, :].astype(low)
        swap_shared(block).start()

    def send_back(block):
        start = pl.multiple_of(block * FULL, FULL)
        whole = whole_ref[pl.ds(start, FULL), :].T.astype(low)
        here_rows = pl.ds(pl.multiple_of(start + core * HALF, HALF), HALF)
        swap_shared(block).wait_recv()
        shared = (shared_ref[here_rows, :] + gots_ref[block].astype(jnp.float32)).T.astype(low)
        g_ref[block, :, WIDE:] = jnp.concatenate([whole[:head], whole[head:], shared[:head], shared[head:]], axis=1)

        @pl.when(block != mine)
        def _():
            back.copy(lax.rem(block + 2 * count - mine - 1, count)).start()

        @pl.when(block == mine)
        def _():
            gall_ref[mine] = g_ref[mine]

    def step(n, carry):
        go(count - 1 - n)
        send_back(count - n)
        return carry

    go(count - 1)
    lax.fori_loop(1, 2, step, 0)
    first.middle()
    chain.step(2)
    lax.fori_loop(2, 4, step, 0)
    along[0].start()
    lax.fori_loop(4, count, step, 0)
    send_back(0)

    self_grads(count, cores, count, x_in, x_ref, x_sem, g_ref, self_ref)
    column = [
        remote_copy(
            self_ref.at[place], column_ref.at[mine], csend.at[step], crecv.at[step], column_peer(place, cores, rank)
        )
        for step, place in enumerate(places)
    ]
    for copy in column:
        copy.start()

    vectors.second()
    for load in loads:
        load.wait()
    for n in range(3, depth):
        chain.step(n)

    encoder_back(ranks, head, enc_ref, wkv_ref, idx_ref, dkvall_ref, encp_ref, grad2_ref)
    swap = remote_copy(encp_ref.at[1 - core], got_ref, swap_sem.at[0], swap_sem.at[1], (1 - core, seq, rank))
    swap.start()
    second.start()
    red2_ref[...] = first.finish().astype(low).reshape(red2_ref.shape)
    along[1].start()
    along[0].relay(1)
    red5_ref[...] = hidden.finish().astype(low).reshape(red5_ref.shape)
    along[3].start()
    swap.wait()
    sum_ref[...] = (encp_ref[core].astype(jnp.float32) + got_ref[...].astype(jnp.float32)).astype(low)
    deal_enc.start()
    second.middle()

    for step in range(count - 1):
        back.wait_from(step)
    dx_ref[...] = input_rows(depth, gall_ref, dh1_ref, ws_ref)
    deal_in.start()
    along[0].relay(2)
    along[1].relay(1)
    along[3].relay(1)

    for copy in column:
        copy.wait()
    column_ref[mine] = self_ref[mine]
    merge_heads(depth, head, column_ref, group_ref)
    plane = [
        remote_copy(group_ref.at[peer[2]], plane_ref.at[rank], psend.at[step], precv.at[step], peer)
        for step, peer in enumerate(first.peers)
    ]
    for copy in plane:
        copy.start()
    red4_ref[...] = second.finish().astype(low).reshape(red4_ref.shape)
    along[2].start()
    along[1].relay(2)
    along[3].relay(2)
    vectors.third()
    along[2].relay(1)

    deal_enc.finish()
    fold = encall_ref.shape[2]
    for item in range(per_core):
        for half in range(cores):
            for side in range(2):
                rows = slice((2 * half + side) * fold, (2 * half + side + 1) * fold)
                encg_ref[item, rows, :] = encall_ref[item, half, :, side * part : (side + 1) * part]
    w1_ref[...] = along[0].finish()
    squares_ref[...] = along[1].finish()
    along[2].relay(2)
    rest_ref[...] = along[3].finish()
    for copy in plane:
        copy.wait()
    total = group_ref[rank].astype(jnp.float32)
    for step in range(1, ranks):
        total = total + plane_ref[lax.rem(rank + step, ranks)].astype(jnp.float32)
    total_ref[...] = total
    vectors.finish()
    chain.finish()
    ask.finish_sends()
    back.finish_sends()
    for block in range(count):
        swap_shared(block).wait_send()
    deal_in.finish()
    pairs_ref[...] = along[2].finish()


def attend_self_back(per_core, *args):
    cores, depth, ranks = lax.axis_size(ITEM), lax.axis_size(SEQ), lax.axis_size(TENSOR)
    (
        dq2, dh2, h1, y1, o1, squares, gain, q, k, kt, v, o, lse, dkv, index, vec_mid, bv, red1, enc, wkv, ws, x_all, grad
    ) = args
    places, head, _ = q.shape
    rows, width = y1.shape
    low, full = jnp.bfloat16, jnp.float32
    part, lanes = 3 * head, width // cores
    all_rows = places * rows
    dma = pltpu.SemaphoreType.DMA
    grads = (cores, ranks, lanes, 2 * part)
    message = (places, head, WIDE + 2 * FULL + 2 * HALF)
    sums = pltpu.VMEM((all_rows, 2 * head), full)
    fold = enc.shape[0] // (2 * cores)
    rest = grad.shape[2] - width
    vec_shape = (places, (vec_mid.shape[0] + 6) // places, width)
    few = width // places
    high = few + 16
    red1 = red1.reshape(depth, few, width)
    along = [pltpu.VMEM((depth, few, columns), low) for columns in (2 * part, 2 * part, rest)]
    into = [pltpu.VMEM((depth + 1, few, columns), low) for columns in (width, 2 * part, 2 * part, rest)]
    args = (*args[:17], red1, *args[18:])
    return call_kernel(
        functools.partial(self_back_kernel, cores, depth, ranks, part),
        "back_self",
        [
            ((per_core, cores, rows, width), low),
            ((per_core, enc.shape[0], part), low),
            ((high, 3 * part), full),
            ((few, 2 * part), full),
            ((few, 2 * part), full),
            ((few, rest), full),
            ((few, width), full),
            (vec_shape, full),
        ],
        list(args),
        scratch=[
            pltpu.VMEM((cores, ranks, 2 * part, lanes), low),
            pltpu.VMEM(enc.shape, low),
            pltpu.VMEM(wkv.shape, low),
            pltpu.VMEM(ws.shape, low),
            pltpu.VMEM((2,) + x_all.shape[1:], low),
            pltpu.VMEM((cores, ranks, fold, 2 * part), low),
            pltpu.VMEM((ranks, fold, 2 * part), low),
            pltpu.VMEM((ranks, fold, 2 * part), low),
            pltpu.VMEM((per_core, cores, fold, 2 * part), low),
            pltpu.VMEM(q.shape, low),
            pltpu.VMEM(q.shape, low),
            pltpu.VMEM(message, low),
            pltpu.VMEM(message, low),
            sums,
            sums,
            pltpu.VMEM((depth,) + dkv.shape, low),
            pltpu.VMEM(grads, low),
            pltpu.VMEM((rows, width), full),
            pltpu.VMEM((rows, width), low),
            pltpu.VMEM((places, high, 6 * head), low),
            pltpu.VMEM((places, high, 6 * head), low),
            pltpu.VMEM((depth, high, 3 * part), low),
            pltpu.VMEM((ranks, high, 3 * part), low),
        ]
        + [pltpu.VMEM(red1.shape, low)]
        + along
        + into
        + [pltpu.VMEM((places, HALF, 2 * head), low), pltpu.VMEM((places, HALF, 2 * head), low)]
        + [dma((places,)), dma((places,)), dma((3 + cores * ranks,)), dma((2,)), dma((2,))]
        + send_scratch(places)
        + send_scratch(places)
        + [dma((2, depth)), dma((depth,))]
        + send_scratch(places)
        + send_scratch(ranks)
        + [dma((4, depth)), dma((4, depth + 1))]
        + reduce_scratch(ranks, lanes, 2 * part, low)
        + reduce_scratch(ranks, lanes, 2 * part, low)[1:]
        + deal_scratch(cores, ranks, per_core)
        + deal_scratch(cores, ranks, per_core)
        + sum_scratch(ranks, lanes, rest, low)
        + vector_scratch(vec_shape, places, ranks),
        collective_id=6,
        in_spaces=[pltpu.VMEM] * 5 + [pl.ANY] + [pltpu.VMEM] * 12 + [pl.ANY] * 5,
        us=100,
    )


def column_body(
    dec_input,
    encoder_states,
    retrieved,
    self_wq,
    self_bq,
    self_wk,
    self_wv,
    self_bv,
    self_wo,
    self_bo,
    norm1_gain,
    norm1_bias,
    cross_wq,
    cross_bq,
    cross_wk,
    cross_wv,
    cross_bv,
    cross_wo,
    cross_bo,
    norm2_gain,
    norm2_bias,
    ffn_w1,
    ffn_b1,
    ffn_w2,
    ffn_b2,
    norm3_gain,
    norm3_bias,
    out_grad,
):
    low, full = jnp.bfloat16, jnp.float32
    core, seq, rank = here()
    cores, depth, ranks = lax.axis_size(ITEM), lax.axis_size(SEQ), lax.axis_size(TENSOR)
    per_core, _, width = dec_input.shape
    slots = retrieved.shape[2]
    part = self_wq.shape[1]
    head = part // 3
    places = cores * depth
    lanes = width // cores
    hidden = ffn_w1.shape[1]

    (
        x_all, enc, weights_kv, weights_self, weights_square, weights_in, weights_out,
        grad_mine, index, vectors, q1, k1, k1t, v1, o1_parts, lse1, o1,
        h1, y1, q2, k2, k2t, v2, o2_parts, lse2, o2,
    ) = front(
        dec_input, out_grad, encoder_states, retrieved, [self_bq, self_bv, cross_bq, cross_bv, ffn_b1],
        [cross_wk.T, cross_wv.T], [self_wq.T, self_wk.T, self_wv.T], [self_wo, cross_wq.T, cross_wo],
        ffn_w1, ffn_w2, [self_bo, norm1_gain, norm1_bias],
    )
    x_all = x_all.reshape(places, FULL, width)
    layer_out, do2, dh2, vec_mid, grad_mid = middle(
        per_core,
        o2,
        y1,
        grad_mine,
        weights_square,
        weights_in,
        weights_out,
        [
            cross_bo,
            norm2_gain,
            norm2_bias,
            vectors,
            ffn_b2,
            norm3_gain,
            norm3_bias,
        ],
    )
    dq2, dkv2, bv, first_sum = attend_cross_back(q2, k2, k2t, v2, o2_parts, lse2, do2, grad_mid, hidden)
    input_grad, encoder_grad, total, squares, pairs, rest, gffn_w1, vectors = attend_self_back(
        per_core,
        dq2, dh2, h1, y1, o1, weights_square, norm1_gain,
        q1, k1, k1t, v1, o1_parts, lse1, dkv2, index, vec_mid, bv, first_sum, enc, weights_kv, weights_self, x_all, grad_mid,
    )
    (
        layer_out, input_grad, encoder_grad,
        gself_wq, gself_wk, gself_wv, gself_wo, gcross_wq, gcross_wk, gcross_wv, gcross_wo, gffn_w2,
        gself_bq, gself_bv, gself_bo, gnorm1_gain, gnorm1_bias,
        gcross_bq, gcross_bv, gcross_bo, gnorm2_gain, gnorm2_bias, gffn_b1, gffn_b2, gnorm3_gain, gnorm3_bias,
    ) = outputs(head, width, total, squares, pairs, rest, vectors, [layer_out, input_grad, encoder_grad])
    layer_out = layer_out.reshape(per_core, cores * FULL, width)
    input_grad = input_grad.reshape(per_core, cores * FULL, width)
    gffn_w2 = gffn_w2.T
    return (
        layer_out,
        input_grad,
        encoder_grad,
        gself_wq,
        gself_bq,
        gself_wk,
        gself_wv,
        gself_bv,
        gself_wo,
        gself_bo,
        gnorm1_gain,
        gnorm1_bias,
        gcross_wq,
        gcross_bq,
        gcross_wk,
        gcross_wv,
        gcross_bv,
        gcross_wo,
        gcross_bo,
        gnorm2_gain,
        gnorm2_bias,
        gffn_w1,
        gffn_b1,
        gffn_w2,
        gffn_b2,
        gnorm3_gain,
        gnorm3_bias,
    )


def solution(mesh):
    placed = (
        P(ITEM, SEQ, None),
        P(ITEM, SEQ, None),
        P(ITEM, TENSOR, None),
        P(None, TENSOR),
        P(TENSOR),
        P(None, TENSOR),
        P(None, TENSOR),
        P(TENSOR),
        P(TENSOR, None),
        P(),
        P(),
        P(),
        P(None, TENSOR),
        P(TENSOR),
        P(None, TENSOR),
        P(None, TENSOR),
        P(TENSOR),
        P(TENSOR, None),
        P(),
        P(),
        P(),
        P(None, TENSOR),
        P(TENSOR),
        P(TENSOR, None),
        P(),
        P(),
        P(),
        P(ITEM, SEQ, None),
    )
    reduced = (
        P(ITEM, SEQ, None),
        P(ITEM, SEQ, None),
        P(ITEM, SEQ, TENSOR),
        P((ITEM, SEQ), TENSOR),
        P(TENSOR),
        P((ITEM, SEQ), TENSOR),
        P((ITEM, SEQ), TENSOR),
        P(TENSOR),
        P(TENSOR, (ITEM, SEQ)),
        P(),
        P(),
        P(),
        P((ITEM, SEQ), TENSOR),
        P(TENSOR),
        P((ITEM, SEQ), TENSOR),
        P((ITEM, SEQ), TENSOR),
        P(TENSOR),
        P(TENSOR, (ITEM, SEQ)),
        P(),
        P(),
        P(),
        P((ITEM, SEQ), TENSOR),
        P(TENSOR),
        P(TENSOR, (ITEM, SEQ)),
        P(),
        P(),
        P(),
    )

    def layer(*arrays):
        chosen = column_body if column_plan_fits(mesh, arrays) else general_body
        return jax.shard_map(
            chosen,
            mesh=mesh,
            in_specs=placed,
            out_specs=reduced,
            check_vma=False,
        )(*arrays)

    return layer
```
